32 devices in a mesh: basis: 16 (over z, y, core), state: 2 (over x).
Axes of the slice: x: 2, y: 2, z: 4, core: 2. Of those that a mesh axis runs over, the one named last changes fastest.
Arguments:
- vectors: bfloat16 [512, 81920], P('state', 'basis'), may hold values from -6 to 6
- blocks: bfloat16 [640, 18, 128, 128], P('basis', 'state'), may hold values from -0.125 to 0.125
- columns: int32 [640, 18], P('basis', 'state'), may hold values from 0 to 639, as said below
- counts: int32 [640], P('basis'), may hold values from 4 to 18, as said below
Outputs:
- sigma: bfloat16 [512, 81920], P('state', 'basis')
The draws below stay inside these ranges and needn't reach their ends.
Inputs may be any that keep to these rules, and one draw needn't show every extreme that they name: Every block column lies within 36 blocks of its block row and inside the basis; a row's slots name distinct columns except near the basis ends, where a column may repeat. Slots k < counts[r] are live; some block row has all 18 slots live.
All inputs are finite; a program needn't handle non-finite values.
Results may differ from the reference program's by a relative error of at most 0.001.
Values may be sent and summed in bfloat16 or wider, within the bound.
No kernel may reach another device: no remote copies, remote signals or barrier semaphores. Data moves between devices by JAX's collectives and lax.ppermute only.
A program may use at most 192 MiB of HBM per device.

```python
import jax
import jax.numpy as jnp
from jax import lax

B = 128
S = 512
W = 36
NB = 640
N = 81920
K = 18


def draw_columns(key, part):
    row_keys = jax.random.split(jax.random.fold_in(key, 11), NB)
    offsets = jax.vmap(lambda single: jax.random.permutation(single, 2 * W + 1))(row_keys)[:, :K] - W
    row_index = jnp.arange(NB, dtype=jnp.int32)[:, None]
    target = row_index + offsets.astype(jnp.int32)
    target = jnp.where(target < 0, -target, target)
    target = jnp.where(target > NB - 1, 2 * (NB - 1) - target, target)
    return target.astype(jnp.int32)


def draw_counts(key, part):
    first_key, second_key = jax.random.split(jax.random.fold_in(key, 23))
    values = jax.random.randint(first_key, (NB,), max(1, K // 4), K + 1, dtype=jnp.int32)
    where_full = jax.random.randint(second_key, (), 0, NB, dtype=jnp.int32)
    return values.at[where_full].set(K).astype(jnp.int32)


def level_of(stream_key, extent, cuts, smallest, top_value):
    factor_of, own = 1.0, jax.random.fold_in(stream_key, 6)
    for position, blocks in cuts:
        draws = jnp.exp(jax.random.uniform(jax.random.fold_in(own, position), (blocks,), jnp.float32, smallest / len(cuts), top_value / len(cuts)))
        factor_of = factor_of * jnp.repeat(draws, extent[position] // blocks).reshape([-1 if axis == position else 1 for axis in range(len(extent))])
    return factor_of


def normal_values(stream_key, shape, width, bound, cuts=(), held_as=jnp.bfloat16):
    level = level_of(stream_key, shape, cuts, -0.22, 0.18) if cuts else 1.0
    array = jax.random.normal(stream_key, shape, jnp.float32) * width * level
    return jnp.minimum(jnp.maximum(array, -bound), bound).astype(held_as)


def setup_inputs(seed: int = 0) -> dict:
    key_of = jax.random.split(jax.random.key(seed), 5)
    return {
        "vectors": normal_values(key_of[0], (S, N), 1.0, 6.0, ((0, 2), (1, 16))),
        "blocks": normal_values(key_of[1], (NB, K, B, B), (B * K) ** -0.5, 0.125, ((0, 16), (1, 2))),
        "columns": draw_columns(jax.random.fold_in(key_of[4], 71), 0),
        "counts": draw_counts(jax.random.fold_in(key_of[4], 71), 0),
    }


def reference(vectors, blocks, columns, counts):
    vector_blocks = vectors.reshape(S, NB, B)

    def one_row(pieces):
        panel, column_list, live_count = pieces
        picked = jnp.take(vector_blocks, column_list, axis=1).astype(jnp.float32)
        live_mask = (jnp.arange(K) < live_count).astype(jnp.float32)
        picked = picked * live_mask[None, :, None]
        return jnp.einsum("skb,kcb->sc", picked, panel.astype(jnp.float32))

    result = lax.map(one_row, (blocks, columns, counts))
    return jnp.transpose(result, (1, 0, 2)).reshape(S, NB * B).astype(jnp.bfloat16)
```

```python
import functools

import jax
import jax.numpy as jnp
from jax import lax
from jax.experimental import pallas as pl
from jax.experimental.pallas import tpu as pltpu
from jax.sharding import PartitionSpec as P

W = 36
VMEM_LIMIT = 48 * 1024 * 1024


def rows_after(array, start, size, after):
    def body(*refs):
        source, target, sem = refs[0], refs[-2], refs[-1]
        copy = pltpu.make_async_copy(source.at[pl.ds(start, size)], target, sem)
        copy.start()
        copy.wait()

    shape = (size,) + array.shape[1:]
    return pl.pallas_call(
        body,
        out_shape=jax.ShapeDtypeStruct(shape, array.dtype),
        in_specs=[pl.BlockSpec(memory_space=pl.ANY)] * (1 + len(after)),
        out_specs=pl.BlockSpec(memory_space=pl.ANY),
        scratch_shapes=[pltpu.SemaphoreType.DMA],
        name="rows_after",
    )(array, *after)


def product_kernel(group, slots, block, index_ref, left, own, right, blocks_ref, out_ref, ext, sems):
    step = pl.program_id(0)
    reach, width = left.shape[1], own.shape[1]

    @pl.when(step == 0)
    def _():
        copies = (
            pltpu.make_async_copy(left, ext.at[:, pl.ds(0, reach)], sems.at[0]),
            pltpu.make_async_copy(own, ext.at[:, pl.ds(reach, width)], sems.at[1]),
            pltpu.make_async_copy(right, ext.at[:, pl.ds(reach + width, reach)], sems.at[2]),
        )
        for copy in copies:
            copy.start()
        ext[:, 2 * reach + width :] = jnp.zeros((ext.shape[0], block), ext.dtype)
        for copy in copies:
            copy.wait()

    for member in range(group):
        base = (step * group + member) * slots
        picked = jnp.concatenate(
            [
                ext[:, pl.ds(pl.multiple_of(index_ref[base + slot] * block, block), block)]
                for slot in range(slots)
            ],
            axis=1,
        )
        panel = jnp.concatenate([blocks_ref[member, slot] for slot in range(slots)], axis=1)
        out_ref[:, member * block : (member + 1) * block] = lax.dot_general(
            picked, panel, (((1,), (1,)), ((), ())), preferred_element_type=jnp.float32
        )


def product(index, left, own, right, blocks):
    rows, slots, block, _ = blocks.shape
    states, width = own.shape
    group = 4 if rows % 4 == 0 else 1
    ext_width = 2 * left.shape[1] + width + block
    anywhere = pl.BlockSpec(memory_space=pl.ANY)
    return pl.pallas_call(
        functools.partial(product_kernel, group, slots, block),
        out_shape=jax.ShapeDtypeStruct((states, width), jnp.float32),
        grid_spec=pltpu.PrefetchScalarGridSpec(
            num_scalar_prefetch=1,
            grid=(rows // group,),
            in_specs=[
                anywhere,
                anywhere,
                anywhere,
                pl.BlockSpec((group, slots, block, block), lambda i, _: (i, 0, 0, 0)),
            ],
            out_specs=pl.BlockSpec((states, group * block), lambda i, _: (0, i)),
            scratch_shapes=[pltpu.VMEM((states, ext_width), own.dtype), pltpu.SemaphoreType.DMA((3,))],
        ),
        compiler_params=pltpu.CompilerParams(vmem_limit_bytes=VMEM_LIMIT),
        cost_estimate=pl.CostEstimate(
            flops=2 * states * width * slots * block,
            bytes_accessed=2 * blocks.size + 2 * states * ext_width + 4 * states * width,
            transcendentals=0,
        ),
        name="product",
    )(index, left, own, right, blocks)


def on_device(vectors, blocks, columns, counts):
    states, width = vectors.shape
    rows, slots, block, _ = blocks.shape
    reach = W * block
    basis_size, state_size = lax.axis_size("basis"), lax.axis_size("state")
    chunks = 2 if states % 32 == 0 else 1
    size = states // chunks

    slot_index = lax.axis_index("state") * slots + jnp.arange(slots, dtype=jnp.int32)
    relative = columns - (lax.axis_index("basis") * rows - W)
    zeros_at = rows + 2 * W
    index = jnp.where(slot_index[None, :] < counts[:, None], relative, zeros_at).reshape(-1)

    up = [(i, i + 1) for i in range(basis_size - 1)]
    down = [(i + 1, i) for i in range(basis_size - 1)]

    def halo(piece):
        left = lax.ppermute(piece[:, width - reach :], "basis", up)
        right = lax.ppermute(piece[:, :reach], "basis", down)
        return left, right

    def shifted(piece, shift):
        return lax.ppermute(piece, "state", [(i, (i + shift) % state_size) for i in range(state_size)])

    own = [vectors[c * size : (c + 1) * size] for c in range(chunks)]
    sums = [[None] * state_size for _ in range(chunks)]
    before = []
    first_halo = halo(own[0])
    last_halo = None
    for shift in range(1, state_size):
        for c in range(chunks):
            mine = rows_after(vectors, c * size, size, before) if before else own[c]
            theirs = shifted(mine, shift)
            before = [theirs]
            last_halo = halo(theirs)
            partial = product(index, last_halo[0], theirs, last_halo[1], blocks)
            sums[c][shift] = shifted(partial, -shift)
    out = []
    for c in range(chunks):
        if c == 0:
            left, right = first_halo
        else:
            left, right = halo(rows_after(vectors, c * size, size, last_halo) if last_halo else own[c])
        total = product(index, left, own[c], right, blocks)
        for shift in range(1, state_size):
            total = total + sums[c][shift]
        out.append(total.astype(jnp.bfloat16))
    return jnp.concatenate(out, axis=0)


def solution(mesh):
    in_specs = (
        P("state", "basis"),
        P("basis", "state", None, None),
        P("basis", "state"),
        P("basis"),
    )
    out_specs = P("state", "basis")
    return jax.shard_map(
        on_device, mesh=mesh, in_specs=in_specs, out_specs=out_specs, check_vma=False
    )
```

```python
import functools
import math

import jax
import jax.numpy as jnp
from jax import lax
from jax.experimental import pallas as pl
from jax.experimental.pallas import tpu as pltpu
from jax.sharding import PartitionSpec as P

W = 36
VMEM_LIMIT = 48 * 1024 * 1024
TOP = 32767.0
FINE = 65536.0
SMALLEST = 2.0**-100


def zero_after(*arrays):
    corners = [array[0, 0] for array in arrays]
    return sum((corner != corner).astype(jnp.int32) for corner in corners)


def rows_after(array, start, size, after):
    if not after:
        return array[start : start + size]
    unit = math.gcd(start, size)
    units = array.reshape((array.shape[0] // unit, unit) + array.shape[1:])
    part = lax.dynamic_slice_in_dim(units, start // unit + zero_after(*after), size // unit, axis=0)
    return part.reshape((size,) + array.shape[1:])


def fill(left, own, right, ext, sems):
    reach, width = left.shape[1], own.shape[1]
    copies = (
        pltpu.make_async_copy(left, ext.at[:, pl.ds(0, reach)], sems.at[0]),
        pltpu.make_async_copy(own, ext.at[:, pl.ds(reach, width)], sems.at[1]),
        pltpu.make_async_copy(right, ext.at[:, pl.ds(reach + width, reach)], sems.at[2]),
    )
    for copy in copies:
        copy.start()
    ext[:, 2 * reach + width :] = jnp.zeros((ext.shape[0], ext.shape[1] - 2 * reach - width), ext.dtype)
    for copy in copies:
        copy.wait()


def row_sums(index_ref, row, slots, block, ext, panel):
    picked = jnp.concatenate(
        [
            ext[:, pl.ds(pl.multiple_of(index_ref[row * slots + slot] * block, block), block)]
            for slot in range(slots)
        ],
        axis=1,
    )
    return jnp.dot(picked, panel, preferred_element_type=jnp.float32)


def own_kernel(group, slots, block, index_ref, left, own, right, panels_ref, out_ref, ext, sems):
    step = pl.program_id(0)

    @pl.when(step == 0)
    def _():
        fill(left, own, right, ext, sems)

    for member in range(group):
        out_ref[:, member * block : (member + 1) * block] = row_sums(
            index_ref, step * group + member, slots, block, ext, panels_ref[member]
        )


def level_code(top):
    return jnp.ceil(jnp.log2(jnp.maximum(top, SMALLEST)) * FINE).astype(jnp.int32)


def level_of(code):
    return jnp.exp2(code.astype(jnp.float32) * (1.0 / FINE))


def coded_kernel(group, slots, block, words, index_ref, left, own, right, panels_ref, out_ref, ext, sems):
    step = pl.program_id(0)

    @pl.when(step == 0)
    def _():
        fill(left, own, right, ext, sems)
        out_ref[:, words * block :] = jnp.zeros((out_ref.shape[0], block), jnp.int32)

    lane = lax.broadcasted_iota(jnp.int32, (out_ref.shape[0], block), 1)
    codes = out_ref[:, words * block :]
    coded = []
    for member in range(group):
        row = step * group + member
        sums = row_sums(index_ref, row, slots, block, ext, panels_ref[member])
        code = level_code(jnp.max(jnp.abs(sums), axis=1, keepdims=True))
        codes = jnp.where(lane == row, code, codes)
        scaled = jnp.round(sums * (TOP / level_of(code)))
        coded.append(jnp.clip(scaled, -TOP, TOP).astype(jnp.int32))
    out_ref[:, words * block :] = codes
    for pair in range(group // 2):
        word = (coded[2 * pair + 1] << 16) | (coded[2 * pair] & 0xFFFF)
        at = pl.multiple_of((step * (group // 2) + pair) * block, block)
        out_ref[:, pl.ds(at, block)] = word


def products(index, left, own, right, panels, coded):
    rows, depth, block = panels.shape
    slots = depth // block
    states, width = own.shape
    group = 4
    ext_width = 2 * left.shape[1] + width + block
    in_hbm = pl.BlockSpec(memory_space=pltpu.HBM)
    if coded:
        words = rows // 2
        kernel = functools.partial(coded_kernel, group, slots, block, words)
        out_shape = jax.ShapeDtypeStruct((states, (words + 1) * block), jnp.int32)
        out_spec = pl.BlockSpec(out_shape.shape, lambda i, _: (0, 0))
    else:
        kernel = functools.partial(own_kernel, group, slots, block)
        out_shape = jax.ShapeDtypeStruct((states, width), jnp.float32)
        out_spec = pl.BlockSpec((states, group * block), lambda i, _: (0, i))
    return pl.pallas_call(
        kernel,
        out_shape=out_shape,
        grid_spec=pltpu.PrefetchScalarGridSpec(
            num_scalar_prefetch=1,
            grid=(rows // group,),
            in_specs=[
                in_hbm,
                in_hbm,
                in_hbm,
                pl.BlockSpec((group, depth, block), lambda i, _: (i, 0, 0)),
            ],
            out_specs=out_spec,
            scratch_shapes=[pltpu.VMEM((states, ext_width), own.dtype), pltpu.SemaphoreType.DMA((3,))],
        ),
        compiler_params=pltpu.CompilerParams(vmem_limit_bytes=VMEM_LIMIT),
        cost_estimate=pl.CostEstimate(
            flops=2 * states * width * depth,
            bytes_accessed=2 * panels.size + 2 * states * ext_width + 4 * states * width,
            transcendentals=0,
        ),
        name="coded_products" if coded else "own_products",
    )(index, left, own, right, panels)


def finish_kernel(partials, block, pairs, own_ref, *refs):
    out_ref = refs[-1]
    step = pl.program_id(0)
    lane = lax.broadcasted_iota(jnp.int32, (own_ref.shape[0], block), 1)
    levels = [level_of(refs[2 * p + 1][...]) * (1.0 / TOP) for p in range(partials)]
    for pair in range(pairs):
        for half in range(2):
            at = (2 * pair + half) * block
            row = (step * pairs + pair) * 2 + half
            total = own_ref[:, at : at + block]
            for p in range(partials):
                word = refs[2 * p][:, pair * block : (pair + 1) * block]
                value = (word >> 16) if half else ((word << 16) >> 16)
                level = jnp.max(jnp.where(lane == row, levels[p], 0.0), axis=1, keepdims=True)
                total = total + value.astype(jnp.float32) * level
            out_ref[:, at : at + block] = total.astype(out_ref.dtype)


def finish(own_sums, coded, out, chunk, chunks, block):
    states, width = own_sums.shape
    words = width // block // 2
    pairs = 4 if words % 4 == 0 else 1
    in_specs = [pl.BlockSpec((states, 2 * pairs * block), lambda i: (0, i))]
    operands = [own_sums]
    for array in coded:
        in_specs.append(pl.BlockSpec((states, pairs * block), lambda i: (0, i)))
        in_specs.append(pl.BlockSpec((states, block), lambda i: (0, words)))
        operands += [array, array]
    aliases = {}
    if out is not None:
        aliases = {len(operands): 0}
        in_specs.append(pl.BlockSpec(memory_space=pl.ANY))
        operands.append(out)
    return pl.pallas_call(
        functools.partial(finish_kernel, len(coded), block, pairs),
        out_shape=jax.ShapeDtypeStruct((chunks * states, width), jnp.bfloat16),
        grid=(words // pairs,),
        in_specs=in_specs,
        out_specs=pl.BlockSpec((states, 2 * pairs * block), lambda i: (chunk, i)),
        input_output_aliases=aliases,
        compiler_params=pltpu.CompilerParams(vmem_limit_bytes=VMEM_LIMIT),
        cost_estimate=pl.CostEstimate(
            flops=4 * states * width, bytes_accessed=8 * states * width, transcendentals=0
        ),
        name="finish",
    )(*operands)


def on_device(vectors, blocks, columns, counts):
    states, width = vectors.shape
    rows, slots, block, _ = blocks.shape
    reach = W * block
    basis_size, state_size = lax.axis_size("basis"), lax.axis_size("state")
    chunks = 2
    size = states // chunks

    slot_index = lax.axis_index("state") * slots + jnp.arange(slots, dtype=jnp.int32)
    relative = columns - (lax.axis_index("basis") * rows - W)
    zeros_at = rows + 2 * W
    index = jnp.where(slot_index[None, :] < counts[:, None], relative, zeros_at).reshape(-1)
    panels = jnp.swapaxes(blocks, 2, 3).reshape(rows, slots * block, block)

    up = [(i, i + 1) for i in range(basis_size - 1)]
    down = [(i + 1, i) for i in range(basis_size - 1)]

    def halo(piece):
        left = lax.ppermute(piece[:, width - reach :], "basis", up)
        right = lax.ppermute(piece[:, :reach], "basis", down)
        return left, right

    def shifted(piece, shift):
        return lax.ppermute(piece, "state", [(i, (i + shift) % state_size) for i in range(state_size)])

    coded = [[] for _ in range(chunks)]
    arrived = []
    ends = halo(vectors[:size])
    own_ends = [ends]
    for shift in range(1, state_size):
        for c in range(chunks):
            theirs = shifted(rows_after(vectors, c * size, size, arrived), shift)
            arrived = [theirs]
            ends = halo(theirs)
            partial = products(index, ends[0], theirs, ends[1], panels, True)
            coded[c].append(shifted(partial, -shift))
    out = None
    for c in range(chunks):
        if c:
            own_ends.append(halo(rows_after(vectors, c * size, size, ends)))
        left, right = own_ends[c]
        sums = products(index, left, vectors[c * size : (c + 1) * size], right, panels, False)
        out = finish(sums, coded[c], out, c, chunks, block)
    return out


def solution(mesh):
    in_specs = (
        P("state", "basis"),
        P("basis", "state", None, None),
        P("basis", "state"),
        P("basis"),
    )
    out_specs = P("state", "basis")
    return jax.shard_map(
        on_device, mesh=mesh, in_specs=in_specs, out_specs=out_specs, check_vma=False
    )
```

```python
import functools
import math

import jax
import jax.numpy as jnp
from jax import lax
from jax.experimental import pallas as pl
from jax.experimental.pallas import tpu as pltpu
from jax.sharding import PartitionSpec as P

W = 36
VMEM_LIMIT = 48 * 1024 * 1024
TOP = 32767.0
FINE = 65536.0
SMALLEST = 2.0**-100


def after(array, *others):
    return lax.optimization_barrier((array, *others))[0]


def fill(left, own, right, ext, sems):
    reach, width = left.shape[1], own.shape[1]
    copies = (
        pltpu.make_async_copy(left, ext.at[:, pl.ds(0, reach)], sems.at[0]),
        pltpu.make_async_copy(own, ext.at[:, pl.ds(reach, width)], sems.at[1]),
        pltpu.make_async_copy(right, ext.at[:, pl.ds(reach + width, reach)], sems.at[2]),
    )
    for copy in copies:
        copy.start()
    ext[:, 2 * reach + width :] = jnp.zeros((ext.shape[0], ext.shape[1] - 2 * reach - width), ext.dtype)
    for copy in copies:
        copy.wait()


def row_sums(index_ref, row, slots, block, ext, panel_ref):
    picked = jnp.concatenate(
        [
            ext[:, pl.ds(pl.multiple_of(index_ref[row * slots + slot] * block, block), block)]
            for slot in range(slots)
        ],
        axis=1,
    )
    panel = jnp.concatenate([panel_ref[slot] for slot in range(slots)], axis=1)
    return lax.dot_general(
        picked, panel, (((1,), (1,)), ((), ())), preferred_element_type=jnp.float32
    )


def own_kernel(group, slots, block, index_ref, left, own, right, blocks_ref, out_ref, ext, sems):
    step = pl.program_id(0)

    @pl.when(step == 0)
    def _():
        fill(left, own, right, ext, sems)

    for member in range(group):
        out_ref[:, member * block : (member + 1) * block] = row_sums(
            index_ref, step * group + member, slots, block, ext, blocks_ref.at[member]
        )


def level_code(top):
    return jnp.ceil(jnp.log2(jnp.maximum(top, SMALLEST)) * FINE).astype(jnp.int32)


def level_of(code):
    return jnp.exp2(code.astype(jnp.float32) * (1.0 / FINE))


def coded_kernel(group, slots, block, words, index_ref, left, own, right, blocks_ref, out_ref, ext, sems):
    step = pl.program_id(0)

    @pl.when(step == 0)
    def _():
        fill(left, own, right, ext, sems)
        out_ref[:, words * block :] = jnp.zeros((out_ref.shape[0], block), jnp.int32)

    lane = lax.broadcasted_iota(jnp.int32, (out_ref.shape[0], block), 1)
    codes = out_ref[:, words * block :]
    coded = []
    for member in range(group):
        row = step * group + member
        sums = row_sums(index_ref, row, slots, block, ext, blocks_ref.at[member])
        code = level_code(jnp.max(jnp.abs(sums), axis=1, keepdims=True))
        codes = jnp.where(lane == row, code, codes)
        scaled = jnp.round(sums * (TOP / level_of(code)))
        coded.append(jnp.clip(scaled, -TOP, TOP).astype(jnp.int32))
    out_ref[:, words * block :] = codes
    for pair in range(group // 2):
        word = (coded[2 * pair + 1] << 16) | (coded[2 * pair] & 0xFFFF)
        at = pl.multiple_of((step * (group // 2) + pair) * block, block)
        out_ref[:, pl.ds(at, block)] = word


def products(index, left, own, right, blocks, coded):
    rows, slots, block, _ = blocks.shape
    states, width = own.shape
    group = 4
    ext_width = 2 * left.shape[1] + width + block
    in_hbm = pl.BlockSpec(memory_space=pltpu.HBM)
    if coded:
        words = rows // 2
        kernel = functools.partial(coded_kernel, group, slots, block, words)
        out_shape = jax.ShapeDtypeStruct((states, (words + 1) * block), jnp.int32)
        out_spec = pl.BlockSpec(out_shape.shape, lambda i, _: (0, 0))
    else:
        kernel = functools.partial(own_kernel, group, slots, block)
        out_shape = jax.ShapeDtypeStruct((states, width), jnp.float32)
        out_spec = pl.BlockSpec((states, group * block), lambda i, _: (0, i))
    return pl.pallas_call(
        kernel,
        out_shape=out_shape,
        grid_spec=pltpu.PrefetchScalarGridSpec(
            num_scalar_prefetch=1,
            grid=(rows // group,),
            in_specs=[
                in_hbm,
                in_hbm,
                in_hbm,
                pl.BlockSpec((group, slots, block, block), lambda i, _: (i, 0, 0, 0)),
            ],
            out_specs=out_spec,
            scratch_shapes=[pltpu.VMEM((states, ext_width), own.dtype), pltpu.SemaphoreType.DMA((3,))],
        ),
        compiler_params=pltpu.CompilerParams(vmem_limit_bytes=VMEM_LIMIT),
        cost_estimate=pl.CostEstimate(
            flops=2 * states * width * slots * block,
            bytes_accessed=2 * blocks.size + 2 * states * ext_width + 4 * states * width,
            transcendentals=0,
        ),
        name="coded_products" if coded else "own_products",
    )(index, left, own, right, blocks)


def finish_kernel(partials, block, pairs, own_ref, *refs):
    out_ref = refs[-1]
    lane = lax.broadcasted_iota(jnp.int32, (own_ref.shape[0], block), 1)
    levels = [level_of(refs[2 * p + 1][...]) * (1.0 / TOP) for p in range(partials)]
    for pair in range(pairs):
        for half in range(2):
            at = (2 * pair + half) * block
            row = 2 * pair + half
            total = own_ref[:, at : at + block]
            for p in range(partials):
                word = refs[2 * p][:, pair * block : (pair + 1) * block]
                value = (word >> 16) if half else ((word << 16) >> 16)
                level = jnp.max(jnp.where(lane == row, levels[p], 0.0), axis=1, keepdims=True)
                total = total + value.astype(jnp.float32) * level
            out_ref[:, at : at + block] = total.astype(out_ref.dtype)


def finish(own_sums, own_start, coded, coded_start, out, start, size, states, block):
    width = own_sums.shape[1]
    words = width // block // 2
    unit = math.gcd(math.gcd(size, start), math.gcd(start - own_start, start - coded_start))
    own_at, coded_at, out_at = (start - own_start) // unit, (start - coded_start) // unit, start // unit
    in_specs = [pl.BlockSpec((unit, width), lambda i: (own_at + i, 0))]
    operands = [own_sums]
    for array in coded:
        in_specs.append(pl.BlockSpec((unit, words * block), lambda i: (coded_at + i, 0)))
        in_specs.append(pl.BlockSpec((unit, block), lambda i: (coded_at + i, words)))
        operands += [array, array]
    aliases = {}
    if out is not None:
        aliases = {len(operands): 0}
        in_specs.append(pl.BlockSpec(memory_space=pl.ANY))
        operands.append(out)
    return pl.pallas_call(
        functools.partial(finish_kernel, len(coded), block, words),
        out_shape=jax.ShapeDtypeStruct((states, width), jnp.bfloat16),
        grid=(size // unit,),
        in_specs=in_specs,
        out_specs=pl.BlockSpec((unit, width), lambda i: (out_at + i, 0)),
        input_output_aliases=aliases,
        compiler_params=pltpu.CompilerParams(vmem_limit_bytes=VMEM_LIMIT),
        cost_estimate=pl.CostEstimate(
            flops=4 * size * width, bytes_accessed=8 * size * width, transcendentals=0
        ),
        name="finish",
    )(*operands)


def starts_of(sizes):
    return [sum(sizes[:i]) for i in range(len(sizes))]


def on_device(vectors, blocks, columns, counts):
    states, width = vectors.shape
    rows, slots, block, _ = blocks.shape
    reach = W * block
    basis_size, state_size = lax.axis_size("basis"), lax.axis_size("state")
    if states % 128 == 0:
        sizes = (3 * states // 8, 3 * states // 8, states // 4)
        own_sizes = (states // 2, states // 2)
    else:
        sizes, own_sizes = (states,), (states,)
    starts, own_starts = starts_of(sizes), starts_of(own_sizes)

    slot_index = lax.axis_index("state") * slots + jnp.arange(slots, dtype=jnp.int32)
    relative = columns - (lax.axis_index("basis") * rows - W)
    zeros_at = rows + 2 * W
    index = jnp.where(slot_index[None, :] < counts[:, None], relative, zeros_at).reshape(-1)

    up = [(i, i + 1) for i in range(basis_size - 1)]
    down = [(i + 1, i) for i in range(basis_size - 1)]

    def halo(piece, *others):
        edges = (piece[:, width - reach :], piece[:, :reach])
        if others:
            edges = lax.optimization_barrier((*edges, *others))[:2]
        return lax.ppermute(edges[0], "basis", up), lax.ppermute(edges[1], "basis", down)

    def shifted(piece, shift):
        return lax.ppermute(piece, "state", [(i, (i + shift) % state_size) for i in range(state_size)])

    pieces = [vectors[at : at + size] for at, size in zip(own_starts, own_sizes)]
    own_ends = [halo(pieces[0])]
    own_sums = []

    def own_part(part, *others):
        if part == len(own_ends):
            own_ends.append(halo(pieces[part], *others))
        elif part == len(own_sums):
            own_sums.append(products(index, own_ends[part][0], pieces[part], own_ends[part][1], blocks, False))

    coded = [[] for _ in sizes]
    theirs, ends, sent = [], [], []
    count = (state_size - 1) * len(sizes)
    for n in range(count):
        shift, c = 1 + n // len(sizes), n % len(sizes)
        piece = vectors[starts[c] : starts[c] + sizes[c]]
        if n == 2:
            own_part(0)
            piece = after(piece, theirs[n - 1], own_sums[0])
        elif n:
            piece = after(piece, theirs[n - 1])
        theirs.append(shifted(piece, shift))
        if n >= 2:
            sent.append(products(index, *around(ends[n - 2], theirs[n - 2]), blocks, True))
        before = own_ends[0] if n == 0 else (sent[n - 2],) if n >= 2 else ()
        ends.append(halo(theirs[n], *before))
    for n in range(max(count - 2, 0), count):
        sent.append(products(index, *around(ends[n], theirs[n]), blocks, True))
    received = []
    for n in range(count):
        message = after(sent[n], received[n - 2]) if n >= 2 else sent[n]
        received.append(shifted(message, -(1 + n // len(sizes))))
        coded[n % len(sizes)].append(received[n])
    for part in range(len(own_sizes)):
        own_part(part, *ends[max(count - 2, 0)])
        own_part(part)

    out = None
    for part, own_size in enumerate(own_sizes):
        for c, size in enumerate(sizes):
            at = max(own_starts[part], starts[c])
            end = min(own_starts[part] + own_size, starts[c] + size)
            if at < end:
                out = finish(
                    own_sums[part], own_starts[part], coded[c], starts[c], out, at, end - at, states, block
                )
    return out


def around(ends, piece):
    return ends[0], piece, ends[1]


def solution(mesh):
    in_specs = (
        P("state", "basis"),
        P("basis", "state", None, None),
        P("basis", "state"),
        P("basis"),
    )
    out_specs = P("state", "basis")
    return jax.shard_map(
        on_device, mesh=mesh, in_specs=in_specs, out_specs=out_specs, check_vma=False
    )
```

```python
import functools
import math

import jax
import jax.numpy as jnp
from jax import lax
from jax.experimental import pallas as pl
from jax.experimental.pallas import tpu as pltpu
from jax.sharding import PartitionSpec as P

W = 36
VMEM_LIMIT = 16 * 1024 * 1024
TOP = 32767.0
FINE = 65536.0
SMALLEST = 2.0**-100


def after(array, *others):
    return lax.optimization_barrier((array, *others))[0]


def fill(sources, plan, ext):
    at, step = 0, 16
    for part, (start, size, _) in enumerate(plan):
        left, own, right = sources[3 * part : 3 * part + 3]
        reach, width = left.shape[1], own.shape[1]

        @pl.loop(0, size // step)
        def _(i, left=left, own=own, right=right, start=start, at=at, reach=reach, width=width):
            here = pl.ds(pl.multiple_of(i * step, step), step)
            mine = pl.ds(pl.multiple_of(start + i * step, step), step)
            to = pl.ds(pl.multiple_of(at + i * step, step), step)
            ext[to, :reach] = left[here, :]
            ext[to, reach : reach + width] = own[mine, :]
            ext[to, reach + width : 2 * reach + width] = right[here, :]

        at += size


def row_sums(index_ref, row, slots, block, ext, panel_ref):
    picked = jnp.concatenate(
        [
            ext[:, pl.ds(pl.multiple_of(index_ref[row * slots + slot] * block, block), block)]
            for slot in range(slots)
        ],
        axis=1,
    )
    panel = jnp.concatenate([panel_ref[slot] for slot in range(slots)], axis=1)
    return lax.dot_general(
        picked, panel, (((1,), (1,)), ((), ())), preferred_element_type=jnp.float32
    )


def level_code(top):
    return jnp.ceil(jnp.log2(jnp.maximum(top, SMALLEST)) * FINE).astype(jnp.int32)


def level_of(code):
    return jnp.exp2(code.astype(jnp.float32) * (1.0 / FINE))


def code_into(out_ref, first, block, words, sums):
    lane = lax.broadcasted_iota(jnp.int32, (out_ref.shape[0], block), 1)
    codes = out_ref[:, words * block :]
    values = []
    for member, mine in enumerate(sums):
        code = level_code(jnp.max(jnp.abs(mine), axis=1, keepdims=True))
        codes = jnp.where(lane == first + member, code, codes)
        scaled = jnp.round(mine * (TOP / level_of(code)))
        values.append(jnp.clip(scaled, -TOP, TOP).astype(jnp.int32))
    out_ref[:, words * block :] = codes
    for pair in range(len(sums) // 2):
        word = (values[2 * pair + 1] << 16) | (values[2 * pair] & 0xFFFF)
        at = pl.multiple_of((first // 2 + pair) * block, block)
        out_ref[:, pl.ds(at, block)] = word


def products_kernel(plan, group, slots, block, words, index_ref, *refs):
    parts = len(plan)
    sources, panels = refs[: 3 * parts], refs[3 * parts]
    outs, ext = refs[3 * parts + 1 : 4 * parts + 1], refs[-1]

    fill(sources, plan, ext)
    end = ext.shape[1] - block
    ext[:, end:] = jnp.zeros((ext.shape[0], block), ext.dtype)
    for (_, size, coded), out_ref in zip(plan, outs):
        if coded:
            out_ref[:, words * block :] = jnp.zeros((size, block), jnp.int32)

    @pl.loop(0, panels.shape[0] // group)
    def _(step):
        first = step * group
        sums = [
            row_sums(index_ref, first + member, slots, block, ext, panels.at[first + member])
            for member in range(group)
        ]
        at = 0
        for (_, size, coded), out_ref in zip(plan, outs):
            mine = [total[at : at + size] for total in sums]
            if coded:
                code_into(out_ref, first, block, words, mine)
            else:
                for member in range(group):
                    column = pl.multiple_of((first + member) * block, block)
                    out_ref[:, pl.ds(column, block)] = mine[member]
            at += size


def products(index, parts, blocks):
    rows, slots, block, _ = blocks.shape
    reach, width = parts[0][0].shape[1], parts[0][1].shape[1]
    plan = tuple(part[3:] for part in parts)
    states = sum(size for _, size, _ in plan)
    group, words = 8 if rows % 8 == 0 else 2, rows // 2
    ext_width = 2 * reach + width + block
    in_vmem = pl.BlockSpec(memory_space=pltpu.VMEM)
    arrays = [array for part in parts for array in part[:3]] + [blocks]
    out_shape = []
    for _, size, coded in plan:
        if coded:
            out_shape.append(jax.ShapeDtypeStruct((size, (words + 1) * block), jnp.int32))
        else:
            out_shape.append(jax.ShapeDtypeStruct((size, width), jnp.float32))
    return pl.pallas_call(
        functools.partial(products_kernel, plan, group, slots, block, words),
        out_shape=out_shape,
        in_specs=[pl.BlockSpec(memory_space=pltpu.SMEM)] + [in_vmem] * len(arrays),
        out_specs=[in_vmem] * len(plan),
        scratch_shapes=[pltpu.VMEM((states, ext_width), parts[0][1].dtype)],
        compiler_params=pltpu.CompilerParams(vmem_limit_bytes=VMEM_LIMIT),
        cost_estimate=pl.CostEstimate(flops=1, bytes_accessed=1, transcendentals=0),
        name="products",
    )(index, *[pltpu.with_memory_space_constraint(array, pltpu.VMEM) for array in arrays])


def finish_kernel(partials, block, pairs, own_ref, *refs):
    out_ref = refs[-1]
    lane = lax.broadcasted_iota(jnp.int32, (own_ref.shape[0], block), 1)
    levels = [level_of(refs[2 * p + 1][...]) * (1.0 / TOP) for p in range(partials)]
    for pair in range(pairs):
        for half in range(2):
            at = (2 * pair + half) * block
            row = 2 * pair + half
            total = own_ref[:, at : at + block]
            for p in range(partials):
                word = refs[2 * p][:, pair * block : (pair + 1) * block]
                value = (word >> 16) if half else ((word << 16) >> 16)
                level = jnp.max(jnp.where(lane == row, levels[p], 0.0), axis=1, keepdims=True)
                total = total + value.astype(jnp.float32) * level
            out_ref[:, at : at + block] = total.astype(out_ref.dtype)


def finish(own_sums, own_start, coded, coded_start, out, start, size, states, block):
    width = own_sums.shape[1]
    words = width // block // 2
    unit = math.gcd(math.gcd(size, start), math.gcd(start - own_start, start - coded_start))
    own_at, coded_at, out_at = (start - own_start) // unit, (start - coded_start) // unit, start // unit
    in_specs = [pl.BlockSpec((unit, width), lambda i: (own_at + i, 0))]
    operands = [own_sums]
    for array in coded:
        in_specs.append(pl.BlockSpec((unit, words * block), lambda i: (coded_at + i, 0)))
        in_specs.append(pl.BlockSpec((unit, block), lambda i: (coded_at + i, words)))
        operands += [array, array]
    aliases = {}
    if out is not None:
        aliases = {len(operands): 0}
        in_specs.append(pl.BlockSpec(memory_space=pl.ANY))
        operands.append(out)
    return pl.pallas_call(
        functools.partial(finish_kernel, len(coded), block, words),
        out_shape=jax.ShapeDtypeStruct((states, width), jnp.bfloat16),
        grid=(size // unit,),
        in_specs=in_specs,
        out_specs=pl.BlockSpec((unit, width), lambda i: (out_at + i, 0)),
        input_output_aliases=aliases,
        compiler_params=pltpu.CompilerParams(vmem_limit_bytes=VMEM_LIMIT),
        cost_estimate=pl.CostEstimate(
            flops=1, bytes_accessed=1, transcendentals=0
        ),
        name="finish",
    )(*operands)


def starts_of(sizes):
    return [sum(sizes[:i]) for i in range(len(sizes))]


def on_device(vectors, blocks, columns, counts):
    states, width = vectors.shape
    rows, slots, block, _ = blocks.shape
    reach = W * block
    basis_size, state_size = lax.axis_size("basis"), lax.axis_size("state")
    if states % 128 == 0:
        sizes = (states // 2, states // 2)
        own_sizes = (states // 2, states // 2)
    else:
        sizes, own_sizes = (states,), (states,)
    starts, own_starts = starts_of(sizes), starts_of(own_sizes)

    slot_index = lax.axis_index("state") * slots + jnp.arange(slots, dtype=jnp.int32)
    relative = columns - (lax.axis_index("basis") * rows - W)
    zeros_at = rows + 2 * W
    index = jnp.where(slot_index[None, :] < counts[:, None], relative, zeros_at).reshape(-1)

    up = [(i, i + 1) for i in range(basis_size - 1)]
    down = [(i + 1, i) for i in range(basis_size - 1)]

    def halo(piece, *others):
        edges = (piece[:, width - reach :], piece[:, :reach])
        if others:
            edges = lax.optimization_barrier((*edges, *others))[:2]
        return lax.ppermute(edges[0], "basis", up), lax.ppermute(edges[1], "basis", down)

    def shifted(piece, shift):
        return lax.ppermute(piece, "state", [(i, (i + shift) % state_size) for i in range(state_size)])

    def own_halo(part, *others):
        return halo(vectors[own_starts[part] : own_starts[part] + own_sizes[part]], *others)

    def own_part(part, ends):
        return (ends[0], vectors, ends[1], own_starts[part], own_sizes[part], False)

    def their_part(n):
        return (ends[n][0], theirs[n], ends[n][1], 0, theirs[n].shape[0], True)

    messages = [(shift, c) for shift in range(1, state_size) for c in range(len(sizes))]
    count = len(messages)
    theirs, ends, sent, received = [], [], [], []
    first = own_halo(0)
    for n, (shift, c) in enumerate(messages):
        piece = vectors[starts[c] : starts[c] + sizes[c]]
        theirs.append(shifted(after(piece, theirs[n - 1], *first) if n else piece, shift))
    for n in range(count):
        ends.append(halo(theirs[n]))
        if n == 0:
            own_sums = products(index, [own_part(0, first)], blocks)
        sent += products(after(index, own_sums[0]), [their_part(n)], blocks)
        if n == 0 and len(own_sizes) > 1:
            last = own_halo(1, theirs[min(1, count - 1)], sent[0])
    coded = [[] for _ in sizes]
    for n, (shift, c) in enumerate(messages):
        received.append(shifted(sent[n], -shift))
        coded[c].append(received[n])
    if len(own_sizes) > 1:
        own_sums += products(index, [own_part(1, last)], blocks)

    out = None
    for part, own_size in enumerate(own_sizes):
        for c, size in enumerate(sizes):
            at = max(own_starts[part], starts[c])
            end = min(own_starts[part] + own_size, starts[c] + size)
            if at < end:
                out = finish(
                    own_sums[part], own_starts[part], coded[c], starts[c], out, at, end - at, states, block
                )
    return out


def solution(mesh):
    in_specs = (
        P("state", "basis"),
        P("basis", "state", None, None),
        P("basis", "state"),
        P("basis"),
    )
    out_specs = P("state", "basis")
    return jax.shard_map(
        on_device, mesh=mesh, in_specs=in_specs, out_specs=out_specs, check_vma=False
    )
```

```python
import functools
import math

import jax
import jax.numpy as jnp
from jax import lax
from jax.experimental import pallas as pl
from jax.experimental.pallas import tpu as pltpu
from jax.sharding import PartitionSpec as P

W = 36
VMEM_LIMIT = 32 * 1024 * 1024
TOP = 32767.0
FINE = 65536.0
SMALLEST = 2.0**-100


def after(array, *others):
    return lax.optimization_barrier((array, *others))[0]


def fill(sources, plan, ext, sems):
    copies, at = [], 0
    for part, (start, size, _) in enumerate(plan):
        left, own, right = sources[3 * part : 3 * part + 3]
        reach, width = left.shape[1], own.shape[1]
        rows = pl.ds(at, size)
        copies += [
            pltpu.make_async_copy(left, ext.at[rows, pl.ds(0, reach)], sems.at[3 * part]),
            pltpu.make_async_copy(
                own.at[pl.ds(start, size)], ext.at[rows, pl.ds(reach, width)], sems.at[3 * part + 1]
            ),
            pltpu.make_async_copy(right, ext.at[rows, pl.ds(reach + width, reach)], sems.at[3 * part + 2]),
        ]
        at += size
    for copy in copies:
        copy.start()
    return copies


def row_sums(index_ref, row, slots, block, ext, panel_ref):
    picked = jnp.concatenate(
        [
            ext[:, pl.ds(pl.multiple_of(index_ref[row * slots + slot] * block, block), block)]
            for slot in range(slots)
        ],
        axis=1,
    )
    panel = jnp.concatenate([panel_ref[slot] for slot in range(slots)], axis=1)
    return lax.dot_general(
        picked, panel, (((1,), (1,)), ((), ())), preferred_element_type=jnp.float32
    )


def level_code(top):
    return jnp.ceil(jnp.log2(jnp.maximum(top, SMALLEST)) * FINE).astype(jnp.int32)


def level_of(code):
    return jnp.exp2(code.astype(jnp.float32) * (1.0 / FINE))


def code_into(out_ref, first, block, words, sums):
    lane = lax.broadcasted_iota(jnp.int32, (out_ref.shape[0], block), 1)
    codes = out_ref[:, words * block :]
    values = []
    for member, mine in enumerate(sums):
        code = level_code(jnp.max(jnp.abs(mine), axis=1, keepdims=True))
        codes = jnp.where(lane == first + member, code, codes)
        scaled = jnp.round(mine * (TOP / level_of(code)))
        values.append(jnp.clip(scaled, -TOP, TOP).astype(jnp.int32))
    out_ref[:, words * block :] = codes
    for pair in range(len(sums) // 2):
        word = (values[2 * pair + 1] << 16) | (values[2 * pair] & 0xFFFF)
        at = pl.multiple_of((first // 2 + pair) * block, block)
        out_ref[:, pl.ds(at, block)] = word


def products_kernel(plan, group, slots, block, words, index_ref, *refs):
    parts = len(plan)
    sources, blocks_ref = refs[: 3 * parts], refs[3 * parts]
    outs, (ext, panels, sems, panel_sems) = refs[3 * parts + 1 : 4 * parts + 1], refs[4 * parts + 1 :]
    groups = panels.shape[0] // group

    def panel_copy(step):
        rows = pl.ds(step * group, group)
        return pltpu.make_async_copy(blocks_ref.at[rows], panels.at[rows], panel_sems.at[step])

    copies = fill(sources, plan, ext, sems)
    for step in range(groups):
        panel_copy(step).start()
    end = ext.shape[1] - block
    ext[:, end:] = jnp.zeros((ext.shape[0], block), ext.dtype)
    for (_, size, coded), out_ref in zip(plan, outs):
        if coded:
            out_ref[:, words * block :] = jnp.zeros((size, block), jnp.int32)
    for copy in copies:
        copy.wait()

    @pl.loop(0, groups)
    def _(step):
        panel_copy(step).wait()
        first = step * group
        sums = [
            row_sums(index_ref, first + member, slots, block, ext, panels.at[first + member])
            for member in range(group)
        ]
        at = 0
        for (_, size, coded), out_ref in zip(plan, outs):
            mine = [total[at : at + size] for total in sums]
            if coded:
                code_into(out_ref, first, block, words, mine)
            else:
                for member in range(group):
                    column = pl.multiple_of((first + member) * block, block)
                    out_ref[:, pl.ds(column, block)] = mine[member]
            at += size


def products(index, parts, blocks):
    rows, slots, block, _ = blocks.shape
    reach, width = parts[0][0].shape[1], parts[0][1].shape[1]
    plan = tuple(part[3:] for part in parts)
    states = sum(size for _, size, _ in plan)
    group, words = 8 if rows % 8 == 0 else 2, rows // 2
    sources = [array for part in parts for array in part[:3]]
    anywhere = pl.BlockSpec(memory_space=pl.ANY)
    out_shape = []
    for _, size, coded in plan:
        if coded:
            out_shape.append(jax.ShapeDtypeStruct((size, (words + 1) * block), jnp.int32))
        else:
            out_shape.append(jax.ShapeDtypeStruct((size, width), jnp.float32))
    return pl.pallas_call(
        functools.partial(products_kernel, plan, group, slots, block, words),
        out_shape=out_shape,
        in_specs=[pl.BlockSpec(memory_space=pltpu.SMEM)]
        + [anywhere] * len(sources)
        + [pl.BlockSpec(memory_space=pltpu.HBM)],
        out_specs=[pl.BlockSpec(memory_space=pltpu.VMEM)] * len(plan),
        scratch_shapes=[
            pltpu.VMEM((states, 2 * reach + width + block), parts[0][1].dtype),
            pltpu.VMEM(blocks.shape, blocks.dtype),
            pltpu.SemaphoreType.DMA((len(sources),)),
            pltpu.SemaphoreType.DMA((rows // group,)),
        ],
        compiler_params=pltpu.CompilerParams(vmem_limit_bytes=VMEM_LIMIT),
        cost_estimate=pl.CostEstimate(flops=1, bytes_accessed=1, transcendentals=0),
        name="products",
    )(index, *sources, pltpu.with_memory_space_constraint(blocks, pltpu.HBM))


def finish_kernel(partials, block, pairs, own_ref, *refs):
    out_ref = refs[-1]
    lane = lax.broadcasted_iota(jnp.int32, (own_ref.shape[0], block), 1)
    levels = [level_of(refs[2 * p + 1][...]) * (1.0 / TOP) for p in range(partials)]
    for pair in range(pairs):
        for half in range(2):
            at = (2 * pair + half) * block
            row = 2 * pair + half
            total = own_ref[:, at : at + block]
            for p in range(partials):
                word = refs[2 * p][:, pair * block : (pair + 1) * block]
                value = (word >> 16) if half else ((word << 16) >> 16)
                level = jnp.max(jnp.where(lane == row, levels[p], 0.0), axis=1, keepdims=True)
                total = total + value.astype(jnp.float32) * level
            out_ref[:, at : at + block] = total.astype(out_ref.dtype)


def finish(own_sums, own_start, coded, coded_start, out, start, size, states, block):
    width = own_sums.shape[1]
    words = width // block // 2
    unit = math.gcd(math.gcd(size, start), math.gcd(start - own_start, start - coded_start))
    own_at, coded_at, out_at = (start - own_start) // unit, (start - coded_start) // unit, start // unit
    in_specs = [pl.BlockSpec((unit, width), lambda i: (own_at + i, 0))]
    operands = [own_sums]
    for array in coded:
        in_specs.append(pl.BlockSpec((unit, words * block), lambda i: (coded_at + i, 0)))
        in_specs.append(pl.BlockSpec((unit, block), lambda i: (coded_at + i, words)))
        operands += [array, array]
    aliases = {}
    if out is not None:
        aliases = {len(operands): 0}
        in_specs.append(pl.BlockSpec(memory_space=pl.ANY))
        operands.append(out)
    return pl.pallas_call(
        functools.partial(finish_kernel, len(coded), block, words),
        out_shape=jax.ShapeDtypeStruct((states, width), jnp.bfloat16),
        grid=(size // unit,),
        in_specs=in_specs,
        out_specs=pl.BlockSpec((unit, width), lambda i: (out_at + i, 0)),
        input_output_aliases=aliases,
        compiler_params=pltpu.CompilerParams(vmem_limit_bytes=VMEM_LIMIT),
        cost_estimate=pl.CostEstimate(
            flops=1, bytes_accessed=1, transcendentals=0
        ),
        name="finish",
    )(*operands)


def starts_of(sizes):
    return [sum(sizes[:i]) for i in range(len(sizes))]


def on_device(vectors, blocks, columns, counts):
    states, width = vectors.shape
    rows, slots, block, _ = blocks.shape
    reach = W * block
    basis_size, state_size = lax.axis_size("basis"), lax.axis_size("state")
    if states % 128 == 0:
        sizes = (states // 4, 3 * states // 8, 3 * states // 8)
        own_sizes = (3 * states // 8, 5 * states // 8)
    else:
        sizes, own_sizes = (states,), (states,)
    starts, own_starts = starts_of(sizes), starts_of(own_sizes)

    slot_index = lax.axis_index("state") * slots + jnp.arange(slots, dtype=jnp.int32)
    relative = columns - (lax.axis_index("basis") * rows - W)
    zeros_at = rows + 2 * W
    index = jnp.where(slot_index[None, :] < counts[:, None], relative, zeros_at).reshape(-1)

    up = [(i, i + 1) for i in range(basis_size - 1)]
    down = [(i + 1, i) for i in range(basis_size - 1)]

    def edges_of(piece, *others):
        edges = (piece[:, width - reach :], piece[:, :reach])
        return lax.optimization_barrier((*edges, *others))[:2] if others else edges

    def halo(edges):
        return lax.ppermute(edges[0], "basis", up), lax.ppermute(edges[1], "basis", down)

    def shifted(piece, shift):
        return lax.ppermute(piece, "state", [(i, (i + shift) % state_size) for i in range(state_size)])

    def own_edges(part, *others):
        return edges_of(vectors[own_starts[part] : own_starts[part] + own_sizes[part]], *others)

    def own_part(part, ends):
        return (ends[0], vectors, ends[1], own_starts[part], own_sizes[part], False)

    def their_part(n):
        return (ends[n][0], theirs[n], ends[n][1], 0, theirs[n].shape[0], True)

    messages = [(shift, c) for shift in range(1, state_size) for c in range(len(sizes))]
    count = len(messages)
    theirs, edges, ends, sent, own_sums, received = [], [], [], [], [], []
    first = halo(own_edges(0))
    for n, (shift, c) in enumerate(messages):
        piece = vectors[starts[c] : starts[c] + sizes[c]]
        theirs.append(shifted(after(piece, theirs[0], *(first if n > 1 else ())) if n else piece, shift))

    def compute(n):
        parts = [their_part(n)]
        if n == min(1, count - 1):
            parts.append(own_part(0, first))
        later = edges[n + 1] if n + 1 < count else ()
        result = products(after(index, *later) if later else index, parts, blocks)
        sent.append(result[0])
        own_sums.extend(result[1:])

    for n in range(count):
        edges.append(edges_of(theirs[n], *(first if n == 0 else ())))
        ends.append(halo(edges[n]))
        if n:
            compute(n - 1)
    if len(own_sizes) > 1:
        last = halo(own_edges(1, *edges[-1], *sent[-1:]))
    compute(count - 1)
    coded = [[] for _ in sizes]
    for n, (shift, c) in enumerate(messages):
        message = after(sent[n], received[n - 1]) if n else sent[n]
        received.append(shifted(message, -shift))
        coded[c].append(received[n])
    if len(own_sizes) > 1:
        own_sums += products(index, [own_part(1, last)], blocks)

    out = None
    for part, own_size in enumerate(own_sizes):
        for c, size in enumerate(sizes):
            at = max(own_starts[part], starts[c])
            end = min(own_starts[part] + own_size, starts[c] + size)
            if at < end:
                out = finish(
                    own_sums[part], own_starts[part], coded[c], starts[c], out, at, end - at, states, block
                )
    return out


def solution(mesh):
    in_specs = (
        P("state", "basis"),
        P("basis", "state", None, None),
        P("basis", "state"),
        P("basis"),
    )
    out_specs = P("state", "basis")
    return jax.shard_map(
        on_device, mesh=mesh, in_specs=in_specs, out_specs=out_specs, check_vma=False
    )
```

```python
import functools
import math

import jax
import jax.numpy as jnp
from jax import lax
from jax.experimental import pallas as pl
from jax.experimental.pallas import tpu as pltpu
from jax.sharding import PartitionSpec as P

W = 36
VMEM_LIMIT = 32 * 1024 * 1024
TOP = 32767.0
FINE = 65536.0
SMALLEST = 2.0**-100


def after(array, *others):
    return lax.optimization_barrier((array, *others))[0]


def fill(sources, plan, ext, sems):
    copies, at = [], 0
    for part, (starts, size, _) in enumerate(plan):
        column = 0
        for n in range(3 * part, 3 * part + 3):
            width = sources[n].shape[1]
            source = sources[n].at[pl.ds(starts[n - 3 * part], size)]
            target = ext.at[pl.ds(at, size), pl.ds(column, width)]
            copies.append(pltpu.make_async_copy(source, target, sems.at[n]))
            column += width
        at += size
    for copy in copies:
        copy.start()
    return copies


def row_sums(index_ref, row, slots, block, ext, panel_ref):
    picked = jnp.concatenate(
        [
            ext[:, pl.ds(pl.multiple_of(index_ref[row * slots + slot] * block, block), block)]
            for slot in range(slots)
        ],
        axis=1,
    )
    panel = jnp.concatenate([panel_ref[slot] for slot in range(slots)], axis=1)
    return lax.dot_general(
        picked, panel, (((1,), (1,)), ((), ())), preferred_element_type=jnp.float32
    )


def level_code(top):
    return jnp.ceil(jnp.log2(jnp.maximum(top, SMALLEST)) * FINE).astype(jnp.int32)


def level_of(code):
    return jnp.exp2(code.astype(jnp.float32) * (1.0 / FINE))


def code_into(out_ref, first, block, words, sums):
    lane = lax.broadcasted_iota(jnp.int32, (out_ref.shape[0], block), 1)
    codes = out_ref[:, words * block :]
    values = []
    for member, mine in enumerate(sums):
        code = level_code(jnp.max(jnp.abs(mine), axis=1, keepdims=True))
        codes = jnp.where(lane == first + member, code, codes)
        scaled = jnp.round(mine * (TOP / level_of(code)))
        values.append(jnp.clip(scaled, -TOP, TOP).astype(jnp.int32))
    out_ref[:, words * block :] = codes
    for pair in range(len(sums) // 2):
        word = (values[2 * pair + 1] << 16) | (values[2 * pair] & 0xFFFF)
        at = pl.multiple_of((first // 2 + pair) * block, block)
        out_ref[:, pl.ds(at, block)] = word


def products_kernel(plan, group, slots, block, words, index_ref, *refs):
    parts = len(plan)
    sources, blocks_ref = refs[: 3 * parts], refs[3 * parts]
    outs, (ext, panels, sems, panel_sems) = refs[3 * parts + 1 : 4 * parts + 1], refs[4 * parts + 1 :]
    groups = panels.shape[0] // group

    def panel_copy(step):
        rows = pl.ds(step * group, group)
        return pltpu.make_async_copy(blocks_ref.at[rows], panels.at[rows], panel_sems.at[step])

    copies = fill(sources, plan, ext, sems)
    for step in range(groups):
        panel_copy(step).start()
    end = ext.shape[1] - block
    ext[:, end:] = jnp.zeros((ext.shape[0], block), ext.dtype)
    for (_, size, coded), out_ref in zip(plan, outs):
        if coded:
            out_ref[:, words * block :] = jnp.zeros((size, block), jnp.int32)
    for copy in copies:
        copy.wait()

    @pl.loop(0, groups)
    def _(step):
        panel_copy(step).wait()
        first = step * group
        sums = [
            row_sums(index_ref, first + member, slots, block, ext, panels.at[first + member])
            for member in range(group)
        ]
        at = 0
        for (_, size, coded), out_ref in zip(plan, outs):
            mine = [total[at : at + size] for total in sums]
            if coded:
                code_into(out_ref, first, block, words, mine)
            else:
                for member in range(group):
                    column = pl.multiple_of((first + member) * block, block)
                    out_ref[:, pl.ds(column, block)] = mine[member]
            at += size


def products(index, parts, blocks):
    rows, slots, block, _ = blocks.shape
    reach, width = parts[0][0].shape[1], parts[0][1].shape[1]
    plan = tuple(part[3:] for part in parts)
    states = sum(size for _, size, _ in plan)
    group, words = 8 if rows % 8 == 0 else 2, rows // 2
    sources = [array for part in parts for array in part[:3]]
    anywhere = pl.BlockSpec(memory_space=pl.ANY)
    out_shape = []
    for _, size, coded in plan:
        if coded:
            out_shape.append(jax.ShapeDtypeStruct((size, (words + 1) * block), jnp.int32))
        else:
            out_shape.append(jax.ShapeDtypeStruct((size, width), jnp.float32))
    return pl.pallas_call(
        functools.partial(products_kernel, plan, group, slots, block, words),
        out_shape=out_shape,
        in_specs=[pl.BlockSpec(memory_space=pltpu.SMEM)]
        + [anywhere] * len(sources)
        + [pl.BlockSpec(memory_space=pltpu.HBM)],
        out_specs=[pl.BlockSpec(memory_space=pltpu.VMEM)] * len(plan),
        scratch_shapes=[
            pltpu.VMEM((states, 2 * reach + width + block), parts[0][1].dtype),
            pltpu.VMEM(blocks.shape, blocks.dtype),
            pltpu.SemaphoreType.DMA((len(sources),)),
            pltpu.SemaphoreType.DMA((rows // group,)),
        ],
        compiler_params=pltpu.CompilerParams(vmem_limit_bytes=VMEM_LIMIT),
        cost_estimate=pl.CostEstimate(flops=1, bytes_accessed=1, transcendentals=0),
        name="products",
    )(index, *sources, pltpu.with_memory_space_constraint(blocks, pltpu.HBM))


def finish_kernel(partials, block, pairs, own_ref, *refs):
    out_ref = refs[-1]
    lane = lax.broadcasted_iota(jnp.int32, (own_ref.shape[0], block), 1)
    levels = [level_of(refs[2 * p + 1][...]) * (1.0 / TOP) for p in range(partials)]
    for pair in range(pairs):
        for half in range(2):
            at = (2 * pair + half) * block
            row = 2 * pair + half
            total = own_ref[:, at : at + block]
            for p in range(partials):
                word = refs[2 * p][:, pair * block : (pair + 1) * block]
                value = (word >> 16) if half else ((word << 16) >> 16)
                level = jnp.max(jnp.where(lane == row, levels[p], 0.0), axis=1, keepdims=True)
                total = total + value.astype(jnp.float32) * level
            out_ref[:, at : at + block] = total.astype(out_ref.dtype)


def finish(own_sums, own_start, coded, coded_start, out, start, size, states, block):
    width = own_sums.shape[1]
    words = width // block // 2
    unit = math.gcd(math.gcd(size, start), math.gcd(start - own_start, start - coded_start))
    own_at, coded_at, out_at = (start - own_start) // unit, (start - coded_start) // unit, start // unit
    in_specs = [pl.BlockSpec((unit, width), lambda i: (own_at + i, 0))]
    operands = [own_sums]
    for array in coded:
        in_specs.append(pl.BlockSpec((unit, words * block), lambda i: (coded_at + i, 0)))
        in_specs.append(pl.BlockSpec((unit, block), lambda i: (coded_at + i, words)))
        operands += [array, array]
    aliases = {}
    if out is not None:
        aliases = {len(operands): 0}
        in_specs.append(pl.BlockSpec(memory_space=pl.ANY))
        operands.append(out)
    return pl.pallas_call(
        functools.partial(finish_kernel, len(coded), block, words),
        out_shape=jax.ShapeDtypeStruct((states, width), jnp.bfloat16),
        grid=(size // unit,),
        in_specs=in_specs,
        out_specs=pl.BlockSpec((unit, width), lambda i: (out_at + i, 0)),
        input_output_aliases=aliases,
        compiler_params=pltpu.CompilerParams(vmem_limit_bytes=VMEM_LIMIT),
        cost_estimate=pl.CostEstimate(
            flops=1, bytes_accessed=1, transcendentals=0
        ),
        name="finish",
    )(*operands)


def starts_of(sizes):
    return [sum(sizes[:i]) for i in range(len(sizes))]


def on_device(vectors, blocks, columns, counts):
    states, width = vectors.shape
    rows, slots, block, _ = blocks.shape
    reach = W * block
    basis_size, state_size = lax.axis_size("basis"), lax.axis_size("state")
    if states % 128 == 0:
        sizes = (states // 4, 3 * states // 8, 3 * states // 8)
        own_sizes = (states // 2, states // 2)
    else:
        sizes, own_sizes = (states,), (states,)
    starts, own_starts = starts_of(sizes), starts_of(own_sizes)

    slot_index = lax.axis_index("state") * slots + jnp.arange(slots, dtype=jnp.int32)
    relative = columns - (lax.axis_index("basis") * rows - W)
    zeros_at = rows + 2 * W
    index = jnp.where(slot_index[None, :] < counts[:, None], relative, zeros_at).reshape(-1)

    up = [(i, i + 1) for i in range(basis_size - 1)]
    down = [(i + 1, i) for i in range(basis_size - 1)]

    def halo(piece, *others):
        edges = (piece[:, width - reach :], piece[:, :reach])
        if others:
            edges = lax.optimization_barrier((*edges, *others))[:2]
        return edges, (lax.ppermute(edges[0], "basis", up), lax.ppermute(edges[1], "basis", down))

    def shifted(piece, shift):
        return lax.ppermute(piece, "state", [(i, (i + shift) % state_size) for i in range(state_size)])

    def own_part(part):
        start = own_starts[part]
        return (own_left, vectors, own_rights[part], (start, start, 0), own_sizes[part], False)

    def their_part(n):
        return (ends[n][0], theirs[n], ends[n][1], (0, 0, 0), theirs[n].shape[0], True)

    messages = [(shift, c) for shift in range(1, state_size) for c in range(len(sizes))]
    count = len(messages)
    theirs, edges, ends, sent, received = [], [], [], [], []
    own_edge = vectors[:, width - reach :]
    own_left = lax.ppermute(own_edge, "basis", up)
    for n, (shift, c) in enumerate(messages):
        piece = vectors[starts[c] : starts[c] + sizes[c]]
        if n:
            piece = after(piece, *((own_edge,) if n == 1 else (theirs[0], own_left)))
        theirs.append(shifted(piece, shift))

    def compute(n):
        later = edges[n + 1] if n + 1 < count else ()
        sent.extend(products(after(index, *later) if later else index, [their_part(n)], blocks))

    for n in range(count):
        pair = halo(theirs[n], *((own_left,) if n == 1 else ()))
        edges.append(pair[0])
        ends.append(pair[1])
        if n:
            compute(n - 1)
    own_rights = []
    for at, size in zip(own_starts, own_sizes):
        edge = after(vectors[at : at + size, :reach], *(ends[-1] if at else edges[-1]), *sent[-1:])
        own_rights.append(lax.ppermute(edge, "basis", down))
    compute(count - 1)
    coded = [[] for _ in sizes]
    for n, (shift, c) in enumerate(messages):
        message = after(sent[n], received[n - 2 + 1]) if n > 0 else sent[n]
        received.append(shifted(message, -shift))
        coded[c].append(received[n])
    own_sums = [products(index, [own_part(part)], blocks)[0] for part in range(len(own_sizes))]

    out = None
    for part, own_size in enumerate(own_sizes):
        for c, size in enumerate(sizes):
            at = max(own_starts[part], starts[c])
            end = min(own_starts[part] + own_size, starts[c] + size)
            if at < end:
                out = finish(
                    own_sums[part], own_starts[part], coded[c], starts[c], out, at, end - at, states, block
                )
    return out


def solution(mesh):
    in_specs = (
        P("state", "basis"),
        P("basis", "state", None, None),
        P("basis", "state"),
        P("basis"),
    )
    out_specs = P("state", "basis")
    return jax.shard_map(
        on_device, mesh=mesh, in_specs=in_specs, out_specs=out_specs, check_vma=False
    )
```

```python
import functools
import math

import jax
import jax.numpy as jnp
from jax import lax
from jax.experimental import pallas as pl
from jax.experimental.pallas import tpu as pltpu
from jax.sharding import PartitionSpec as P

W = 36
VMEM_LIMIT = 32 * 1024 * 1024
TOP = 32767.0
FINE = 65536.0
SMALLEST = 2.0**-100


def after(array, *others):
    return lax.optimization_barrier((array, *others))[0]


def fill(sources, plan, ext, sems):
    copies, at = [], 0
    for part, (start, size, _) in enumerate(plan):
        left, own, right = sources[3 * part : 3 * part + 3]
        reach, width = left.shape[1], own.shape[1]
        rows = pl.ds(at, size)
        copies += [
            pltpu.make_async_copy(left, ext.at[rows, pl.ds(0, reach)], sems.at[3 * part]),
            pltpu.make_async_copy(
                own.at[pl.ds(start, size)], ext.at[rows, pl.ds(reach, width)], sems.at[3 * part + 1]
            ),
            pltpu.make_async_copy(right, ext.at[rows, pl.ds(reach + width, reach)], sems.at[3 * part + 2]),
        ]
        at += size
    for copy in copies:
        copy.start()
    return copies


def row_sums(index_ref, row, slots, block, ext, panel_ref):
    picked = jnp.concatenate(
        [
            ext[:, pl.ds(pl.multiple_of(index_ref[row * slots + slot] * block, block), block)]
            for slot in range(slots)
        ],
        axis=1,
    )
    panel = jnp.concatenate([panel_ref[slot] for slot in range(slots)], axis=1)
    return lax.dot_general(
        picked, panel, (((1,), (1,)), ((), ())), preferred_element_type=jnp.float32
    )


def level_code(top):
    return jnp.ceil(jnp.log2(jnp.maximum(top, SMALLEST)) * FINE).astype(jnp.int32)


def level_of(code):
    return jnp.exp2(code.astype(jnp.float32) * (1.0 / FINE))


def code_into(out_ref, first, block, words, sums):
    lane = lax.broadcasted_iota(jnp.int32, (out_ref.shape[0], block), 1)
    codes = out_ref[:, words * block :]
    values = []
    for member, mine in enumerate(sums):
        code = level_code(jnp.max(jnp.abs(mine), axis=1, keepdims=True))
        codes = jnp.where(lane == first + member, code, codes)
        scaled = jnp.round(mine * (TOP / level_of(code)))
        values.append(jnp.clip(scaled, -TOP, TOP).astype(jnp.int32))
    out_ref[:, words * block :] = codes
    for pair in range(len(sums) // 2):
        word = (values[2 * pair + 1] << 16) | (values[2 * pair] & 0xFFFF)
        at = pl.multiple_of((first // 2 + pair) * block, block)
        out_ref[:, pl.ds(at, block)] = word


def products_kernel(plan, group, slots, block, words, index_ref, *refs):
    parts = len(plan)
    sources, blocks_ref = refs[: 3 * parts], refs[3 * parts]
    outs, (ext, panels, sems, panel_sems) = refs[3 * parts + 1 : 4 * parts + 1], refs[4 * parts + 1 :]
    groups = panels.shape[0] // group

    def panel_copy(step):
        rows = pl.ds(step * group, group)
        return pltpu.make_async_copy(blocks_ref.at[rows], panels.at[rows], panel_sems.at[step])

    copies = fill(sources, plan, ext, sems)
    for step in range(groups):
        panel_copy(step).start()
    end = ext.shape[1] - block
    ext[:, end:] = jnp.zeros((ext.shape[0], block), ext.dtype)
    for (_, size, coded), out_ref in zip(plan, outs):
        if coded:
            out_ref[:, words * block :] = jnp.zeros((size, block), jnp.int32)
    for copy in copies:
        copy.wait()

    @pl.loop(0, groups)
    def _(step):
        panel_copy(step).wait()
        first = step * group
        sums = [
            row_sums(index_ref, first + member, slots, block, ext, panels.at[first + member])
            for member in range(group)
        ]
        at = 0
        for (_, size, coded), out_ref in zip(plan, outs):
            mine = [total[at : at + size] for total in sums]
            if coded:
                code_into(out_ref, first, block, words, mine)
            else:
                for member in range(group):
                    column = pl.multiple_of((first + member) * block, block)
                    out_ref[:, pl.ds(column, block)] = mine[member]
            at += size


def products(index, parts, blocks):
    rows, slots, block, _ = blocks.shape
    reach, width = parts[0][0].shape[1], parts[0][1].shape[1]
    plan = tuple(part[3:] for part in parts)
    states = sum(size for _, size, _ in plan)
    group, words = 8 if rows % 8 == 0 else 2, rows // 2
    sources = [array for part in parts for array in part[:3]]
    anywhere = pl.BlockSpec(memory_space=pl.ANY)
    out_shape = []
    for _, size, coded in plan:
        if coded:
            out_shape.append(jax.ShapeDtypeStruct((size, (words + 1) * block), jnp.int32))
        else:
            out_shape.append(jax.ShapeDtypeStruct((size, width), jnp.float32))
    return pl.pallas_call(
        functools.partial(products_kernel, plan, group, slots, block, words),
        out_shape=out_shape,
        in_specs=[pl.BlockSpec(memory_space=pltpu.SMEM)]
        + [anywhere] * len(sources)
        + [pl.BlockSpec(memory_space=pltpu.HBM)],
        out_specs=[pl.BlockSpec(memory_space=pltpu.VMEM)] * len(plan),
        scratch_shapes=[
            pltpu.VMEM((states, 2 * reach + width + block), parts[0][1].dtype),
            pltpu.VMEM(blocks.shape, blocks.dtype),
            pltpu.SemaphoreType.DMA((len(sources),)),
            pltpu.SemaphoreType.DMA((rows // group,)),
        ],
        compiler_params=pltpu.CompilerParams(vmem_limit_bytes=VMEM_LIMIT),
        cost_estimate=pl.CostEstimate(flops=1, bytes_accessed=1, transcendentals=0),
        name="products",
    )(index, *sources, pltpu.with_memory_space_constraint(blocks, pltpu.HBM))


def finish_kernel(partials, block, pairs, own_ref, *refs):
    out_ref = refs[-1]
    lane = lax.broadcasted_iota(jnp.int32, (own_ref.shape[0], block), 1)
    levels = [level_of(refs[2 * p + 1][...]) * (1.0 / TOP) for p in range(partials)]
    for pair in range(pairs):
        for half in range(2):
            at = (2 * pair + half) * block
            row = 2 * pair + half
            total = own_ref[:, at : at + block]
            for p in range(partials):
                word = refs[2 * p][:, pair * block : (pair + 1) * block]
                value = (word >> 16) if half else ((word << 16) >> 16)
                level = jnp.max(jnp.where(lane == row, levels[p], 0.0), axis=1, keepdims=True)
                total = total + value.astype(jnp.float32) * level
            out_ref[:, at : at + block] = total.astype(out_ref.dtype)


def finish(own_sums, own_start, coded, coded_start, out, start, size, states, block):
    width = own_sums.shape[1]
    words = width // block // 2
    unit = math.gcd(math.gcd(size, start), math.gcd(start - own_start, start - coded_start))
    own_at, coded_at, out_at = (start - own_start) // unit, (start - coded_start) // unit, start // unit
    in_specs = [pl.BlockSpec((unit, width), lambda i: (own_at + i, 0))]
    operands = [own_sums]
    for array in coded:
        in_specs.append(pl.BlockSpec((unit, words * block), lambda i: (coded_at + i, 0)))
        in_specs.append(pl.BlockSpec((unit, block), lambda i: (coded_at + i, words)))
        operands += [array, array]
    aliases = {}
    if out is not None:
        aliases = {len(operands): 0}
        in_specs.append(pl.BlockSpec(memory_space=pl.ANY))
        operands.append(out)
    return pl.pallas_call(
        functools.partial(finish_kernel, len(coded), block, words),
        out_shape=jax.ShapeDtypeStruct((states, width), jnp.bfloat16),
        grid=(size // unit,),
        in_specs=in_specs,
        out_specs=pl.BlockSpec((unit, width), lambda i: (out_at + i, 0)),
        input_output_aliases=aliases,
        compiler_params=pltpu.CompilerParams(vmem_limit_bytes=VMEM_LIMIT),
        cost_estimate=pl.CostEstimate(
            flops=1, bytes_accessed=1, transcendentals=0
        ),
        name="finish",
    )(*operands)


def starts_of(sizes):
    return [sum(sizes[:i]) for i in range(len(sizes))]


def on_device(vectors, blocks, columns, counts):
    states, width = vectors.shape
    rows, slots, block, _ = blocks.shape
    reach = W * block
    basis_size, state_size = lax.axis_size("basis"), lax.axis_size("state")
    if states % 128 == 0:
        sizes = (3 * states // 8, 3 * states // 8, states // 4)
        own_sizes = (states // 2, states // 2)
    else:
        sizes, own_sizes = (states,), (states,)
    starts, own_starts = starts_of(sizes), starts_of(own_sizes)

    slot_index = lax.axis_index("state") * slots + jnp.arange(slots, dtype=jnp.int32)
    relative = columns - (lax.axis_index("basis") * rows - W)
    zeros_at = rows + 2 * W
    index = jnp.where(slot_index[None, :] < counts[:, None], relative, zeros_at).reshape(-1)

    up = [(i, i + 1) for i in range(basis_size - 1)]
    down = [(i + 1, i) for i in range(basis_size - 1)]

    def edges_of(piece, *others):
        edges = (piece[:, width - reach :], piece[:, :reach])
        return lax.optimization_barrier((*edges, *others))[:2] if others else edges

    def halo(edges):
        return lax.ppermute(edges[0], "basis", up), lax.ppermute(edges[1], "basis", down)

    def shifted(piece, shift):
        return lax.ppermute(piece, "state", [(i, (i + shift) % state_size) for i in range(state_size)])

    def own_edges(part, *others):
        return edges_of(vectors[own_starts[part] : own_starts[part] + own_sizes[part]], *others)

    def own_part(part, ends):
        return (ends[0], vectors, ends[1], own_starts[part], own_sizes[part], False)

    def their_part(n):
        return (ends[n][0], theirs[n], ends[n][1], 0, theirs[n].shape[0], True)

    messages = [(shift, c) for shift in range(1, state_size) for c in range(len(sizes))]
    count = len(messages)
    theirs, edges, ends, sent, own_sums, received = [], [], [], [], [], []
    first_edges = own_edges(0)
    first = halo(first_edges)
    for n, (shift, c) in enumerate(messages):
        piece = vectors[starts[c] : starts[c] + sizes[c]]
        if n:
            piece = after(piece, *(first_edges if n == 1 else first))
        theirs.append(shifted(piece, shift))

    def compute(n):
        parts = [their_part(n)]
        if n == min(1, count - 1):
            parts.append(own_part(0, first))
        later = edges[n + 1] if n + 1 < len(edges) else ()
        result = products(after(index, *later) if later else index, parts, blocks)
        sent.append(result[0])
        own_sums.extend(result[1:])

    for n in range(count):
        edges.append(edges_of(theirs[n], *(first if n == 0 else ())))
        ends.append(halo(edges[n]))
        if n:
            compute(n - 1)
    if len(own_sizes) > 1:
        edges.append(own_edges(1, *ends[-1], *sent[-1:]))
        last = halo(edges[-1])
    compute(count - 1)
    coded = [[] for _ in sizes]
    for n, (shift, c) in enumerate(messages):
        message = after(sent[n], received[n - 1]) if n else sent[n]
        received.append(shifted(message, -shift))
        coded[c].append(received[n])
    if len(own_sizes) > 1:
        own_sums += products(index, [own_part(1, last)], blocks)

    out = None
    for part, own_size in enumerate(own_sizes):
        for c, size in enumerate(sizes):
            at = max(own_starts[part], starts[c])
            end = min(own_starts[part] + own_size, starts[c] + size)
            if at < end:
                out = finish(
                    own_sums[part], own_starts[part], coded[c], starts[c], out, at, end - at, states, block
                )
    return out


def solution(mesh):
    in_specs = (
        P("state", "basis"),
        P("basis", "state", None, None),
        P("basis", "state"),
        P("basis"),
    )
    out_specs = P("state", "basis")
    return jax.shard_map(
        on_device, mesh=mesh, in_specs=in_specs, out_specs=out_specs, check_vma=False
    )
```

```python
import functools
import math

import jax
import jax.numpy as jnp
from jax import lax
from jax.experimental import pallas as pl
from jax.experimental.pallas import tpu as pltpu
from jax.sharding import PartitionSpec as P

W = 36
VMEM_LIMIT = 32 * 1024 * 1024
TOP = 32767.0
FINE = 65536.0
SMALLEST = 2.0**-100


def after(array, *others):
    return lax.optimization_barrier((array, *others))[0]


def fill(sources, plan, ext, sems):
    copies, at = [], 0
    for part, (start, size, _) in enumerate(plan):
        left, own, right = sources[3 * part : 3 * part + 3]
        reach, width = left.shape[1], own.shape[1]
        rows = pl.ds(at, size)
        copies += [
            pltpu.make_async_copy(left, ext.at[rows, pl.ds(0, reach)], sems.at[3 * part]),
            pltpu.make_async_copy(
                own.at[pl.ds(start, size)], ext.at[rows, pl.ds(reach, width)], sems.at[3 * part + 1]
            ),
            pltpu.make_async_copy(right, ext.at[rows, pl.ds(reach + width, reach)], sems.at[3 * part + 2]),
        ]
        at += size
    for copy in copies:
        copy.start()
    return copies


def row_sums(index_ref, row, slots, block, ext, panel_ref):
    picked = jnp.concatenate(
        [
            ext[:, pl.ds(pl.multiple_of(index_ref[row * slots + slot] * block, block), block)]
            for slot in range(slots)
        ],
        axis=1,
    )
    panel = jnp.concatenate([panel_ref[slot] for slot in range(slots)], axis=1)
    return lax.dot_general(
        picked, panel, (((1,), (1,)), ((), ())), preferred_element_type=jnp.float32
    )


def level_code(top):
    return jnp.ceil(jnp.log2(jnp.maximum(top, SMALLEST)) * FINE).astype(jnp.int32)


def level_of(code):
    return jnp.exp2(code.astype(jnp.float32) * (1.0 / FINE))


def code_into(out_ref, first, block, words, sums):
    lane = lax.broadcasted_iota(jnp.int32, (out_ref.shape[0], block), 1)
    codes = out_ref[:, words * block :]
    values = []
    for member, mine in enumerate(sums):
        code = level_code(jnp.max(jnp.abs(mine), axis=1, keepdims=True))
        codes = jnp.where(lane == first + member, code, codes)
        scaled = jnp.round(mine * (TOP / level_of(code)))
        values.append(jnp.clip(scaled, -TOP, TOP).astype(jnp.int32))
    out_ref[:, words * block :] = codes
    for pair in range(len(sums) // 2):
        word = (values[2 * pair + 1] << 16) | (values[2 * pair] & 0xFFFF)
        at = pl.multiple_of((first // 2 + pair) * block, block)
        out_ref[:, pl.ds(at, block)] = word


def products_kernel(plan, group, slots, block, words, index_ref, *refs):
    parts = len(plan)
    sources, blocks_ref = refs[: 3 * parts], refs[3 * parts]
    outs, (ext, panels, sems, panel_sems) = refs[3 * parts + 1 : 4 * parts + 1], refs[4 * parts + 1 :]
    groups = panels.shape[0] // group
    half = group // 2

    def panel_copies(step):
        return [
            pltpu.make_async_copy(
                blocks_ref.at[pl.ds(step * group + at, half)],
                panels.at[pl.ds(step * group + at, half)],
                panel_sems.at[2 * step + at // half],
            )
            for at in (0, half)
        ]

    copies = fill(sources, plan, ext, sems)
    for copy in panel_copies(0):
        copy.start()
    end = ext.shape[1] - block
    ext[:, end:] = jnp.zeros((ext.shape[0], block), ext.dtype)
    for (_, size, coded), out_ref in zip(plan, outs):
        if coded:
            out_ref[:, words * block :] = jnp.zeros((size, block), jnp.int32)
    for copy in copies:
        copy.wait()

    @pl.loop(0, groups)
    def _(step):
        for copy in panel_copies(step):
            copy.wait()

        @pl.when(step + 1 < groups)
        def _():
            for copy in panel_copies(step + 1):
                copy.start()

        first = step * group
        sums = [
            row_sums(index_ref, first + member, slots, block, ext, panels.at[first + member])
            for member in range(group)
        ]
        at = 0
        for (_, size, coded), out_ref in zip(plan, outs):
            mine = [total[at : at + size] for total in sums]
            if coded:
                code_into(out_ref, first, block, words, mine)
            else:
                for member in range(group):
                    column = pl.multiple_of((first + member) * block, block)
                    out_ref[:, pl.ds(column, block)] = mine[member]
            at += size


def products(index, parts, blocks):
    rows, slots, block, _ = blocks.shape
    reach, width = parts[0][0].shape[1], parts[0][1].shape[1]
    plan = tuple(part[3:] for part in parts)
    states = sum(size for _, size, _ in plan)
    group, words = 8 if rows % 8 == 0 else 2, rows // 2
    sources = [array for part in parts for array in part[:3]]
    anywhere = pl.BlockSpec(memory_space=pl.ANY)
    out_shape = []
    for _, size, coded in plan:
        if coded:
            out_shape.append(jax.ShapeDtypeStruct((size, (words + 1) * block), jnp.int32))
        else:
            out_shape.append(jax.ShapeDtypeStruct((size, width), jnp.float32))
    return pl.pallas_call(
        functools.partial(products_kernel, plan, group, slots, block, words),
        out_shape=out_shape,
        in_specs=[pl.BlockSpec(memory_space=pltpu.SMEM)]
        + [anywhere] * len(sources)
        + [pl.BlockSpec(memory_space=pltpu.HBM)],
        out_specs=[pl.BlockSpec(memory_space=pltpu.VMEM)] * len(plan),
        scratch_shapes=[
            pltpu.VMEM((states, 2 * reach + width + block), parts[0][1].dtype),
            pltpu.VMEM(blocks.shape, blocks.dtype),
            pltpu.SemaphoreType.DMA((len(sources),)),
            pltpu.SemaphoreType.DMA((2 * rows // group,)),
        ],
        compiler_params=pltpu.CompilerParams(vmem_limit_bytes=VMEM_LIMIT),
        cost_estimate=pl.CostEstimate(flops=1, bytes_accessed=1, transcendentals=0),
        name="products",
    )(index, *sources, pltpu.with_memory_space_constraint(blocks, pltpu.HBM))


def finish_kernel(partials, block, pairs, own_ref, *refs):
    out_ref = refs[-1]
    lane = lax.broadcasted_iota(jnp.int32, (own_ref.shape[0], block), 1)
    levels = [level_of(refs[2 * p + 1][...]) * (1.0 / TOP) for p in range(partials)]
    for pair in range(pairs):
        for half in range(2):
            at = (2 * pair + half) * block
            row = 2 * pair + half
            total = own_ref[:, at : at + block]
            for p in range(partials):
                word = refs[2 * p][:, pair * block : (pair + 1) * block]
                value = (word >> 16) if half else ((word << 16) >> 16)
                level = jnp.max(jnp.where(lane == row, levels[p], 0.0), axis=1, keepdims=True)
                total = total + value.astype(jnp.float32) * level
            out_ref[:, at : at + block] = total.astype(out_ref.dtype)


def finish(own_sums, own_start, coded, coded_start, out, start, size, states, block):
    width = own_sums.shape[1]
    words = width // block // 2
    unit = math.gcd(math.gcd(size, start), math.gcd(start - own_start, start - coded_start))
    own_at, coded_at, out_at = (start - own_start) // unit, (start - coded_start) // unit, start // unit
    in_specs = [pl.BlockSpec((unit, width), lambda i: (own_at + i, 0))]
    operands = [own_sums]
    for array in coded:
        in_specs.append(pl.BlockSpec((unit, words * block), lambda i: (coded_at + i, 0)))
        in_specs.append(pl.BlockSpec((unit, block), lambda i: (coded_at + i, words)))
        operands += [array, array]
    aliases = {}
    if out is not None:
        aliases = {len(operands): 0}
        in_specs.append(pl.BlockSpec(memory_space=pl.ANY))
        operands.append(out)
    return pl.pallas_call(
        functools.partial(finish_kernel, len(coded), block, words),
        out_shape=jax.ShapeDtypeStruct((states, width), jnp.bfloat16),
        grid=(size // unit,),
        in_specs=in_specs,
        out_specs=pl.BlockSpec((unit, width), lambda i: (out_at + i, 0)),
        input_output_aliases=aliases,
        compiler_params=pltpu.CompilerParams(vmem_limit_bytes=VMEM_LIMIT),
        cost_estimate=pl.CostEstimate(
            flops=1, bytes_accessed=1, transcendentals=0
        ),
        name="finish",
    )(*operands)


def starts_of(sizes):
    return [sum(sizes[:i]) for i in range(len(sizes))]


def on_device(vectors, blocks, columns, counts):
    states, width = vectors.shape
    rows, slots, block, _ = blocks.shape
    reach = W * block
    basis_size, state_size = lax.axis_size("basis"), lax.axis_size("state")
    if states % 128 == 0:
        sizes = (3 * states // 8, 3 * states // 8, states // 4)
        own_sizes = (3 * states // 8, 5 * states // 8)
    else:
        sizes, own_sizes = (states,), (states,)
    starts, own_starts = starts_of(sizes), starts_of(own_sizes)

    slot_index = lax.axis_index("state") * slots + jnp.arange(slots, dtype=jnp.int32)
    relative = columns - (lax.axis_index("basis") * rows - W)
    zeros_at = rows + 2 * W
    index = jnp.where(slot_index[None, :] < counts[:, None], relative, zeros_at).reshape(-1)

    up = [(i, i + 1) for i in range(basis_size - 1)]
    down = [(i + 1, i) for i in range(basis_size - 1)]

    def edges_of(piece, *others):
        edges = (piece[:, width - reach :], piece[:, :reach])
        return lax.optimization_barrier((*edges, *others))[:2] if others else edges

    def halo(edges):
        return lax.ppermute(edges[0], "basis", up), lax.ppermute(edges[1], "basis", down)

    def shifted(piece, shift):
        return lax.ppermute(piece, "state", [(i, (i + shift) % state_size) for i in range(state_size)])

    def own_edges(part, *others):
        return edges_of(vectors[own_starts[part] : own_starts[part] + own_sizes[part]], *others)

    def own_part(part, ends):
        return (ends[0], vectors, ends[1], own_starts[part], own_sizes[part], False)

    def their_part(n):
        return (ends[n][0], theirs[n], ends[n][1], 0, theirs[n].shape[0], True)

    messages = [(shift, c) for shift in range(1, state_size) for c in range(len(sizes))]
    count = len(messages)
    theirs, edges, ends, sent, own_sums, received = [], [], [], [], [], []
    first_edges = own_edges(0)
    first = halo(first_edges)
    for n, (shift, c) in enumerate(messages):
        piece = vectors[starts[c] : starts[c] + sizes[c]]
        if n:
            piece = after(piece, *(first_edges if n == 1 else first))
        theirs.append(shifted(piece, shift))

    def compute(n):
        parts = [their_part(n)]
        if n == min(1, count - 1):
            parts.append(own_part(0, first))
        later = edges[n + 1] if n + 1 < len(edges) else ()
        result = products(after(index, *later) if later else index, parts, blocks)
        sent.append(result[0])
        own_sums.extend(result[1:])

    for n in range(count):
        edges.append(edges_of(theirs[n], *(first if n == 0 else ())))
        ends.append(halo(edges[n]))
        if n:
            compute(n - 1)
    if len(own_sizes) > 1:
        edges.append(own_edges(1, *ends[-1], *sent[-1:]))
        last = halo(edges[-1])
    compute(count - 1)
    coded = [[] for _ in sizes]
    for n, (shift, c) in enumerate(messages):
        message = after(sent[n], received[n - 1]) if n else sent[n]
        received.append(shifted(message, -shift))
        coded[c].append(received[n])
    if len(own_sizes) > 1:
        own_sums += products(index, [own_part(1, last)], blocks)

    out = None
    for part, own_size in enumerate(own_sizes):
        for c, size in enumerate(sizes):
            at = max(own_starts[part], starts[c])
            end = min(own_starts[part] + own_size, starts[c] + size)
            if at < end:
                out = finish(
                    own_sums[part], own_starts[part], coded[c], starts[c], out, at, end - at, states, block
                )
    return out


def solution(mesh):
    in_specs = (
        P("state", "basis"),
        P("basis", "state", None, None),
        P("basis", "state"),
        P("basis"),
    )
    out_specs = P("state", "basis")
    return jax.shard_map(
        on_device, mesh=mesh, in_specs=in_specs, out_specs=out_specs, check_vma=False
    )
```

```python
import functools
import math

import jax
import jax.numpy as jnp
from jax import lax
from jax.experimental import pallas as pl
from jax.experimental.pallas import tpu as pltpu
from jax.sharding import PartitionSpec as P

W = 36
VMEM_LIMIT = 32 * 1024 * 1024
TOP = 32767.0
FINE = 65536.0
SMALLEST = 2.0**-100


def after(array, *others):
    return lax.optimization_barrier((array, *others))[0]


def fill(sources, plan, ext, sems):
    copies, at = [], 0
    for part, (start, size, _) in enumerate(plan):
        left, own, right = sources[3 * part : 3 * part + 3]
        reach, width = left.shape[1], own.shape[1]
        rows = pl.ds(at, size)
        copies += [
            pltpu.make_async_copy(left, ext.at[rows, pl.ds(0, reach)], sems.at[3 * part]),
            pltpu.make_async_copy(
                own.at[pl.ds(start, size)], ext.at[rows, pl.ds(reach, width)], sems.at[3 * part + 1]
            ),
            pltpu.make_async_copy(right, ext.at[rows, pl.ds(reach + width, reach)], sems.at[3 * part + 2]),
        ]
        at += size
    for copy in copies:
        copy.start()
    return copies


def row_sums(index_ref, row, slots, block, ext, panel_ref):
    picked = jnp.concatenate(
        [
            ext[:, pl.ds(pl.multiple_of(index_ref[row * slots + slot] * block, block), block)]
            for slot in range(slots)
        ],
        axis=1,
    )
    panel = jnp.concatenate([panel_ref[slot] for slot in range(slots)], axis=1)
    return lax.dot_general(
        picked, panel, (((1,), (1,)), ((), ())), preferred_element_type=jnp.float32
    )


def level_code(top):
    return jnp.ceil(jnp.log2(jnp.maximum(top, SMALLEST)) * FINE).astype(jnp.int32)


def level_of(code):
    return jnp.exp2(code.astype(jnp.float32) * (1.0 / FINE))


def code_into(out_ref, first, block, words, sums):
    lane = lax.broadcasted_iota(jnp.int32, (out_ref.shape[0], block), 1)
    codes = out_ref[:, words * block :]
    values = []
    for member, mine in enumerate(sums):
        code = level_code(jnp.max(jnp.abs(mine), axis=1, keepdims=True))
        codes = jnp.where(lane == first + member, code, codes)
        scaled = jnp.round(mine * (TOP / level_of(code)))
        values.append(jnp.clip(scaled, -TOP, TOP).astype(jnp.int32))
    out_ref[:, words * block :] = codes
    for pair in range(len(sums) // 2):
        word = (values[2 * pair + 1] << 16) | (values[2 * pair] & 0xFFFF)
        at = pl.multiple_of((first // 2 + pair) * block, block)
        out_ref[:, pl.ds(at, block)] = word


def products_kernel(plan, group, slots, block, words, index_ref, *refs):
    parts = len(plan)
    sources, blocks_ref = refs[: 3 * parts], refs[3 * parts]
    outs, (ext, panels, sems, panel_sems) = refs[3 * parts + 1 : 4 * parts + 1], refs[4 * parts + 1 :]
    rows, pieces = panels.shape[0], panel_sems.shape[0]
    piece = rows // pieces

    def panel_copy(n):
        here = pl.ds(n * piece, piece)
        return pltpu.make_async_copy(blocks_ref.at[here], panels.at[here], panel_sems.at[n])

    copies = fill(sources, plan, ext, sems)
    for n in range(pieces):
        panel_copy(n).start()
    end = ext.shape[1] - block
    ext[:, end:] = jnp.zeros((ext.shape[0], block), ext.dtype)
    for (_, size, coded), out_ref in zip(plan, outs):
        if coded:
            out_ref[:, words * block :] = jnp.zeros((size, block), jnp.int32)
    for copy in copies:
        copy.wait()

    @pl.loop(0, rows // group)
    def _(step):
        for n in range(group // piece):
            panel_copy(step * (group // piece) + n).wait()
        first = step * group
        sums = [
            row_sums(index_ref, first + member, slots, block, ext, panels.at[first + member])
            for member in range(group)
        ]
        at = 0
        for (_, size, coded), out_ref in zip(plan, outs):
            mine = [total[at : at + size] for total in sums]
            if coded:
                code_into(out_ref, first, block, words, mine)
            else:
                for member in range(group):
                    column = pl.multiple_of((first + member) * block, block)
                    out_ref[:, pl.ds(column, block)] = mine[member]
            at += size


def products(index, parts, blocks):
    rows, slots, block, _ = blocks.shape
    reach, width = parts[0][0].shape[1], parts[0][1].shape[1]
    plan = tuple(part[3:] for part in parts)
    states = sum(size for _, size, _ in plan)
    group, words = 8 if rows % 8 == 0 else 2, rows // 2
    sources = [array for part in parts for array in part[:3]]
    anywhere = pl.BlockSpec(memory_space=pl.ANY)
    out_shape = []
    for _, size, coded in plan:
        if coded:
            out_shape.append(jax.ShapeDtypeStruct((size, (words + 1) * block), jnp.int32))
        else:
            out_shape.append(jax.ShapeDtypeStruct((size, width), jnp.float32))
    return pl.pallas_call(
        functools.partial(products_kernel, plan, group, slots, block, words),
        out_shape=out_shape,
        in_specs=[pl.BlockSpec(memory_space=pltpu.SMEM)]
        + [anywhere] * len(sources)
        + [pl.BlockSpec(memory_space=pltpu.HBM)],
        out_specs=[pl.BlockSpec(memory_space=pltpu.VMEM)] * len(plan),
        scratch_shapes=[
            pltpu.VMEM((states, 2 * reach + width + block), parts[0][1].dtype),
            pltpu.VMEM(blocks.shape, blocks.dtype),
            pltpu.SemaphoreType.DMA((len(sources),)),
            pltpu.SemaphoreType.DMA((rows // 2,)),
        ],
        compiler_params=pltpu.CompilerParams(vmem_limit_bytes=VMEM_LIMIT),
        cost_estimate=pl.CostEstimate(flops=1, bytes_accessed=1, transcendentals=0),
        name="products",
    )(index, *sources, pltpu.with_memory_space_constraint(blocks, pltpu.HBM))


def finish_kernel(partials, block, pairs, own_ref, *refs):
    out_ref = refs[-1]
    lane = lax.broadcasted_iota(jnp.int32, (own_ref.shape[0], block), 1)
    levels = [level_of(refs[2 * p + 1][...]) * (1.0 / TOP) for p in range(partials)]
    for pair in range(pairs):
        for half in range(2):
            at = (2 * pair + half) * block
            row = 2 * pair + half
            total = own_ref[:, at : at + block]
            for p in range(partials):
                word = refs[2 * p][:, pair * block : (pair + 1) * block]
                value = (word >> 16) if half else ((word << 16) >> 16)
                level = jnp.max(jnp.where(lane == row, levels[p], 0.0), axis=1, keepdims=True)
                total = total + value.astype(jnp.float32) * level
            out_ref[:, at : at + block] = total.astype(out_ref.dtype)


def finish(own_sums, own_start, coded, coded_start, out, start, size, states, block):
    width = own_sums.shape[1]
    words = width // block // 2
    unit = math.gcd(math.gcd(size, start), math.gcd(start - own_start, start - coded_start))
    own_at, coded_at, out_at = (start - own_start) // unit, (start - coded_start) // unit, start // unit
    in_specs = [pl.BlockSpec((unit, width), lambda i: (own_at + i, 0))]
    operands = [own_sums]
    for array in coded:
        in_specs.append(pl.BlockSpec((unit, words * block), lambda i: (coded_at + i, 0)))
        in_specs.append(pl.BlockSpec((unit, block), lambda i: (coded_at + i, words)))
        operands += [array, array]
    aliases = {}
    if out is not None:
        aliases = {len(operands): 0}
        in_specs.append(pl.BlockSpec(memory_space=pl.ANY))
        operands.append(out)
    return pl.pallas_call(
        functools.partial(finish_kernel, len(coded), block, words),
        out_shape=jax.ShapeDtypeStruct((states, width), jnp.bfloat16),
        grid=(size // unit,),
        in_specs=in_specs,
        out_specs=pl.BlockSpec((unit, width), lambda i: (out_at + i, 0)),
        input_output_aliases=aliases,
        compiler_params=pltpu.CompilerParams(vmem_limit_bytes=VMEM_LIMIT),
        cost_estimate=pl.CostEstimate(
            flops=1, bytes_accessed=1, transcendentals=0
        ),
        name="finish",
    )(*operands)


def starts_of(sizes):
    return [sum(sizes[:i]) for i in range(len(sizes))]


def on_device(vectors, blocks, columns, counts):
    states, width = vectors.shape
    rows, slots, block, _ = blocks.shape
    reach = W * block
    basis_size, state_size = lax.axis_size("basis"), lax.axis_size("state")
    if states % 256 == 0:
        sizes = (5 * states // 16, 3 * states // 8, 5 * states // 16)
        own_sizes = (3 * states // 8, 5 * states // 8)
    else:
        sizes, own_sizes = (states,), (states,)
    starts, own_starts = starts_of(sizes), starts_of(own_sizes)

    slot_index = lax.axis_index("state") * slots + jnp.arange(slots, dtype=jnp.int32)
    relative = columns - (lax.axis_index("basis") * rows - W)
    zeros_at = rows + 2 * W
    index = jnp.where(slot_index[None, :] < counts[:, None], relative, zeros_at).reshape(-1)

    up = [(i, i + 1) for i in range(basis_size - 1)]
    down = [(i + 1, i) for i in range(basis_size - 1)]

    def edges_of(piece, *others):
        edges = (piece[:, width - reach :], piece[:, :reach])
        return lax.optimization_barrier((*edges, *others))[:2] if others else edges

    def halo(edges):
        return lax.ppermute(edges[0], "basis", up), lax.ppermute(edges[1], "basis", down)

    def shifted(piece, shift):
        return lax.ppermute(piece, "state", [(i, (i + shift) % state_size) for i in range(state_size)])

    def own_edges(part, *others):
        return edges_of(vectors[own_starts[part] : own_starts[part] + own_sizes[part]], *others)

    def own_part(part, ends):
        return (ends[0], vectors, ends[1], own_starts[part], own_sizes[part], False)

    def their_part(n):
        return (ends[n][0], theirs[n], ends[n][1], 0, theirs[n].shape[0], True)

    messages = [(shift, c) for shift in range(1, state_size) for c in range(len(sizes))]
    count = len(messages)
    theirs, edges, ends, sent, own_sums, received = [], [], [], [], [], []
    first_edges = own_edges(0)
    first = halo(first_edges)
    for n, (shift, c) in enumerate(messages):
        piece = vectors[starts[c] : starts[c] + sizes[c]]
        if n:
            piece = after(piece, *(first_edges if n == 1 else first))
        theirs.append(shifted(piece, shift))

    def compute(n):
        if n == 0:
            own_sums.extend(products(after(index, *edges[0]), [own_part(0, first)], blocks))
        later = edges[n + 1] if n + 1 < count else ()
        sent.extend(products(after(index, own_sums[0], *later), [their_part(n)], blocks))

    for n in range(count):
        edges.append(edges_of(theirs[n]))
        ends.append(halo(edges[n]))
        if n:
            compute(n - 1)
    if len(own_sizes) > 1:
        last = halo(own_edges(1, *edges[-1], *sent[-1:]))
    compute(count - 1)
    coded = [[] for _ in sizes]
    for n, (shift, c) in enumerate(messages):
        message = after(sent[n], received[n - 1]) if n else sent[n]
        received.append(shifted(message, -shift))
        coded[c].append(received[n])
    if len(own_sizes) > 1:
        own_sums += products(index, [own_part(1, last)], blocks)

    out = None
    for part, own_size in enumerate(own_sizes):
        for c, size in enumerate(sizes):
            at = max(own_starts[part], starts[c])
            end = min(own_starts[part] + own_size, starts[c] + size)
            if at < end:
                out = finish(
                    own_sums[part], own_starts[part], coded[c], starts[c], out, at, end - at, states, block
                )
    return out


def solution(mesh):
    in_specs = (
        P("state", "basis"),
        P("basis", "state", None, None),
        P("basis", "state"),
        P("basis"),
    )
    out_specs = P("state", "basis")
    return jax.shard_map(
        on_device, mesh=mesh, in_specs=in_specs, out_specs=out_specs, check_vma=False
    )
```

```python
import functools
import math

import jax
import jax.numpy as jnp
from jax import lax
from jax.experimental import pallas as pl
from jax.experimental.pallas import tpu as pltpu
from jax.sharding import PartitionSpec as P

W = 36
VMEM_LIMIT = 32 * 1024 * 1024
TOP = 32767.0
FINE = 65536.0
SMALLEST = 2.0**-100


def after(array, *others):
    return lax.optimization_barrier((array, *others))[0]


def fill(sources, plan, ext, sems):
    copies, at = [], 0
    for part, (start, size, _) in enumerate(plan):
        left, own, right = sources[3 * part : 3 * part + 3]
        reach, width = left.shape[1], own.shape[1]
        rows = pl.ds(at, size)
        copies += [
            pltpu.make_async_copy(left, ext.at[rows, pl.ds(0, reach)], sems.at[3 * part]),
            pltpu.make_async_copy(
                own.at[pl.ds(start, size)], ext.at[rows, pl.ds(reach, width)], sems.at[3 * part + 1]
            ),
            pltpu.make_async_copy(right, ext.at[rows, pl.ds(reach + width, reach)], sems.at[3 * part + 2]),
        ]
        at += size
    for copy in copies:
        copy.start()
    return copies


def row_sums(index_ref, row, slots, block, ext, panel_ref):
    picked = jnp.concatenate(
        [
            ext[:, pl.ds(pl.multiple_of(index_ref[row * slots + slot] * block, block), block)]
            for slot in range(slots)
        ],
        axis=1,
    )
    panel = jnp.concatenate([panel_ref[slot] for slot in range(slots)], axis=1)
    return lax.dot_general(
        picked, panel, (((1,), (1,)), ((), ())), preferred_element_type=jnp.float32
    )


def level_code(top):
    return jnp.ceil(jnp.log2(jnp.maximum(top, SMALLEST)) * FINE).astype(jnp.int32)


def level_of(code):
    return jnp.exp2(code.astype(jnp.float32) * (1.0 / FINE))


def code_into(out_ref, first, block, words, sums):
    lane = lax.broadcasted_iota(jnp.int32, (out_ref.shape[0], block), 1)
    codes = out_ref[:, words * block :]
    values = []
    for member, mine in enumerate(sums):
        code = level_code(jnp.max(jnp.abs(mine), axis=1, keepdims=True))
        codes = jnp.where(lane == first + member, code, codes)
        scaled = jnp.round(mine * (TOP / level_of(code)))
        values.append(jnp.clip(scaled, -TOP, TOP).astype(jnp.int32))
    out_ref[:, words * block :] = codes
    for pair in range(len(sums) // 2):
        word = (values[2 * pair + 1] << 16) | (values[2 * pair] & 0xFFFF)
        at = pl.multiple_of((first // 2 + pair) * block, block)
        out_ref[:, pl.ds(at, block)] = word


def products_kernel(plan, group, slots, block, words, index_ref, *refs):
    parts = len(plan)
    sources, blocks_ref = refs[: 3 * parts], refs[3 * parts]
    outs, (ext, panels, sems, panel_sems) = refs[3 * parts + 1 : 4 * parts + 1], refs[4 * parts + 1 :]
    rows, pieces = panels.shape[0], panel_sems.shape[0]
    piece = rows // pieces

    def panel_copy(n):
        here = pl.ds(n * piece, piece)
        return pltpu.make_async_copy(blocks_ref.at[here], panels.at[here], panel_sems.at[n])

    copies = fill(sources, plan, ext, sems)
    for n in range(pieces):
        panel_copy(n).start()
    end = ext.shape[1] - block
    ext[:, end:] = jnp.zeros((ext.shape[0], block), ext.dtype)
    for (_, size, coded), out_ref in zip(plan, outs):
        if coded:
            out_ref[:, words * block :] = jnp.zeros((size, block), jnp.int32)
    for copy in copies:
        copy.wait()

    @pl.loop(0, rows // group)
    def _(step):
        for n in range(group // piece):
            panel_copy(step * (group // piece) + n).wait()
        first = step * group
        sums = [
            row_sums(index_ref, first + member, slots, block, ext, panels.at[first + member])
            for member in range(group)
        ]
        at = 0
        for (_, size, coded), out_ref in zip(plan, outs):
            mine = [total[at : at + size] for total in sums]
            if coded:
                code_into(out_ref, first, block, words, mine)
            else:
                for member in range(group):
                    column = pl.multiple_of((first + member) * block, block)
                    out_ref[:, pl.ds(column, block)] = mine[member]
            at += size


def products(index, parts, blocks):
    rows, slots, block, _ = blocks.shape
    reach, width = parts[0][0].shape[1], parts[0][1].shape[1]
    plan = tuple(part[3:] for part in parts)
    states = sum(size for _, size, _ in plan)
    group, words = 8 if rows % 8 == 0 else 2, rows // 2
    sources = [array for part in parts for array in part[:3]]
    anywhere = pl.BlockSpec(memory_space=pl.ANY)
    out_shape = []
    for _, size, coded in plan:
        if coded:
            out_shape.append(jax.ShapeDtypeStruct((size, (words + 1) * block), jnp.int32))
        else:
            out_shape.append(jax.ShapeDtypeStruct((size, width), jnp.float32))
    return pl.pallas_call(
        functools.partial(products_kernel, plan, group, slots, block, words),
        out_shape=out_shape,
        in_specs=[pl.BlockSpec(memory_space=pltpu.SMEM)]
        + [anywhere] * len(sources)
        + [pl.BlockSpec(memory_space=pltpu.HBM)],
        out_specs=[pl.BlockSpec(memory_space=pltpu.VMEM)] * len(plan),
        scratch_shapes=[
            pltpu.VMEM((states, 2 * reach + width + block), parts[0][1].dtype),
            pltpu.VMEM(blocks.shape, blocks.dtype),
            pltpu.SemaphoreType.DMA((len(sources),)),
            pltpu.SemaphoreType.DMA((rows // 2,)),
        ],
        compiler_params=pltpu.CompilerParams(vmem_limit_bytes=VMEM_LIMIT),
        cost_estimate=pl.CostEstimate(flops=1, bytes_accessed=1, transcendentals=0),
        name="products",
    )(index, *sources, pltpu.with_memory_space_constraint(blocks, pltpu.HBM))


def finish_kernel(partials, block, pairs, own_ref, *refs):
    out_ref = refs[-1]
    step = pl.program_id(0)
    lane = lax.broadcasted_iota(jnp.int32, (own_ref.shape[0], block), 1)
    levels = [level_of(refs[2 * p + 1][...]) * (1.0 / TOP) for p in range(partials)]
    for pair in range(pairs):
        for half in range(2):
            at = (2 * pair + half) * block
            row = (step * pairs + pair) * 2 + half
            total = own_ref[:, at : at + block]
            for p in range(partials):
                word = refs[2 * p][:, pair * block : (pair + 1) * block]
                value = (word >> 16) if half else ((word << 16) >> 16)
                level = jnp.max(jnp.where(lane == row, levels[p], 0.0), axis=1, keepdims=True)
                total = total + value.astype(jnp.float32) * level
            out_ref[:, at : at + block] = total.astype(out_ref.dtype)


def finish(own_sums, own_start, coded, coded_start, out, start, size, states, block):
    width = own_sums.shape[1]
    words = width // block // 2
    pairs = 4 if words % 4 == 0 else 1
    rows, wide, narrow = pl.Element(size), pl.Element(2 * pairs * block), pl.Element(pairs * block)
    own_at, coded_at = start - own_start, start - coded_start
    in_specs = [pl.BlockSpec((rows, wide), lambda i: (own_at, i * 2 * pairs * block))]
    operands = [own_sums]
    for array in coded:
        in_specs.append(pl.BlockSpec((rows, narrow), lambda i: (coded_at, i * pairs * block)))
        in_specs.append(pl.BlockSpec((rows, pl.Element(block)), lambda i: (coded_at, words * block)))
        operands += [array, array]
    aliases = {}
    if out is not None:
        aliases = {len(operands): 0}
        in_specs.append(pl.BlockSpec(memory_space=pl.ANY))
        operands.append(out)
    return pl.pallas_call(
        functools.partial(finish_kernel, len(coded), block, pairs),
        out_shape=jax.ShapeDtypeStruct((states, width), jnp.bfloat16),
        grid=(words // pairs,),
        in_specs=in_specs,
        out_specs=pl.BlockSpec((rows, wide), lambda i: (start, i * 2 * pairs * block)),
        input_output_aliases=aliases,
        compiler_params=pltpu.CompilerParams(vmem_limit_bytes=VMEM_LIMIT),
        cost_estimate=pl.CostEstimate(flops=1, bytes_accessed=1, transcendentals=0),
        name="finish",
    )(*operands)


def starts_of(sizes):
    return [sum(sizes[:i]) for i in range(len(sizes))]


def on_device(vectors, blocks, columns, counts):
    states, width = vectors.shape
    rows, slots, block, _ = blocks.shape
    reach = W * block
    basis_size, state_size = lax.axis_size("basis"), lax.axis_size("state")
    if states % 256 == 0:
        sizes = (5 * states // 16, 3 * states // 8, 5 * states // 16)
        own_sizes = (7 * states // 16, 9 * states // 16)
    else:
        sizes, own_sizes = (states,), (states,)
    starts, own_starts = starts_of(sizes), starts_of(own_sizes)

    slot_index = lax.axis_index("state") * slots + jnp.arange(slots, dtype=jnp.int32)
    relative = columns - (lax.axis_index("basis") * rows - W)
    zeros_at = rows + 2 * W
    index = jnp.where(slot_index[None, :] < counts[:, None], relative, zeros_at).reshape(-1)

    up = [(i, i + 1) for i in range(basis_size - 1)]
    down = [(i + 1, i) for i in range(basis_size - 1)]

    def edges_of(piece, *others):
        edges = (piece[:, width - reach :], piece[:, :reach])
        return lax.optimization_barrier((*edges, *others))[:2] if others else edges

    def halo(edges):
        return lax.ppermute(edges[0], "basis", up), lax.ppermute(edges[1], "basis", down)

    def shifted(piece, shift):
        return lax.ppermute(piece, "state", [(i, (i + shift) % state_size) for i in range(state_size)])

    def own_edges(part, *others):
        return edges_of(vectors[own_starts[part] : own_starts[part] + own_sizes[part]], *others)

    def own_part(part, ends):
        return (ends[0], vectors, ends[1], own_starts[part], own_sizes[part], False)

    def their_part(n):
        return (ends[n][0], theirs[n], ends[n][1], 0, theirs[n].shape[0], True)

    messages = [(shift, c) for shift in range(1, state_size) for c in range(len(sizes))]
    count = len(messages)
    theirs, edges, ends, sent, own_sums, received = [], [], [], [], [], []
    first_edges = own_edges(0)
    first = halo(first_edges)
    for n, (shift, c) in enumerate(messages):
        source = after(vectors, *(first_edges if n == 1 else first)) if n else vectors
        theirs.append(shifted(source[starts[c] : starts[c] + sizes[c]], shift))

    def compute(n):
        later = edges[n + 1] if n + 1 < count else ()
        if n == min(1, count - 1):
            own_sums.extend(products(after(index, *later) if later else index, [own_part(0, first)], blocks))
            later = (*later, own_sums[0])
        sent.extend(products(after(index, *later) if later else index, [their_part(n)], blocks))

    for n in range(count):
        edges.append(edges_of(theirs[n]))
        ends.append(halo(edges[n]))
        if n:
            compute(n - 1)
    if len(own_sizes) > 1:
        last = halo(own_edges(1, *edges[-1], *sent[-1:]))
    compute(count - 1)
    coded = [[] for _ in sizes]
    for n, (shift, c) in enumerate(messages):
        message = after(sent[n], received[n - 1]) if n else sent[n]
        received.append(shifted(message, -shift))
        coded[c].append(received[n])
    out = None
    for part, own_size in enumerate(own_sizes):
        if part:
            own_sums += products(after(index, out), [own_part(part, last)], blocks)
        for c, size in enumerate(sizes):
            at = max(own_starts[part], starts[c])
            end = min(own_starts[part] + own_size, starts[c] + size)
            if at < end:
                out = finish(
                    own_sums[part], own_starts[part], coded[c], starts[c], out, at, end - at, states, block
                )
    return out


def solution(mesh):
    in_specs = (
        P("state", "basis"),
        P("basis", "state", None, None),
        P("basis", "state"),
        P("basis"),
    )
    out_specs = P("state", "basis")
    return jax.shard_map(
        on_device, mesh=mesh, in_specs=in_specs, out_specs=out_specs, check_vma=False
    )
```

```python
import functools
import math

import jax
import jax.numpy as jnp
from jax import lax
from jax.experimental import pallas as pl
from jax.experimental.pallas import tpu as pltpu
from jax.sharding import PartitionSpec as P

W = 36
VMEM_LIMIT = 32 * 1024 * 1024
TOP = 32767.0
FINE = 65536.0
SMALLEST = 2.0**-100


def after(array, *others):
    return lax.optimization_barrier((array, *others))[0]


def fill(sources, plan, ext, sems):
    copies, at = [], 0
    for part, (start, size, _) in enumerate(plan):
        left, own, right = sources[3 * part : 3 * part + 3]
        reach, width = left.shape[1], own.shape[1]
        rows = pl.ds(at, size)
        copies += [
            pltpu.make_async_copy(left, ext.at[rows, pl.ds(0, reach)], sems.at[3 * part]),
            pltpu.make_async_copy(
                own.at[pl.ds(start, size)], ext.at[rows, pl.ds(reach, width)], sems.at[3 * part + 1]
            ),
            pltpu.make_async_copy(right, ext.at[rows, pl.ds(reach + width, reach)], sems.at[3 * part + 2]),
        ]
        at += size
    for copy in copies:
        copy.start()
    return copies


def row_sums(index_ref, row, slots, block, ext, panel_ref):
    picked = jnp.concatenate(
        [
            ext[:, pl.ds(pl.multiple_of(index_ref[row * slots + slot] * block, block), block)]
            for slot in range(slots)
        ],
        axis=1,
    )
    panel = jnp.concatenate([panel_ref[slot] for slot in range(slots)], axis=1)
    return lax.dot_general(
        picked, panel, (((1,), (1,)), ((), ())), preferred_element_type=jnp.float32
    )


def level_code(top):
    return jnp.ceil(jnp.log2(jnp.maximum(top, SMALLEST)) * FINE).astype(jnp.int32)


def level_of(code):
    return jnp.exp2(code.astype(jnp.float32) * (1.0 / FINE))


def code_into(out_ref, first, block, words, sums):
    lane = lax.broadcasted_iota(jnp.int32, (out_ref.shape[0], block), 1)
    codes = out_ref[:, words * block :]
    values = []
    for member, mine in enumerate(sums):
        code = level_code(jnp.max(jnp.abs(mine), axis=1, keepdims=True))
        codes = jnp.where(lane == first + member, code, codes)
        scaled = jnp.round(mine * (TOP / level_of(code)))
        values.append(jnp.clip(scaled, -TOP, TOP).astype(jnp.int32))
    out_ref[:, words * block :] = codes
    for pair in range(len(sums) // 2):
        word = (values[2 * pair + 1] << 16) | (values[2 * pair] & 0xFFFF)
        at = pl.multiple_of((first // 2 + pair) * block, block)
        out_ref[:, pl.ds(at, block)] = word


def products_kernel(plan, group, slots, block, words, index_ref, *refs):
    parts = len(plan)
    sources, blocks_ref = refs[: 3 * parts], refs[3 * parts]
    outs, (ext, panels, sems, panel_sems) = refs[3 * parts + 1 : 4 * parts + 1], refs[4 * parts + 1 :]
    rows, pieces = panels.shape[0], panel_sems.shape[0]
    piece = rows // pieces

    def panel_copy(n):
        here = pl.ds(n * piece, piece)
        return pltpu.make_async_copy(blocks_ref.at[here], panels.at[here], panel_sems.at[n])

    copies = fill(sources, plan, ext, sems)
    for n in range(pieces):
        panel_copy(n).start()
    end = ext.shape[1] - block
    ext[:, end:] = jnp.zeros((ext.shape[0], block), ext.dtype)
    for (_, size, coded), out_ref in zip(plan, outs):
        if coded:
            out_ref[:, words * block :] = jnp.zeros((size, block), jnp.int32)
    for copy in copies:
        copy.wait()

    @pl.loop(0, rows // group)
    def _(step):
        for n in range(group // piece):
            panel_copy(step * (group // piece) + n).wait()
        first = step * group
        sums = [
            row_sums(index_ref, first + member, slots, block, ext, panels.at[first + member])
            for member in range(group)
        ]
        at = 0
        for (_, size, coded), out_ref in zip(plan, outs):
            mine = [total[at : at + size] for total in sums]
            if coded:
                code_into(out_ref, first, block, words, mine)
            else:
                for member in range(group):
                    column = pl.multiple_of((first + member) * block, block)
                    out_ref[:, pl.ds(column, block)] = mine[member]
            at += size


def products(index, parts, blocks):
    rows, slots, block, _ = blocks.shape
    reach, width = parts[0][0].shape[1], parts[0][1].shape[1]
    plan = tuple(part[3:] for part in parts)
    states = sum(size for _, size, _ in plan)
    group, words = 8 if rows % 8 == 0 else 2, rows // 2
    sources = [array for part in parts for array in part[:3]]
    anywhere = pl.BlockSpec(memory_space=pl.ANY)
    out_shape = []
    for _, size, coded in plan:
        if coded:
            out_shape.append(jax.ShapeDtypeStruct((size, (words + 1) * block), jnp.int32))
        else:
            out_shape.append(jax.ShapeDtypeStruct((size, width), jnp.float32))
    return pl.pallas_call(
        functools.partial(products_kernel, plan, group, slots, block, words),
        out_shape=out_shape,
        in_specs=[pl.BlockSpec(memory_space=pltpu.SMEM)]
        + [anywhere] * len(sources)
        + [pl.BlockSpec(memory_space=pltpu.HBM)],
        out_specs=[pl.BlockSpec(memory_space=pltpu.VMEM)] * len(plan),
        scratch_shapes=[
            pltpu.VMEM((states, 2 * reach + width + block), parts[0][1].dtype),
            pltpu.VMEM(blocks.shape, blocks.dtype),
            pltpu.SemaphoreType.DMA((len(sources),)),
            pltpu.SemaphoreType.DMA((rows // 2,)),
        ],
        compiler_params=pltpu.CompilerParams(vmem_limit_bytes=VMEM_LIMIT),
        cost_estimate=pl.CostEstimate(flops=1, bytes_accessed=1, transcendentals=0),
        name="products",
    )(index, *sources, pltpu.with_memory_space_constraint(blocks, pltpu.HBM))


def finish_kernel(partials, block, pairs, own_ref, *refs):
    out_ref = refs[-1]
    step = pl.program_id(0)
    lane = lax.broadcasted_iota(jnp.int32, (own_ref.shape[0], block), 1)
    levels = [level_of(refs[2 * p + 1][...]) * (1.0 / TOP) for p in range(partials)]
    for pair in range(pairs):
        for half in range(2):
            at = (2 * pair + half) * block
            row = (step * pairs + pair) * 2 + half
            total = own_ref[:, at : at + block]
            for p in range(partials):
                word = refs[2 * p][:, pair * block : (pair + 1) * block]
                value = (word >> 16) if half else ((word << 16) >> 16)
                level = jnp.max(jnp.where(lane == row, levels[p], 0.0), axis=1, keepdims=True)
                total = total + value.astype(jnp.float32) * level
            out_ref[:, at : at + block] = total.astype(out_ref.dtype)


def finish(own_sums, own_start, coded, coded_start, out, start, size, states, block):
    width = own_sums.shape[1]
    words = width // block // 2
    pairs = words // 2 if words % 2 == 0 else 1
    rows, wide, narrow = pl.Element(size), pl.Element(2 * pairs * block), pl.Element(pairs * block)
    own_at, coded_at = start - own_start, start - coded_start
    in_specs = [pl.BlockSpec((rows, wide), lambda i: (own_at, i * 2 * pairs * block))]
    operands = [own_sums]
    for array in coded:
        in_specs.append(pl.BlockSpec((rows, narrow), lambda i: (coded_at, i * pairs * block)))
        in_specs.append(pl.BlockSpec((rows, pl.Element(block)), lambda i: (coded_at, words * block)))
        operands += [array, array]
    aliases = {}
    if out is not None:
        aliases = {len(operands): 0}
        in_specs.append(pl.BlockSpec(memory_space=pl.ANY))
        operands.append(out)
    return pl.pallas_call(
        functools.partial(finish_kernel, len(coded), block, pairs),
        out_shape=jax.ShapeDtypeStruct((states, width), jnp.bfloat16),
        grid=(words // pairs,),
        in_specs=in_specs,
        out_specs=pl.BlockSpec((rows, wide), lambda i: (start, i * 2 * pairs * block)),
        input_output_aliases=aliases,
        compiler_params=pltpu.CompilerParams(vmem_limit_bytes=VMEM_LIMIT),
        cost_estimate=pl.CostEstimate(flops=1, bytes_accessed=1, transcendentals=0),
        name="finish",
    )(*operands)


def starts_of(sizes):
    return [sum(sizes[:i]) for i in range(len(sizes))]


def on_device(vectors, blocks, columns, counts):
    states, width = vectors.shape
    rows, slots, block, _ = blocks.shape
    reach = W * block
    basis_size, state_size = lax.axis_size("basis"), lax.axis_size("state")
    if states % 256 == 0:
        sizes = (5 * states // 16, 3 * states // 8, 5 * states // 16)
        own_sizes = (7 * states // 16, 9 * states // 16)
    else:
        sizes, own_sizes = (states,), (states,)
    starts, own_starts = starts_of(sizes), starts_of(own_sizes)

    slot_index = lax.axis_index("state") * slots + jnp.arange(slots, dtype=jnp.int32)
    relative = columns - (lax.axis_index("basis") * rows - W)
    zeros_at = rows + 2 * W
    index = jnp.where(slot_index[None, :] < counts[:, None], relative, zeros_at).reshape(-1)

    up = [(i, i + 1) for i in range(basis_size - 1)]
    down = [(i + 1, i) for i in range(basis_size - 1)]

    def edges_of(piece, *others):
        edges = (piece[:, width - reach :], piece[:, :reach])
        return lax.optimization_barrier((*edges, *others))[:2] if others else edges

    def halo(edges):
        return lax.ppermute(edges[0], "basis", up), lax.ppermute(edges[1], "basis", down)

    def shifted(piece, shift):
        return lax.ppermute(piece, "state", [(i, (i + shift) % state_size) for i in range(state_size)])

    def own_edges(part, *others):
        return edges_of(vectors[own_starts[part] : own_starts[part] + own_sizes[part]], *others)

    def own_part(part, ends):
        return (ends[0], vectors, ends[1], own_starts[part], own_sizes[part], False)

    def their_part(n):
        return (ends[n][0], theirs[n], ends[n][1], 0, theirs[n].shape[0], True)

    messages = [(shift, c) for shift in range(1, state_size) for c in range(len(sizes))]
    count = len(messages)
    theirs, edges, ends, sent, own_sums, received = [], [], [], [], [], []
    first_edges = own_edges(0)
    first = halo(first_edges)
    for n, (shift, c) in enumerate(messages):
        source = after(vectors, *(first_edges if n == 1 else first)) if n else vectors
        theirs.append(shifted(source[starts[c] : starts[c] + sizes[c]], shift))

    def compute(n):
        later = edges[n + 1] if n + 1 < count else ()
        parts = [their_part(n)]
        if n == count - 1:
            parts.append(own_part(0, first))
        result = products(after(index, *later) if later else index, parts, blocks)
        sent.append(result[0])
        own_sums.extend(result[1:])

    for n in range(count):
        edges.append(edges_of(theirs[n], *(ends[n - 1] if n > 1 else ())))
        ends.append(halo(edges[n]))
        if n:
            compute(n - 1)
    if len(own_sizes) > 1:
        last = halo(own_edges(1, *edges[-1], *sent[-1:]))
    compute(count - 1)
    coded = [[] for _ in sizes]
    for n, (shift, c) in enumerate(messages):
        message = after(sent[n], received[n - 1]) if n else sent[n]
        received.append(shifted(message, -shift))
        coded[c].append(received[n])
    out = None
    for part, own_size in enumerate(own_sizes):
        if part:
            own_sums += products(after(index, out), [own_part(part, last)], blocks)
        for c, size in enumerate(sizes):
            at = max(own_starts[part], starts[c])
            end = min(own_starts[part] + own_size, starts[c] + size)
            if at < end:
                out = finish(
                    own_sums[part], own_starts[part], coded[c], starts[c], out, at, end - at, states, block
                )
    return out


def solution(mesh):
    in_specs = (
        P("state", "basis"),
        P("basis", "state", None, None),
        P("basis", "state"),
        P("basis"),
    )
    out_specs = P("state", "basis")
    return jax.shard_map(
        on_device, mesh=mesh, in_specs=in_specs, out_specs=out_specs, check_vma=False
    )
```

```python
import functools
import math

import jax
import jax.numpy as jnp
from jax import lax
from jax.experimental import pallas as pl
from jax.experimental.pallas import tpu as pltpu
from jax.sharding import PartitionSpec as P

W = 36
VMEM_LIMIT = 32 * 1024 * 1024
TOP = 32767.0
FINE = 65536.0
SMALLEST = 2.0**-100


def after(array, *others):
    return lax.optimization_barrier((array, *others))[0]


def fill(sources, plan, ext, sems):
    copies, at = [], 0
    for part, (start, size, _) in enumerate(plan):
        left, own, right = sources[3 * part : 3 * part + 3]
        reach, width = left.shape[1], own.shape[1]
        rows = pl.ds(at, size)
        copies += [
            pltpu.make_async_copy(left, ext.at[rows, pl.ds(0, reach)], sems.at[3 * part]),
            pltpu.make_async_copy(
                own.at[pl.ds(start, size)], ext.at[rows, pl.ds(reach, width)], sems.at[3 * part + 1]
            ),
            pltpu.make_async_copy(right, ext.at[rows, pl.ds(reach + width, reach)], sems.at[3 * part + 2]),
        ]
        at += size
    for copy in copies:
        copy.start()
    return copies


def row_sums(index_ref, row, slots, block, ext, panel_ref):
    picked = jnp.concatenate(
        [
            ext[:, pl.ds(pl.multiple_of(index_ref[row * slots + slot] * block, block), block)]
            for slot in range(slots)
        ],
        axis=1,
    )
    panel = jnp.concatenate([panel_ref[slot] for slot in range(slots)], axis=1)
    return lax.dot_general(
        picked, panel, (((1,), (1,)), ((), ())), preferred_element_type=jnp.float32
    )


def level_code(top):
    return jnp.ceil(jnp.log2(jnp.maximum(top, SMALLEST)) * FINE).astype(jnp.int32)


def level_of(code):
    return jnp.exp2(code.astype(jnp.float32) * (1.0 / FINE))


def code_into(out_ref, first, block, words, sums):
    lane = lax.broadcasted_iota(jnp.int32, (out_ref.shape[0], block), 1)
    codes = out_ref[:, words * block :]
    values = []
    for member, mine in enumerate(sums):
        code = level_code(jnp.max(jnp.abs(mine), axis=1, keepdims=True))
        codes = jnp.where(lane == first + member, code, codes)
        scaled = jnp.round(mine * (TOP / level_of(code)))
        values.append(jnp.clip(scaled, -TOP, TOP).astype(jnp.int32))
    out_ref[:, words * block :] = codes
    for pair in range(len(sums) // 2):
        word = (values[2 * pair + 1] << 16) | (values[2 * pair] & 0xFFFF)
        at = pl.multiple_of((first // 2 + pair) * block, block)
        out_ref[:, pl.ds(at, block)] = word


def products_kernel(plan, group, slots, block, words, index_ref, *refs):
    parts = len(plan)
    sources, blocks_ref = refs[: 3 * parts], refs[3 * parts]
    outs, (ext, panels, sems, panel_sems) = refs[3 * parts + 1 : 4 * parts + 1], refs[4 * parts + 1 :]
    rows, pieces = panels.shape[0], panel_sems.shape[0]
    piece = rows // pieces

    def panel_copy(n):
        here = pl.ds(n * piece, piece)
        return pltpu.make_async_copy(blocks_ref.at[here], panels.at[here], panel_sems.at[n])

    copies = fill(sources, plan, ext, sems)
    for n in range(pieces):
        panel_copy(n).start()
    end = ext.shape[1] - block
    ext[:, end:] = jnp.zeros((ext.shape[0], block), ext.dtype)
    for (_, size, coded), out_ref in zip(plan, outs):
        if coded:
            out_ref[:, words * block :] = jnp.zeros((size, block), jnp.int32)
    for copy in copies:
        copy.wait()

    @pl.loop(0, rows // group)
    def _(step):
        for n in range(group // piece):
            panel_copy(step * (group // piece) + n).wait()
        first = step * group
        sums = [
            row_sums(index_ref, first + member, slots, block, ext, panels.at[first + member])
            for member in range(group)
        ]
        at = 0
        for (_, size, coded), out_ref in zip(plan, outs):
            mine = [total[at : at + size] for total in sums]
            if coded:
                code_into(out_ref, first, block, words, mine)
            else:
                for member in range(group):
                    column = pl.multiple_of((first + member) * block, block)
                    out_ref[:, pl.ds(column, block)] = mine[member]
            at += size


def products(index, parts, blocks):
    rows, slots, block, _ = blocks.shape
    reach, width = parts[0][0].shape[1], parts[0][1].shape[1]
    plan = tuple(part[3:] for part in parts)
    states = sum(size for _, size, _ in plan)
    group, words = 8 if rows % 8 == 0 else 2, rows // 2
    sources = [array for part in parts for array in part[:3]]
    anywhere = pl.BlockSpec(memory_space=pl.ANY)
    out_shape = []
    for _, size, coded in plan:
        if coded:
            out_shape.append(jax.ShapeDtypeStruct((size, (words + 1) * block), jnp.int32))
        else:
            out_shape.append(jax.ShapeDtypeStruct((size, width), jnp.float32))
    return pl.pallas_call(
        functools.partial(products_kernel, plan, group, slots, block, words),
        out_shape=out_shape,
        in_specs=[pl.BlockSpec(memory_space=pltpu.SMEM)]
        + [anywhere] * len(sources)
        + [pl.BlockSpec(memory_space=pltpu.HBM)],
        out_specs=[pl.BlockSpec(memory_space=pltpu.VMEM)] * len(plan),
        scratch_shapes=[
            pltpu.VMEM((states, 2 * reach + width + block), parts[0][1].dtype),
            pltpu.VMEM(blocks.shape, blocks.dtype),
            pltpu.SemaphoreType.DMA((len(sources),)),
            pltpu.SemaphoreType.DMA((rows // 2,)),
        ],
        compiler_params=pltpu.CompilerParams(vmem_limit_bytes=VMEM_LIMIT),
        cost_estimate=pl.CostEstimate(flops=1, bytes_accessed=1, transcendentals=0),
        name="products",
    )(index, *sources, pltpu.with_memory_space_constraint(blocks, pltpu.HBM))


def finish_kernel(partials, block, pairs, own_ref, *refs):
    out_ref = refs[-1]
    step = pl.program_id(0)
    lane = lax.broadcasted_iota(jnp.int32, (own_ref.shape[0], block), 1)
    levels = [level_of(refs[2 * p + 1][...]) * (1.0 / TOP) for p in range(partials)]
    for pair in range(pairs):
        for half in range(2):
            at = (2 * pair + half) * block
            row = (step * pairs + pair) * 2 + half
            total = own_ref[:, at : at + block]
            for p in range(partials):
                word = refs[2 * p][:, pair * block : (pair + 1) * block]
                value = (word >> 16) if half else ((word << 16) >> 16)
                level = jnp.max(jnp.where(lane == row, levels[p], 0.0), axis=1, keepdims=True)
                total = total + value.astype(jnp.float32) * level
            out_ref[:, at : at + block] = total.astype(out_ref.dtype)


def finish(own_sums, own_start, coded, coded_start, out, start, size, states, block):
    width = own_sums.shape[1]
    words = width // block // 2
    pairs = words // 2 if words % 2 == 0 else 1
    rows, wide, narrow = pl.Element(size), pl.Element(2 * pairs * block), pl.Element(pairs * block)
    own_at, coded_at = start - own_start, start - coded_start
    in_specs = [pl.BlockSpec((rows, wide), lambda i: (own_at, i * 2 * pairs * block))]
    operands = [own_sums]
    for array in coded:
        in_specs.append(pl.BlockSpec((rows, narrow), lambda i: (coded_at, i * pairs * block)))
        in_specs.append(pl.BlockSpec((rows, pl.Element(block)), lambda i: (coded_at, words * block)))
        operands += [array, array]
    aliases = {}
    if out is not None:
        aliases = {len(operands): 0}
        in_specs.append(pl.BlockSpec(memory_space=pl.ANY))
        operands.append(out)
    return pl.pallas_call(
        functools.partial(finish_kernel, len(coded), block, pairs),
        out_shape=jax.ShapeDtypeStruct((states, width), jnp.bfloat16),
        grid=(words // pairs,),
        in_specs=in_specs,
        out_specs=pl.BlockSpec((rows, wide), lambda i: (start, i * 2 * pairs * block)),
        input_output_aliases=aliases,
        compiler_params=pltpu.CompilerParams(vmem_limit_bytes=VMEM_LIMIT),
        cost_estimate=pl.CostEstimate(flops=1, bytes_accessed=1, transcendentals=0),
        name="finish",
    )(*operands)


def starts_of(sizes):
    return [sum(sizes[:i]) for i in range(len(sizes))]


def on_device(vectors, blocks, columns, counts):
    states, width = vectors.shape
    rows, slots, block, _ = blocks.shape
    reach = W * block
    basis_size, state_size = lax.axis_size("basis"), lax.axis_size("state")
    if states % 256 == 0:
        sizes = (5 * states // 16, 5 * states // 16, 3 * states // 8)
        own_sizes = (3 * states // 8, 5 * states // 8)
    else:
        sizes, own_sizes = (states,), (states,)
    starts, own_starts = starts_of(sizes), starts_of(own_sizes)

    slot_index = lax.axis_index("state") * slots + jnp.arange(slots, dtype=jnp.int32)
    relative = columns - (lax.axis_index("basis") * rows - W)
    zeros_at = rows + 2 * W
    index = jnp.where(slot_index[None, :] < counts[:, None], relative, zeros_at).reshape(-1)

    up = [(i, i + 1) for i in range(basis_size - 1)]
    down = [(i + 1, i) for i in range(basis_size - 1)]

    def edges_of(piece, *others):
        edges = (piece[:, width - reach :], piece[:, :reach])
        return lax.optimization_barrier((*edges, *others))[:2] if others else edges

    def halo(edges):
        return lax.ppermute(edges[0], "basis", up), lax.ppermute(edges[1], "basis", down)

    def shifted(piece, shift):
        return lax.ppermute(piece, "state", [(i, (i + shift) % state_size) for i in range(state_size)])

    def own_edges(part, *others):
        return edges_of(vectors[own_starts[part] : own_starts[part] + own_sizes[part]], *others)

    def own_part(part, ends):
        return (ends[0], vectors, ends[1], own_starts[part], own_sizes[part], False)

    def their_part(n):
        return (ends[n][0], theirs[n], ends[n][1], 0, theirs[n].shape[0], True)

    messages = [(shift, c) for shift in range(1, state_size) for c in range(len(sizes))]
    count = len(messages)
    theirs, edges, ends, sent, own_sums, received = [], [], [], [], [], []
    first_edges = own_edges(0)
    first = halo(first_edges)
    for n, (shift, c) in enumerate(messages):
        source = after(vectors, *(first_edges if n == 1 else first)) if n else vectors
        theirs.append(shifted(source[starts[c] : starts[c] + sizes[c]], shift))

    def compute(n):
        later = edges[n + 1] if n + 1 < len(edges) else ()
        sent.extend(products(after(index, *later) if later else index, [their_part(n)], blocks))
        message = after(sent[n], received[n - 1]) if n else sent[n]
        received.append(shifted(message, -messages[n][0]))

    for n in range(count):
        edges.append(edges_of(theirs[n]))
        ends.append(halo(edges[n]))
        if n:
            compute(n - 1)
    if len(own_sizes) > 1:
        edges.append(own_edges(1, *edges[-1], *sent[-1:], *received[:1]))
        last = halo(edges[-1])
    compute(count - 1)
    coded = [[received[n] for n in range(count) if messages[n][1] == c] for c in range(len(sizes))]
    own_sums += products(after(index, sent[-1]), [own_part(0, first)], blocks)
    out = None
    for part, own_size in enumerate(own_sizes):
        if part:
            own_sums += products(after(index, out), [own_part(part, last)], blocks)
        for c, size in enumerate(sizes):
            at = max(own_starts[part], starts[c])
            end = min(own_starts[part] + own_size, starts[c] + size)
            if at < end:
                out = finish(
                    own_sums[part], own_starts[part], coded[c], starts[c], out, at, end - at, states, block
                )
    return out


def solution(mesh):
    in_specs = (
        P("state", "basis"),
        P("basis", "state", None, None),
        P("basis", "state"),
        P("basis"),
    )
    out_specs = P("state", "basis")
    return jax.shard_map(
        on_device, mesh=mesh, in_specs=in_specs, out_specs=out_specs, check_vma=False
    )
```

```python
import functools
import math

import jax
import jax.numpy as jnp
from jax import lax
from jax.experimental import pallas as pl
from jax.experimental.pallas import tpu as pltpu
from jax.sharding import PartitionSpec as P

W = 36
VMEM_LIMIT = 32 * 1024 * 1024
TOP = 32767.0
FINE = 65536.0
SMALLEST = 2.0**-100


def after(array, *others):
    return lax.optimization_barrier((array, *others))[0]


def fill(sources, starts, ext, sems):
    copies, column = [], 0
    for n, (source, start) in enumerate(zip(sources, starts)):
        width = source.shape[1]
        target = ext.at[:, pl.ds(column, width)]
        copies.append(pltpu.make_async_copy(source.at[pl.ds(start, ext.shape[0])], target, sems.at[n]))
        copies[-1].start()
        column += width
    return copies


def row_sums(index_ref, row, slots, block, ext, panel_ref):
    picked = jnp.concatenate(
        [
            ext[:, pl.ds(pl.multiple_of(index_ref[row * slots + slot] * block, block), block)]
            for slot in range(slots)
        ],
        axis=1,
    )
    panel = jnp.concatenate([panel_ref[slot] for slot in range(slots)], axis=1)
    return lax.dot_general(
        picked, panel, (((1,), (1,)), ((), ())), preferred_element_type=jnp.float32
    )


def level_code(top):
    return jnp.ceil(jnp.log2(jnp.maximum(top, SMALLEST)) * FINE).astype(jnp.int32)


def level_of(code):
    return jnp.exp2(code.astype(jnp.float32) * (1.0 / FINE))


def code_into(out_ref, first, block, words, sums):
    lane = lax.broadcasted_iota(jnp.int32, (out_ref.shape[0], block), 1)
    codes = out_ref[:, words * block :]
    values = []
    for member, mine in enumerate(sums):
        code = level_code(jnp.max(jnp.abs(mine), axis=1, keepdims=True))
        codes = jnp.where(lane == first + member, code, codes)
        scaled = jnp.round(mine * (TOP / level_of(code)))
        values.append(jnp.clip(scaled, -TOP, TOP).astype(jnp.int32))
    out_ref[:, words * block :] = codes
    for pair in range(len(sums) // 2):
        word = (values[2 * pair + 1] << 16) | (values[2 * pair] & 0xFFFF)
        at = pl.multiple_of((first // 2 + pair) * block, block)
        out_ref[:, pl.ds(at, block)] = word


def start_panels(blocks_ref, panels, sems):
    piece = panels.shape[0] // sems.shape[0]

    def copy(n):
        here = pl.ds(n * piece, piece)
        return pltpu.make_async_copy(blocks_ref.at[here], panels.at[here], sems.at[n])

    def wait(step, group):
        for n in range(group // piece):
            copy(step * (group // piece) + n).wait()

    for n in range(sems.shape[0]):
        copy(n).start()
    return wait


def coded_kernel(group, slots, block, words, index_ref, *refs):
    sources, (blocks_ref, out_ref, ext, panels, sems, panel_sems) = refs[:3], refs[3:]
    size = ext.shape[0]
    copies = fill(sources, (0, 0, 0), ext, sems)
    wait = start_panels(blocks_ref, panels, panel_sems)
    ext[:, ext.shape[1] - block :] = jnp.zeros((size, block), ext.dtype)
    out_ref[:, words * block :] = jnp.zeros((size, block), jnp.int32)
    for copy in copies:
        copy.wait()

    @pl.loop(0, panels.shape[0] // group)
    def _(step):
        wait(step, group)
        first = step * group
        sums = [
            row_sums(index_ref, first + member, slots, block, ext, panels.at[first + member])
            for member in range(group)
        ]
        code_into(out_ref, first, block, words, sums)


def group_of(rows):
    return 8 if rows % 8 == 0 else 2


def coded_products(index, left, own, right, blocks):
    rows, slots, block, _ = blocks.shape
    size, words, group = own.shape[0], rows // 2, group_of(rows)
    width = 2 * left.shape[1] + own.shape[1] + block
    anywhere = pl.BlockSpec(memory_space=pl.ANY)
    return pl.pallas_call(
        functools.partial(coded_kernel, group, slots, block, words),
        out_shape=jax.ShapeDtypeStruct((size, (words + 1) * block), jnp.int32),
        in_specs=[pl.BlockSpec(memory_space=pltpu.SMEM)] + [anywhere] * 3 + [pl.BlockSpec(memory_space=pltpu.HBM)],
        out_specs=pl.BlockSpec(memory_space=pltpu.VMEM),
        scratch_shapes=[
            pltpu.VMEM((size, width), own.dtype),
            pltpu.VMEM(blocks.shape, blocks.dtype),
            pltpu.SemaphoreType.DMA((3,)),
            pltpu.SemaphoreType.DMA((rows // 2,)),
        ],
        compiler_params=pltpu.CompilerParams(vmem_limit_bytes=VMEM_LIMIT),
        cost_estimate=pl.CostEstimate(flops=1, bytes_accessed=1, transcendentals=0),
        name="coded_products",
    )(index, left, own, right, pltpu.with_memory_space_constraint(blocks, pltpu.HBM))


def decoded(coded_ref, row, half, at, block, words):
    lane = lax.broadcasted_iota(jnp.int32, (coded_ref.shape[0], block), 1)
    codes = coded_ref[:, words * block :].astype(jnp.float32)
    code = jnp.sum(jnp.where(lane == row, codes, 0.0), axis=1, keepdims=True)
    word = coded_ref[:, pl.ds(at, block)]
    value = (word >> 16) if half else ((word << 16) >> 16)
    return value.astype(jnp.float32) * (jnp.exp2(code * (1.0 / FINE)) * (1.0 / TOP))


def final_kernel(group, slots, block, words, starts, pieces, aliased, index_ref, *refs):
    count = sum(partials for _, _, _, partials in pieces)
    sources, blocks_ref, coded = refs[:3], refs[3], refs[4 : 4 + count]
    refs = refs[4 + count + aliased :]
    out_ref, ext, panels, result, sems, panel_sems, coded_sems, out_sems = refs[:8]
    held = refs[8:]
    size, rows = ext.shape[0], panels.shape[0]
    copies = fill(sources, starts, ext, sems)
    n = 0
    for _, length, start, partials in pieces:
        for _ in range(partials):
            source = coded[n].at[pl.ds(start, length)]
            copies.append(pltpu.make_async_copy(source, held[n], coded_sems.at[n]))
            copies[-1].start()
            n += 1
    wait = start_panels(blocks_ref, panels, panel_sems)
    ext[:, ext.shape[1] - block :] = jnp.zeros((size, block), ext.dtype)
    for copy in copies:
        copy.wait()

    def result_copy(step):
        columns = pl.ds(pl.multiple_of(step * group * block, block), group * block)
        target = out_ref.at[pl.ds(starts[1], size), columns]
        return pltpu.make_async_copy(result.at[:, columns], target, out_sems.at[step])

    @pl.loop(0, rows // group)
    def _(step):
        wait(step, group)
        first = step * group
        sums = [
            row_sums(index_ref, first + member, slots, block, ext, panels.at[first + member])
            for member in range(group)
        ]
        for member, mine in enumerate(sums):
            at = pl.multiple_of((first // 2 + member // 2) * block, block)
            column = pl.multiple_of((first + member) * block, block)
            n = 0
            for offset, length, _, partials in pieces:
                total = mine[offset : offset + length]
                for _ in range(partials):
                    total = total + decoded(held[n], first + member, member % 2, at, block, words)
                    n += 1
                result[offset : offset + length, pl.ds(column, block)] = total.astype(result.dtype)
        result_copy(step).start()

    @pl.loop(0, rows // group)
    def _(step):
        result_copy(step).wait()


def final_products(index, left, own, right, starts, size, blocks, pieces, out):
    rows, slots, block, _ = blocks.shape
    words, group = rows // 2, group_of(rows)
    width = own.shape[1]
    arrays = [array for _, _, _, some in pieces for array in some]
    operands = [index, left, own, right, pltpu.with_memory_space_constraint(blocks, pltpu.HBM), *arrays]
    anywhere = pl.BlockSpec(memory_space=pl.ANY)
    aliases = {}
    if out is not None:
        aliases = {len(operands): 0}
        operands.append(out)
    in_specs = [pl.BlockSpec(memory_space=pltpu.SMEM)] + [anywhere] * (len(operands) - 1)
    in_specs[4] = pl.BlockSpec(memory_space=pltpu.HBM)
    shapes = tuple((offset, length, start, len(some)) for offset, length, start, some in pieces)
    return pl.pallas_call(
        functools.partial(final_kernel, group, slots, block, words, starts, shapes, len(aliases)),
        out_shape=jax.ShapeDtypeStruct(own.shape, own.dtype),
        in_specs=in_specs,
        out_specs=anywhere,
        scratch_shapes=[
            pltpu.VMEM((size, 2 * left.shape[1] + width + block), own.dtype),
            pltpu.VMEM(blocks.shape, blocks.dtype),
            pltpu.VMEM((size, width), own.dtype),
            pltpu.SemaphoreType.DMA((3,)),
            pltpu.SemaphoreType.DMA((rows // 2,)),
            pltpu.SemaphoreType.DMA((len(arrays),)),
            pltpu.SemaphoreType.DMA((rows // group,)),
        ]
        + [
            pltpu.VMEM((length, (words + 1) * block), jnp.int32)
            for _, length, _, partials in shapes
            for _ in range(partials)
        ],
        input_output_aliases=aliases,
        compiler_params=pltpu.CompilerParams(vmem_limit_bytes=VMEM_LIMIT),
        cost_estimate=pl.CostEstimate(flops=1, bytes_accessed=1, transcendentals=0),
        name="final_products",
    )(*operands)


def starts_of(sizes):
    return [sum(sizes[:i]) for i in range(len(sizes))]


def on_device(vectors, blocks, columns, counts):
    states, width = vectors.shape
    rows, slots, block, _ = blocks.shape
    reach = W * block
    basis_size, state_size = lax.axis_size("basis"), lax.axis_size("state")
    if states % 256 == 0:
        sizes = (5 * states // 16, 5 * states // 16, 3 * states // 8)
        own_sizes = (3 * states // 8, 5 * states // 8)
    else:
        sizes, own_sizes = (states,), (states,)
    starts, own_starts = starts_of(sizes), starts_of(own_sizes)

    slot_index = lax.axis_index("state") * slots + jnp.arange(slots, dtype=jnp.int32)
    relative = columns - (lax.axis_index("basis") * rows - W)
    zeros_at = rows + 2 * W
    index = jnp.where(slot_index[None, :] < counts[:, None], relative, zeros_at).reshape(-1)

    up = [(i, i + 1) for i in range(basis_size - 1)]
    down = [(i + 1, i) for i in range(basis_size - 1)]

    def edges_of(piece, *others):
        edges = (piece[:, width - reach :], piece[:, :reach])
        return lax.optimization_barrier((*edges, *others))[:2] if others else edges

    def halo(edges):
        return lax.ppermute(edges[0], "basis", up), lax.ppermute(edges[1], "basis", down)

    def shifted(piece, shift):
        return lax.ppermute(piece, "state", [(i, (i + shift) % state_size) for i in range(state_size)])

    def own_edges(part, *others):
        return edges_of(vectors[own_starts[part] : own_starts[part] + own_sizes[part]], *others)

    messages = [(shift, c) for shift in range(1, state_size) for c in range(len(sizes))]
    count = len(messages)
    theirs, edges, ends, sent, received = [], [], [], [], []
    first_edges = own_edges(0)
    first = halo(first_edges)
    for n, (shift, c) in enumerate(messages):
        source = after(vectors, *(first_edges if n == 1 else first)) if n else vectors
        theirs.append(shifted(source[starts[c] : starts[c] + sizes[c]], shift))

    def compute(n):
        later = edges[n + 1] if n + 1 < len(edges) else ()
        ready = after(index, *later) if later else index
        sent.append(coded_products(ready, ends[n][0], theirs[n], ends[n][1], blocks))
        message = after(sent[n], received[n - 1]) if n else sent[n]
        received.append(shifted(message, -messages[n][0]))

    for n in range(count):
        edges.append(edges_of(theirs[n]))
        ends.append(halo(edges[n]))
        if n:
            compute(n - 1)
    own_ends = [first]
    if len(own_sizes) > 1:
        edges.append(own_edges(1, *ends[-1], *sent[-1:], *received[:1]))
        own_ends.append(halo(edges[-1]))
    compute(count - 1)

    out = None
    for part, own_size in enumerate(own_sizes):
        own_start, pieces = own_starts[part], []
        for c, size in enumerate(sizes):
            at = max(own_start, starts[c])
            end = min(own_start + own_size, starts[c] + size)
            if at < end:
                arrays = [received[n] for n in range(count) if messages[n][1] == c]
                pieces.append((at - own_start, end - at, at - starts[c], arrays))
        left, right = own_ends[part]
        ready = after(index, sent[-1], out) if part else after(index, sent[-1])
        out = final_products(
            ready, left, vectors, right, (0, own_start, 0), own_size, blocks, pieces, out
        )
    return out


def solution(mesh):
    in_specs = (
        P("state", "basis"),
        P("basis", "state", None, None),
        P("basis", "state"),
        P("basis"),
    )
    out_specs = P("state", "basis")
    return jax.shard_map(
        on_device, mesh=mesh, in_specs=in_specs, out_specs=out_specs, check_vma=False
    )
```

```python
import functools
import math

import jax
import jax.numpy as jnp
from jax import lax
from jax.experimental import pallas as pl
from jax.experimental.pallas import tpu as pltpu
from jax.sharding import PartitionSpec as P

W = 36
VMEM_LIMIT = 32 * 1024 * 1024
TOP = 32767.0
FINE = 65536.0
SMALLEST = 2.0**-100


def after(array, *others):
    return lax.optimization_barrier((array, *others))[0]


def fill(sources, starts, ext, sems):
    copies, column = [], 0
    for n, (source, start) in enumerate(zip(sources, starts)):
        width = source.shape[1]
        target = ext.at[:, pl.ds(column, width)]
        copies.append(pltpu.make_async_copy(source.at[pl.ds(start, ext.shape[0])], target, sems.at[n]))
        copies[-1].start()
        column += width
    return copies


def row_sums(index_ref, row, slots, block, ext, panel_ref):
    picked = jnp.concatenate(
        [
            ext[:, pl.ds(pl.multiple_of(index_ref[row * slots + slot] * block, block), block)]
            for slot in range(slots)
        ],
        axis=1,
    )
    panel = jnp.concatenate([panel_ref[slot] for slot in range(slots)], axis=1)
    return lax.dot_general(
        picked, panel, (((1,), (1,)), ((), ())), preferred_element_type=jnp.float32
    )


def level_code(top):
    return jnp.ceil(jnp.log2(jnp.maximum(top, SMALLEST)) * FINE).astype(jnp.int32)


def level_of(code):
    return jnp.exp2(code.astype(jnp.float32) * (1.0 / FINE))


def code_into(out_ref, first, block, words, sums):
    lane = lax.broadcasted_iota(jnp.int32, (out_ref.shape[0], block), 1)
    codes = out_ref[:, words * block :]
    values = []
    for member, mine in enumerate(sums):
        code = level_code(jnp.max(jnp.abs(mine), axis=1, keepdims=True))
        codes = jnp.where(lane == first + member, code, codes)
        scaled = jnp.round(mine * (TOP / level_of(code)))
        values.append(jnp.clip(scaled, -TOP, TOP).astype(jnp.int32))
    out_ref[:, words * block :] = codes
    for pair in range(len(sums) // 2):
        word = (values[2 * pair + 1] << 16) | (values[2 * pair] & 0xFFFF)
        at = pl.multiple_of((first // 2 + pair) * block, block)
        out_ref[:, pl.ds(at, block)] = word


def start_panels(blocks_ref, panels, sems):
    piece = panels.shape[0] // sems.shape[0]

    def copy(n):
        here = pl.ds(n * piece, piece)
        return pltpu.make_async_copy(blocks_ref.at[here], panels.at[here], sems.at[n])

    def wait(step, group):
        for n in range(group // piece):
            copy(step * (group // piece) + n).wait()

    for n in range(sems.shape[0]):
        copy(n).start()
    return wait


def coded_kernel(group, slots, block, words, index_ref, *refs):
    sources, (blocks_ref, out_ref, ext, panels, sems, panel_sems) = refs[:3], refs[3:]
    size = ext.shape[0]
    copies = fill(sources, (0, 0, 0), ext, sems)
    wait = start_panels(blocks_ref, panels, panel_sems)
    ext[:, ext.shape[1] - block :] = jnp.zeros((size, block), ext.dtype)
    out_ref[:, words * block :] = jnp.zeros((size, block), jnp.int32)
    for copy in copies:
        copy.wait()

    @pl.loop(0, panels.shape[0] // group)
    def _(step):
        wait(step, group)
        first = step * group
        sums = [
            row_sums(index_ref, first + member, slots, block, ext, panels.at[first + member])
            for member in range(group)
        ]
        code_into(out_ref, first, block, words, sums)


def group_of(rows):
    return 8 if rows % 8 == 0 else 2


def coded_products(index, left, own, right, blocks):
    rows, slots, block, _ = blocks.shape
    size, words, group = own.shape[0], rows // 2, group_of(rows)
    width = 2 * left.shape[1] + own.shape[1] + block
    anywhere = pl.BlockSpec(memory_space=pl.ANY)
    return pl.pallas_call(
        functools.partial(coded_kernel, group, slots, block, words),
        out_shape=jax.ShapeDtypeStruct((size, (words + 1) * block), jnp.int32),
        in_specs=[pl.BlockSpec(memory_space=pltpu.SMEM)] + [anywhere] * 3 + [pl.BlockSpec(memory_space=pltpu.HBM)],
        out_specs=pl.BlockSpec(memory_space=pltpu.VMEM),
        scratch_shapes=[
            pltpu.VMEM((size, width), own.dtype),
            pltpu.VMEM(blocks.shape, blocks.dtype),
            pltpu.SemaphoreType.DMA((3,)),
            pltpu.SemaphoreType.DMA((rows // 2,)),
        ],
        compiler_params=pltpu.CompilerParams(vmem_limit_bytes=VMEM_LIMIT),
        cost_estimate=pl.CostEstimate(flops=1, bytes_accessed=1, transcendentals=0),
        name="coded_products",
    )(index, left, own, right, pltpu.with_memory_space_constraint(blocks, pltpu.HBM))


def decoded(coded_ref, row, half, at, block, words):
    lane = lax.broadcasted_iota(jnp.int32, (coded_ref.shape[0], block), 1)
    codes = coded_ref[:, words * block :].astype(jnp.float32)
    code = jnp.sum(jnp.where(lane == row, codes, 0.0), axis=1, keepdims=True)
    word = coded_ref[:, pl.ds(at, block)]
    value = (word >> 16) if half else ((word << 16) >> 16)
    return value.astype(jnp.float32) * (jnp.exp2(code * (1.0 / FINE)) * (1.0 / TOP))


def final_kernel(group, slots, block, words, starts, pieces, aliased, index_ref, *refs):
    count = sum(partials for _, _, _, partials in pieces)
    sources, blocks_ref, coded = refs[:3], refs[3], refs[4 : 4 + count]
    refs = refs[4 + count + aliased :]
    out_ref, ext, panels, result, sems, panel_sems, coded_sems, out_sems = refs[:8]
    held = refs[8:]
    size, rows = ext.shape[0], panels.shape[0]
    copies = fill(sources, starts, ext, sems)
    n = 0
    for _, length, start, partials in pieces:
        for _ in range(partials):
            source = coded[n].at[pl.ds(start, length)]
            copies.append(pltpu.make_async_copy(source, held[n], coded_sems.at[n]))
            copies[-1].start()
            n += 1
    wait = start_panels(blocks_ref, panels, panel_sems)
    ext[:, ext.shape[1] - block :] = jnp.zeros((size, block), ext.dtype)
    for copy in copies:
        copy.wait()

    def result_copy(step):
        columns = pl.ds(pl.multiple_of(step * group * block, block), group * block)
        target = out_ref.at[pl.ds(starts[1], size), columns]
        return pltpu.make_async_copy(result.at[:, columns], target, out_sems.at[step])

    @pl.loop(0, rows // group)
    def _(step):
        wait(step, group)
        first = step * group
        sums = [
            row_sums(index_ref, first + member, slots, block, ext, panels.at[first + member])
            for member in range(group)
        ]
        for member, mine in enumerate(sums):
            at = pl.multiple_of((first // 2 + member // 2) * block, block)
            column = pl.multiple_of((first + member) * block, block)
            n = 0
            for offset, length, _, partials in pieces:
                total = mine[offset : offset + length]
                for _ in range(partials):
                    total = total + decoded(held[n], first + member, member % 2, at, block, words)
                    n += 1
                result[offset : offset + length, pl.ds(column, block)] = total.astype(result.dtype)
        result_copy(step).start()

    @pl.loop(0, rows // group)
    def _(step):
        result_copy(step).wait()


def final_products(index, left, own, right, starts, size, blocks, pieces, out):
    rows, slots, block, _ = blocks.shape
    words, group = rows // 2, group_of(rows)
    width = own.shape[1]
    arrays = [array for _, _, _, some in pieces for array in some]
    operands = [index, left, own, right, pltpu.with_memory_space_constraint(blocks, pltpu.HBM), *arrays]
    anywhere = pl.BlockSpec(memory_space=pl.ANY)
    aliases = {}
    if out is not None:
        aliases = {len(operands): 0}
        operands.append(out)
    in_specs = [pl.BlockSpec(memory_space=pltpu.SMEM)] + [anywhere] * (len(operands) - 1)
    in_specs[4] = pl.BlockSpec(memory_space=pltpu.HBM)
    shapes = tuple((offset, length, start, len(some)) for offset, length, start, some in pieces)
    return pl.pallas_call(
        functools.partial(final_kernel, group, slots, block, words, starts, shapes, len(aliases)),
        out_shape=jax.ShapeDtypeStruct(own.shape, own.dtype),
        in_specs=in_specs,
        out_specs=anywhere,
        scratch_shapes=[
            pltpu.VMEM((size, 2 * left.shape[1] + width + block), own.dtype),
            pltpu.VMEM(blocks.shape, blocks.dtype),
            pltpu.VMEM((size, width), own.dtype),
            pltpu.SemaphoreType.DMA((3,)),
            pltpu.SemaphoreType.DMA((rows // 2,)),
            pltpu.SemaphoreType.DMA((len(arrays),)),
            pltpu.SemaphoreType.DMA((rows // group,)),
        ]
        + [
            pltpu.VMEM((length, (words + 1) * block), jnp.int32)
            for _, length, _, partials in shapes
            for _ in range(partials)
        ],
        input_output_aliases=aliases,
        compiler_params=pltpu.CompilerParams(vmem_limit_bytes=VMEM_LIMIT),
        cost_estimate=pl.CostEstimate(flops=1, bytes_accessed=1, transcendentals=0),
        name="final_products",
    )(*operands)


def starts_of(sizes):
    return [sum(sizes[:i]) for i in range(len(sizes))]


def on_device(vectors, blocks, columns, counts):
    states, width = vectors.shape
    rows, slots, block, _ = blocks.shape
    reach = W * block
    basis_size, state_size = lax.axis_size("basis"), lax.axis_size("state")
    if states % 256 == 0:
        sizes = (5 * states // 16, 5 * states // 16, 3 * states // 8)
        own_sizes = (3 * states // 8, 5 * states // 8)
    else:
        sizes, own_sizes = (states,), (states,)
    starts, own_starts = starts_of(sizes), starts_of(own_sizes)

    slot_index = lax.axis_index("state") * slots + jnp.arange(slots, dtype=jnp.int32)
    relative = columns - (lax.axis_index("basis") * rows - W)
    zeros_at = rows + 2 * W
    index = jnp.where(slot_index[None, :] < counts[:, None], relative, zeros_at).reshape(-1)

    up = [(i, i + 1) for i in range(basis_size - 1)]
    down = [(i + 1, i) for i in range(basis_size - 1)]

    def edges_of(piece, *others):
        edges = (piece[:, width - reach :], piece[:, :reach])
        return lax.optimization_barrier((*edges, *others))[:2] if others else edges

    def halo(edges):
        return lax.ppermute(edges[0], "basis", up), lax.ppermute(edges[1], "basis", down)

    def shifted(piece, shift):
        return lax.ppermute(piece, "state", [(i, (i + shift) % state_size) for i in range(state_size)])

    def own_edges(part, *others):
        return edges_of(vectors[own_starts[part] : own_starts[part] + own_sizes[part]], *others)

    messages = [(shift, c) for shift in range(1, state_size) for c in range(len(sizes))]
    count = len(messages)
    theirs, edges, ends, sent, received = [], [], [], [], []
    first_edges = own_edges(0)
    first = halo(first_edges)
    for n, (shift, c) in enumerate(messages):
        source = after(vectors, *(first_edges if n == 1 else first)) if n else vectors
        theirs.append(shifted(source[starts[c] : starts[c] + sizes[c]], shift))

    def compute(n):
        later = edges[n + 1] if n + 1 < len(edges) else ()
        ready = after(index, *later) if later else index
        sent.append(coded_products(ready, ends[n][0], theirs[n], ends[n][1], blocks))
        message = after(sent[n], received[n - 1]) if n else sent[n]
        received.append(shifted(message, -messages[n][0]))

    for n in range(count):
        edges.append(edges_of(theirs[n]))
        ends.append(halo(edges[n]))
        if n:
            compute(n - 1)
    compute(count - 1)
    own_ends = [first]
    if len(own_sizes) > 1:
        own_ends.append(halo(own_edges(1, sent[-1])))

    out = None
    for part, own_size in enumerate(own_sizes):
        own_start, pieces = own_starts[part], []
        for c, size in enumerate(sizes):
            at = max(own_start, starts[c])
            end = min(own_start + own_size, starts[c] + size)
            if at < end:
                arrays = [received[n] for n in range(count) if messages[n][1] == c]
                pieces.append((at - own_start, end - at, at - starts[c], arrays))
        left, right = own_ends[part]
        ready = after(index, sent[-1], out) if part else after(index, sent[-1])
        out = final_products(
            ready, left, vectors, right, (0, own_start, 0), own_size, blocks, pieces, out
        )
    return out


def solution(mesh):
    in_specs = (
        P("state", "basis"),
        P("basis", "state", None, None),
        P("basis", "state"),
        P("basis"),
    )
    out_specs = P("state", "basis")
    return jax.shard_map(
        on_device, mesh=mesh, in_specs=in_specs, out_specs=out_specs, check_vma=False
    )
```

```python
import functools
import math

import jax
import jax.numpy as jnp
from jax import lax
from jax.experimental import pallas as pl
from jax.experimental.pallas import tpu as pltpu
from jax.sharding import PartitionSpec as P

W = 36
VMEM_LIMIT = 32 * 1024 * 1024
TOP = 32767.0
FINE = 65536.0
SMALLEST = 2.0**-100


def after(array, *others):
    return lax.optimization_barrier((array, *others))[0]


def fill(sources, plan, ext, sems):
    copies, at = [], 0
    for part, (start, size, _) in enumerate(plan):
        left, own, right = sources[3 * part : 3 * part + 3]
        reach, width = left.shape[1], own.shape[1]
        rows = pl.ds(at, size)
        copies += [
            pltpu.make_async_copy(left, ext.at[rows, pl.ds(0, reach)], sems.at[3 * part]),
            pltpu.make_async_copy(
                own.at[pl.ds(start, size)], ext.at[rows, pl.ds(reach, width)], sems.at[3 * part + 1]
            ),
            pltpu.make_async_copy(right, ext.at[rows, pl.ds(reach + width, reach)], sems.at[3 * part + 2]),
        ]
        at += size
    for copy in copies:
        copy.start()
    return copies


def row_sums(index_ref, row, slots, block, ext, panel_ref):
    picked = jnp.concatenate(
        [
            ext[:, pl.ds(pl.multiple_of(index_ref[row * slots + slot] * block, block), block)]
            for slot in range(slots)
        ],
        axis=1,
    )
    panel = jnp.concatenate([panel_ref[slot] for slot in range(slots)], axis=1)
    return lax.dot_general(
        picked, panel, (((1,), (1,)), ((), ())), preferred_element_type=jnp.float32
    )


def level_code(top):
    return jnp.ceil(jnp.log2(jnp.maximum(top, SMALLEST)) * FINE).astype(jnp.int32)


def level_of(code):
    return jnp.exp2(code.astype(jnp.float32) * (1.0 / FINE))


def code_into(out_ref, first, block, words, sums):
    lane = lax.broadcasted_iota(jnp.int32, (out_ref.shape[0], block), 1)
    codes = out_ref[:, words * block :]
    values = []
    for member, mine in enumerate(sums):
        code = level_code(jnp.max(jnp.abs(mine), axis=1, keepdims=True))
        codes = jnp.where(lane == first + member, code, codes)
        scaled = jnp.round(mine * (TOP / level_of(code)))
        values.append(jnp.clip(scaled, -TOP, TOP).astype(jnp.int32))
    out_ref[:, words * block :] = codes
    for pair in range(len(sums) // 2):
        word = (values[2 * pair + 1] << 16) | (values[2 * pair] & 0xFFFF)
        at = pl.multiple_of((first // 2 + pair) * block, block)
        out_ref[:, pl.ds(at, block)] = word


def products_kernel(plan, group, slots, block, words, index_ref, *refs):
    parts = len(plan)
    sources, blocks_ref = refs[: 3 * parts], refs[3 * parts]
    outs, (ext, panels, sems, panel_sems) = refs[3 * parts + 1 : 4 * parts + 1], refs[4 * parts + 1 :]
    rows, pieces = panels.shape[0], panel_sems.shape[0]
    piece = rows // pieces

    def panel_copy(n):
        here = pl.ds(n * piece, piece)
        return pltpu.make_async_copy(blocks_ref.at[here], panels.at[here], panel_sems.at[n])

    copies = fill(sources, plan, ext, sems)
    for n in range(pieces):
        panel_copy(n).start()
    end = ext.shape[1] - block
    ext[:, end:] = jnp.zeros((ext.shape[0], block), ext.dtype)
    for (_, size, coded), out_ref in zip(plan, outs):
        if coded:
            out_ref[:, words * block :] = jnp.zeros((size, block), jnp.int32)
    for copy in copies:
        copy.wait()

    @pl.loop(0, rows // group)
    def _(step):
        for n in range(group // piece):
            panel_copy(step * (group // piece) + n).wait()
        first = step * group
        sums = [
            row_sums(index_ref, first + member, slots, block, ext, panels.at[first + member])
            for member in range(group)
        ]
        at = 0
        for (_, size, coded), out_ref in zip(plan, outs):
            mine = [total[at : at + size] for total in sums]
            if coded:
                code_into(out_ref, first, block, words, mine)
            else:
                for member in range(group):
                    column = pl.multiple_of((first + member) * block, block)
                    out_ref[:, pl.ds(column, block)] = mine[member]
            at += size


def products(index, parts, blocks):
    rows, slots, block, _ = blocks.shape
    reach, width = parts[0][0].shape[1], parts[0][1].shape[1]
    plan = tuple(part[3:] for part in parts)
    states = sum(size for _, size, _ in plan)
    group, words = 8 if rows % 8 == 0 else 2, rows // 2
    sources = [array for part in parts for array in part[:3]]
    anywhere = pl.BlockSpec(memory_space=pl.ANY)
    out_shape = []
    for _, size, coded in plan:
        if coded:
            out_shape.append(jax.ShapeDtypeStruct((size, (words + 1) * block), jnp.int32))
        else:
            out_shape.append(jax.ShapeDtypeStruct((size, width), jnp.float32))
    return pl.pallas_call(
        functools.partial(products_kernel, plan, group, slots, block, words),
        out_shape=out_shape,
        in_specs=[pl.BlockSpec(memory_space=pltpu.SMEM)]
        + [anywhere] * len(sources)
        + [pl.BlockSpec(memory_space=pltpu.HBM)],
        out_specs=[pl.BlockSpec(memory_space=pltpu.VMEM)] * len(plan),
        scratch_shapes=[
            pltpu.VMEM((states, 2 * reach + width + block), parts[0][1].dtype),
            pltpu.VMEM(blocks.shape, blocks.dtype),
            pltpu.SemaphoreType.DMA((len(sources),)),
            pltpu.SemaphoreType.DMA((rows // 2,)),
        ],
        compiler_params=pltpu.CompilerParams(vmem_limit_bytes=VMEM_LIMIT),
        cost_estimate=pl.CostEstimate(flops=1, bytes_accessed=1, transcendentals=0),
        name="products",
    )(index, *sources, pltpu.with_memory_space_constraint(blocks, pltpu.HBM))


def finish_kernel(partials, block, pairs, own_ref, *refs):
    out_ref = refs[-1]
    step = pl.program_id(0)
    lane = lax.broadcasted_iota(jnp.int32, (own_ref.shape[0], block), 1)
    levels = [level_of(refs[2 * p + 1][...]) * (1.0 / TOP) for p in range(partials)]
    for pair in range(pairs):
        for half in range(2):
            at = (2 * pair + half) * block
            row = (step * pairs + pair) * 2 + half
            total = own_ref[:, at : at + block]
            for p in range(partials):
                word = refs[2 * p][:, pair * block : (pair + 1) * block]
                value = (word >> 16) if half else ((word << 16) >> 16)
                level = jnp.max(jnp.where(lane == row, levels[p], 0.0), axis=1, keepdims=True)
                total = total + value.astype(jnp.float32) * level
            out_ref[:, at : at + block] = total.astype(out_ref.dtype)


def finish(own_sums, own_start, coded, coded_start, out, start, size, states, block):
    width = own_sums.shape[1]
    words = width // block // 2
    pairs = words // 2 if words % 2 == 0 else 1
    rows, wide, narrow = pl.Element(size), pl.Element(2 * pairs * block), pl.Element(pairs * block)
    own_at, coded_at = start - own_start, start - coded_start
    in_specs = [pl.BlockSpec((rows, wide), lambda i: (own_at, i * 2 * pairs * block))]
    operands = [own_sums]
    for array in coded:
        in_specs.append(pl.BlockSpec((rows, narrow), lambda i: (coded_at, i * pairs * block)))
        in_specs.append(pl.BlockSpec((rows, pl.Element(block)), lambda i: (coded_at, words * block)))
        operands += [array, array]
    aliases = {}
    if out is not None:
        aliases = {len(operands): 0}
        in_specs.append(pl.BlockSpec(memory_space=pl.ANY))
        operands.append(out)
    return pl.pallas_call(
        functools.partial(finish_kernel, len(coded), block, pairs),
        out_shape=jax.ShapeDtypeStruct((states, width), jnp.bfloat16),
        grid=(words // pairs,),
        in_specs=in_specs,
        out_specs=pl.BlockSpec((rows, wide), lambda i: (start, i * 2 * pairs * block)),
        input_output_aliases=aliases,
        compiler_params=pltpu.CompilerParams(vmem_limit_bytes=VMEM_LIMIT),
        cost_estimate=pl.CostEstimate(flops=1, bytes_accessed=1, transcendentals=0),
        name="finish",
    )(*operands)


def starts_of(sizes):
    return [sum(sizes[:i]) for i in range(len(sizes))]


def on_device(vectors, blocks, columns, counts):
    states, width = vectors.shape
    rows, slots, block, _ = blocks.shape
    reach = W * block
    basis_size, state_size = lax.axis_size("basis"), lax.axis_size("state")
    if states % 256 == 0:
        sizes = (5 * states // 16, 3 * states // 8, 5 * states // 16)
        own_sizes = (7 * states // 16, 9 * states // 16)
    else:
        sizes, own_sizes = (states,), (states,)
    starts, own_starts = starts_of(sizes), starts_of(own_sizes)

    slot_index = lax.axis_index("state") * slots + jnp.arange(slots, dtype=jnp.int32)
    relative = columns - (lax.axis_index("basis") * rows - W)
    zeros_at = rows + 2 * W
    index = jnp.where(slot_index[None, :] < counts[:, None], relative, zeros_at).reshape(-1)

    up = [(i, i + 1) for i in range(basis_size - 1)]
    down = [(i + 1, i) for i in range(basis_size - 1)]

    def edges_of(piece, *others):
        edges = (piece[:, width - reach :], piece[:, :reach])
        return lax.optimization_barrier((*edges, *others))[:2] if others else edges

    def halo(edges):
        return lax.ppermute(edges[0], "basis", up), lax.ppermute(edges[1], "basis", down)

    def shifted(piece, shift):
        return lax.ppermute(piece, "state", [(i, (i + shift) % state_size) for i in range(state_size)])

    def own_edges(part, *others):
        return edges_of(vectors[own_starts[part] : own_starts[part] + own_sizes[part]], *others)

    def own_part(part, ends):
        return (ends[0], vectors, ends[1], own_starts[part], own_sizes[part], False)

    def their_part(n):
        return (ends[n][0], theirs[n], ends[n][1], 0, theirs[n].shape[0], True)

    messages = [(shift, c) for shift in range(1, state_size) for c in range(len(sizes))]
    count = len(messages)
    theirs, edges, ends, sent, own_sums, received = [], [], [], [], [], []
    first_edges = own_edges(0)
    first = halo(first_edges)
    for n, (shift, c) in enumerate(messages):
        source = after(vectors, *(first_edges if n == 1 else first)) if n else vectors
        theirs.append(shifted(source[starts[c] : starts[c] + sizes[c]], shift))

    def compute(n):
        later = edges[n + 1] if n + 1 < len(edges) else ()
        sent.extend(products(after(index, *later) if later else index, [their_part(n)], blocks))
        message = after(sent[n], received[n - 1]) if n else sent[n]
        received.append(shifted(message, -messages[n][0]))

    for n in range(count):
        edges.append(edges_of(theirs[n]))
        ends.append(halo(edges[n]))
        if n:
            compute(n - 1)
    if len(own_sizes) > 1:
        edges.append(own_edges(1, *edges[-1], *sent[-1:], *received[:1]))
        last = halo(edges[-1])
    compute(count - 1)
    coded = [[received[n] for n in range(count) if messages[n][1] == c] for c in range(len(sizes))]
    own_sums += products(after(index, sent[-1]), [own_part(0, first)], blocks)
    out = None
    for part, own_size in enumerate(own_sizes):
        if part:
            own_sums += products(after(index, out), [own_part(part, last)], blocks)
        for c, size in enumerate(sizes):
            at = max(own_starts[part], starts[c])
            end = min(own_starts[part] + own_size, starts[c] + size)
            if at < end:
                out = finish(
                    own_sums[part], own_starts[part], coded[c], starts[c], out, at, end - at, states, block
                )
    return out


def solution(mesh):
    in_specs = (
        P("state", "basis"),
        P("basis", "state", None, None),
        P("basis", "state"),
        P("basis"),
    )
    out_specs = P("state", "basis")
    return jax.shard_map(
        on_device, mesh=mesh, in_specs=in_specs, out_specs=out_specs, check_vma=False
    )
```

```python
import functools
import math

import jax
import jax.numpy as jnp
from jax import lax
from jax.experimental import pallas as pl
from jax.experimental.pallas import tpu as pltpu
from jax.sharding import PartitionSpec as P

W = 36
VMEM_LIMIT = 32 * 1024 * 1024
TOP = 32767.0
FINE = 65536.0
SMALLEST = 2.0**-100


def after(array, *others):
    return lax.optimization_barrier((array, *others))[0]


def fill(sources, plan, ext, sems):
    copies, at = [], 0
    for part, (start, size, _) in enumerate(plan):
        for offset in range(0, size, 16):
            column = 0
            for n, source in enumerate(sources[3 * part : 3 * part + 3]):
                width = source.shape[1]
                rows = pl.ds(offset + (start if n == 1 else 0), 16)
                target = ext.at[pl.ds(at + offset, 16), pl.ds(column, width)]
                copies.append(pltpu.make_async_copy(source.at[rows], target, sems.at[len(copies)]))
                column += width
        at += size
    for copy in copies:
        copy.start()
    return copies


def row_sums(index_ref, row, slots, block, ext, panel_ref):
    picked = jnp.concatenate(
        [
            ext[:, pl.ds(pl.multiple_of(index_ref[row * slots + slot] * block, block), block)]
            for slot in range(slots)
        ],
        axis=1,
    )
    panel = jnp.concatenate([panel_ref[slot] for slot in range(slots)], axis=1)
    return lax.dot_general(
        picked, panel, (((1,), (1,)), ((), ())), preferred_element_type=jnp.float32
    )


def level_code(top):
    return jnp.ceil(jnp.log2(jnp.maximum(top, SMALLEST)) * FINE).astype(jnp.int32)


def level_of(code):
    return jnp.exp2(code.astype(jnp.float32) * (1.0 / FINE))


def code_into(out_ref, first, block, words, sums):
    lane = lax.broadcasted_iota(jnp.int32, (out_ref.shape[0], block), 1)
    codes = out_ref[:, words * block :]
    values = []
    for member, mine in enumerate(sums):
        code = level_code(jnp.max(jnp.abs(mine), axis=1, keepdims=True))
        codes = jnp.where(lane == first + member, code, codes)
        scaled = jnp.round(mine * (TOP / level_of(code)))
        values.append(jnp.clip(scaled, -TOP, TOP).astype(jnp.int32))
    out_ref[:, words * block :] = codes
    for pair in range(len(sums) // 2):
        word = (values[2 * pair + 1] << 16) | (values[2 * pair] & 0xFFFF)
        at = pl.multiple_of((first // 2 + pair) * block, block)
        out_ref[:, pl.ds(at, block)] = word


def products_kernel(plan, group, slots, block, words, index_ref, *refs):
    parts = len(plan)
    sources, blocks_ref = refs[: 3 * parts], refs[3 * parts]
    outs, (ext, panels, sems, panel_sems) = refs[3 * parts + 1 : 4 * parts + 1], refs[4 * parts + 1 :]
    rows, pieces = panels.shape[0], panel_sems.shape[0]
    piece = rows // pieces

    def panel_copy(n):
        here = pl.ds(n * piece, piece)
        return pltpu.make_async_copy(blocks_ref.at[here], panels.at[here], panel_sems.at[n])

    early = group // piece
    copies = fill(sources, plan, ext, sems)
    for n in range(early):
        panel_copy(n).start()
    end = ext.shape[1] - block
    ext[:, end:] = jnp.zeros((ext.shape[0], block), ext.dtype)
    for (_, size, coded), out_ref in zip(plan, outs):
        if coded:
            out_ref[:, words * block :] = jnp.zeros((size, block), jnp.int32)
    for copy in copies:
        copy.wait()
    for n in range(early, pieces):
        panel_copy(n).start()

    @pl.loop(0, rows // group)
    def _(step):
        for n in range(group // piece):
            panel_copy(step * (group // piece) + n).wait()
        first = step * group
        sums = [
            row_sums(index_ref, first + member, slots, block, ext, panels.at[first + member])
            for member in range(group)
        ]
        at = 0
        for (_, size, coded), out_ref in zip(plan, outs):
            mine = [total[at : at + size] for total in sums]
            if coded:
                code_into(out_ref, first, block, words, mine)
            else:
                for member in range(group):
                    column = pl.multiple_of((first + member) * block, block)
                    out_ref[:, pl.ds(column, block)] = mine[member]
            at += size


def products(index, parts, blocks):
    rows, slots, block, _ = blocks.shape
    reach, width = parts[0][0].shape[1], parts[0][1].shape[1]
    plan = tuple(part[3:] for part in parts)
    states = sum(size for _, size, _ in plan)
    group, words = 8 if rows % 8 == 0 else 2, rows // 2
    sources = [array for part in parts for array in part[:3]]
    anywhere = pl.BlockSpec(memory_space=pl.ANY)
    out_shape = []
    for _, size, coded in plan:
        if coded:
            out_shape.append(jax.ShapeDtypeStruct((size, (words + 1) * block), jnp.int32))
        else:
            out_shape.append(jax.ShapeDtypeStruct((size, width), jnp.float32))
    return pl.pallas_call(
        functools.partial(products_kernel, plan, group, slots, block, words),
        out_shape=out_shape,
        in_specs=[pl.BlockSpec(memory_space=pltpu.SMEM)]
        + [anywhere] * len(sources)
        + [pl.BlockSpec(memory_space=pltpu.HBM)],
        out_specs=[pl.BlockSpec(memory_space=pltpu.VMEM)] * len(plan),
        scratch_shapes=[
            pltpu.VMEM((states, 2 * reach + width + block), parts[0][1].dtype),
            pltpu.VMEM(blocks.shape, blocks.dtype),
            pltpu.SemaphoreType.DMA((3 * states // 16,)),
            pltpu.SemaphoreType.DMA((rows // 2,)),
        ],
        compiler_params=pltpu.CompilerParams(vmem_limit_bytes=VMEM_LIMIT),
        cost_estimate=pl.CostEstimate(flops=1, bytes_accessed=1, transcendentals=0),
        name="products",
    )(index, *sources, pltpu.with_memory_space_constraint(blocks, pltpu.HBM))


def finish_kernel(partials, block, pairs, own_ref, *refs):
    out_ref = refs[-1]
    step = pl.program_id(0)
    lane = lax.broadcasted_iota(jnp.int32, (own_ref.shape[0], block), 1)
    levels = [level_of(refs[2 * p + 1][...]) * (1.0 / TOP) for p in range(partials)]
    for pair in range(pairs):
        for half in range(2):
            at = (2 * pair + half) * block
            row = (step * pairs + pair) * 2 + half
            total = own_ref[:, at : at + block]
            for p in range(partials):
                word = refs[2 * p][:, pair * block : (pair + 1) * block]
                value = (word >> 16) if half else ((word << 16) >> 16)
                level = jnp.max(jnp.where(lane == row, levels[p], 0.0), axis=1, keepdims=True)
                total = total + value.astype(jnp.float32) * level
            out_ref[:, at : at + block] = total.astype(out_ref.dtype)


def finish(own_sums, own_start, coded, coded_start, out, start, size, states, block):
    width = own_sums.shape[1]
    words = width // block // 2
    pairs = words // 2 if words % 2 == 0 else 1
    rows, wide, narrow = pl.Element(size), pl.Element(2 * pairs * block), pl.Element(pairs * block)
    own_at, coded_at = start - own_start, start - coded_start
    in_specs = [pl.BlockSpec((rows, wide), lambda i: (own_at, i * 2 * pairs * block))]
    operands = [own_sums]
    for array in coded:
        in_specs.append(pl.BlockSpec((rows, narrow), lambda i: (coded_at, i * pairs * block)))
        in_specs.append(pl.BlockSpec((rows, pl.Element(block)), lambda i: (coded_at, words * block)))
        operands += [array, array]
    aliases = {}
    if out is not None:
        aliases = {len(operands): 0}
        in_specs.append(pl.BlockSpec(memory_space=pl.ANY))
        operands.append(out)
    return pl.pallas_call(
        functools.partial(finish_kernel, len(coded), block, pairs),
        out_shape=jax.ShapeDtypeStruct((states, width), jnp.bfloat16),
        grid=(words // pairs,),
        in_specs=in_specs,
        out_specs=pl.BlockSpec((rows, wide), lambda i: (start, i * 2 * pairs * block)),
        input_output_aliases=aliases,
        compiler_params=pltpu.CompilerParams(vmem_limit_bytes=VMEM_LIMIT),
        cost_estimate=pl.CostEstimate(flops=1, bytes_accessed=1, transcendentals=0),
        name="finish",
    )(*operands)


def starts_of(sizes):
    return [sum(sizes[:i]) for i in range(len(sizes))]


def on_device(vectors, blocks, columns, counts):
    states, width = vectors.shape
    rows, slots, block, _ = blocks.shape
    reach = W * block
    basis_size, state_size = lax.axis_size("basis"), lax.axis_size("state")
    if states % 256 == 0:
        sizes = (5 * states // 16, 3 * states // 8, 5 * states // 16)
        own_sizes = (7 * states // 16, 9 * states // 16)
    else:
        sizes, own_sizes = (states,), (states,)
    starts, own_starts = starts_of(sizes), starts_of(own_sizes)

    slot_index = lax.axis_index("state") * slots + jnp.arange(slots, dtype=jnp.int32)
    relative = columns - (lax.axis_index("basis") * rows - W)
    zeros_at = rows + 2 * W
    index = jnp.where(slot_index[None, :] < counts[:, None], relative, zeros_at).reshape(-1)

    up = [(i, i + 1) for i in range(basis_size - 1)]
    down = [(i + 1, i) for i in range(basis_size - 1)]

    def edges_of(piece, *others):
        edges = (piece[:, width - reach :], piece[:, :reach])
        return lax.optimization_barrier((*edges, *others))[:2] if others else edges

    def halo(edges):
        return lax.ppermute(edges[0], "basis", up), lax.ppermute(edges[1], "basis", down)

    def shifted(piece, shift):
        return lax.ppermute(piece, "state", [(i, (i + shift) % state_size) for i in range(state_size)])

    def own_edges(part, *others):
        return edges_of(vectors[own_starts[part] : own_starts[part] + own_sizes[part]], *others)

    def own_part(part, ends):
        return (ends[0], vectors, ends[1], own_starts[part], own_sizes[part], False)

    def their_part(n):
        return (ends[n][0], theirs[n], ends[n][1], 0, theirs[n].shape[0], True)

    messages = [(shift, c) for shift in range(1, state_size) for c in range(len(sizes))]
    count = len(messages)
    theirs, edges, ends, sent, own_sums, received = [], [], [], [], [], []
    first_edges = own_edges(0)
    first = halo(first_edges)
    for n, (shift, c) in enumerate(messages):
        source = after(vectors, *(first_edges if n == 1 else first)) if n else vectors
        theirs.append(shifted(source[starts[c] : starts[c] + sizes[c]], shift))

    def compute(n):
        later = edges[n + 1] if n + 1 < count else ()
        if n == min(1, count - 1):
            own_sums.extend(products(after(index, *later) if later else index, [own_part(0, first)], blocks))
            later = (*later, own_sums[0])
        sent.extend(products(after(index, *later) if later else index, [their_part(n)], blocks))

    for n in range(count):
        edges.append(edges_of(theirs[n]))
        ends.append(halo(edges[n]))
        if n:
            compute(n - 1)
    if len(own_sizes) > 1:
        last = halo(own_edges(1, *edges[-1], *sent[-1:]))
    compute(count - 1)
    coded = [[] for _ in sizes]
    for n, (shift, c) in enumerate(messages):
        message = after(sent[n], received[n - 1]) if n else sent[n]
        received.append(shifted(message, -shift))
        coded[c].append(received[n])
    out = None
    for part, own_size in enumerate(own_sizes):
        if part:
            own_sums += products(after(index, out), [own_part(part, last)], blocks)
        for c, size in enumerate(sizes):
            at = max(own_starts[part], starts[c])
            end = min(own_starts[part] + own_size, starts[c] + size)
            if at < end:
                out = finish(
                    own_sums[part], own_starts[part], coded[c], starts[c], out, at, end - at, states, block
                )
    return out


def solution(mesh):
    in_specs = (
        P("state", "basis"),
        P("basis", "state", None, None),
        P("basis", "state"),
        P("basis"),
    )
    out_specs = P("state", "basis")
    return jax.shard_map(
        on_device, mesh=mesh, in_specs=in_specs, out_specs=out_specs, check_vma=False
    )
```

```python
import functools
import math

import jax
import jax.numpy as jnp
from jax import lax
from jax.experimental import pallas as pl
from jax.experimental.pallas import tpu as pltpu
from jax.sharding import PartitionSpec as P

W = 36
VMEM_LIMIT = 32 * 1024 * 1024
TOP = 32767.0
FINE = 65536.0
SMALLEST = 2.0**-100


def after(array, *others):
    return lax.optimization_barrier((array, *others))[0]


def fill(sources, plan, ext):
    at, step = 0, 16
    for part, (start, size, _) in enumerate(plan):
        left, own, right = sources[3 * part : 3 * part + 3]
        reach, width = left.shape[1], own.shape[1]

        @pl.loop(0, size // step)
        def _(i, left=left, own=own, right=right, start=start, at=at, reach=reach, width=width):
            here = pl.ds(pl.multiple_of(i * step, step), step)
            mine = pl.ds(pl.multiple_of(start + i * step, step), step)
            to = pl.ds(pl.multiple_of(at + i * step, step), step)
            ext[to, :reach] = left[here, :]
            ext[to, reach : reach + width] = own[mine, :]
            ext[to, reach + width : 2 * reach + width] = right[here, :]

        at += size


def row_sums(index_ref, row, slots, block, ext, panel_ref):
    picked = jnp.concatenate(
        [
            ext[:, pl.ds(pl.multiple_of(index_ref[row * slots + slot] * block, block), block)]
            for slot in range(slots)
        ],
        axis=1,
    )
    panel = jnp.concatenate([panel_ref[slot] for slot in range(slots)], axis=1)
    return lax.dot_general(
        picked, panel, (((1,), (1,)), ((), ())), preferred_element_type=jnp.float32
    )


def level_code(top):
    return jnp.ceil(jnp.log2(jnp.maximum(top, SMALLEST)) * FINE).astype(jnp.int32)


def level_of(code):
    return jnp.exp2(code.astype(jnp.float32) * (1.0 / FINE))


def code_into(out_ref, first, block, words, sums):
    lane = lax.broadcasted_iota(jnp.int32, (out_ref.shape[0], block), 1)
    codes = out_ref[:, words * block :]
    values = []
    for member, mine in enumerate(sums):
        code = level_code(jnp.max(jnp.abs(mine), axis=1, keepdims=True))
        codes = jnp.where(lane == first + member, code, codes)
        scaled = jnp.round(mine * (TOP / level_of(code)))
        values.append(jnp.clip(scaled, -TOP, TOP).astype(jnp.int32))
    out_ref[:, words * block :] = codes
    for pair in range(len(sums) // 2):
        word = (values[2 * pair + 1] << 16) | (values[2 * pair] & 0xFFFF)
        at = pl.multiple_of((first // 2 + pair) * block, block)
        out_ref[:, pl.ds(at, block)] = word


def products_kernel(plan, group, slots, block, words, index_ref, *refs):
    parts = len(plan)
    sources, blocks_ref = refs[: 3 * parts], refs[3 * parts]
    outs, (ext, panels, panel_sems) = refs[3 * parts + 1 : 4 * parts + 1], refs[4 * parts + 1 :]
    rows, pieces = panels.shape[0], panel_sems.shape[0]
    piece = rows // pieces

    def panel_copy(n):
        here = pl.ds(n * piece, piece)
        return pltpu.make_async_copy(blocks_ref.at[here], panels.at[here], panel_sems.at[n])

    for n in range(pieces):
        panel_copy(n).start()
    fill(sources, plan, ext)
    end = ext.shape[1] - block
    ext[:, end:] = jnp.zeros((ext.shape[0], block), ext.dtype)
    for (_, size, coded), out_ref in zip(plan, outs):
        if coded:
            out_ref[:, words * block :] = jnp.zeros((size, block), jnp.int32)

    @pl.loop(0, rows // group)
    def _(step):
        for n in range(group // piece):
            panel_copy(step * (group // piece) + n).wait()
        first = step * group
        sums = [
            row_sums(index_ref, first + member, slots, block, ext, panels.at[first + member])
            for member in range(group)
        ]
        at = 0
        for (_, size, coded), out_ref in zip(plan, outs):
            mine = [total[at : at + size] for total in sums]
            if coded:
                code_into(out_ref, first, block, words, mine)
            else:
                for member in range(group):
                    column = pl.multiple_of((first + member) * block, block)
                    out_ref[:, pl.ds(column, block)] = mine[member]
            at += size


def products(index, parts, blocks):
    rows, slots, block, _ = blocks.shape
    reach, width = parts[0][0].shape[1], parts[0][1].shape[1]
    plan = tuple(part[3:] for part in parts)
    states = sum(size for _, size, _ in plan)
    group, words = 8 if rows % 8 == 0 else 2, rows // 2
    sources = [array for part in parts for array in part[:3]]
    in_vmem = pl.BlockSpec(memory_space=pltpu.VMEM)
    out_shape = []
    for _, size, coded in plan:
        if coded:
            out_shape.append(jax.ShapeDtypeStruct((size, (words + 1) * block), jnp.int32))
        else:
            out_shape.append(jax.ShapeDtypeStruct((size, width), jnp.float32))
    return pl.pallas_call(
        functools.partial(products_kernel, plan, group, slots, block, words),
        out_shape=out_shape,
        in_specs=[pl.BlockSpec(memory_space=pltpu.SMEM)]
        + [in_vmem] * len(sources)
        + [pl.BlockSpec(memory_space=pltpu.HBM)],
        out_specs=[in_vmem] * len(plan),
        scratch_shapes=[
            pltpu.VMEM((states, 2 * reach + width + block), parts[0][1].dtype),
            pltpu.VMEM(blocks.shape, blocks.dtype),
            pltpu.SemaphoreType.DMA((rows // 2,)),
        ],
        compiler_params=pltpu.CompilerParams(vmem_limit_bytes=VMEM_LIMIT),
        cost_estimate=pl.CostEstimate(flops=1, bytes_accessed=1, transcendentals=0),
        name="products",
    )(index, *sources, pltpu.with_memory_space_constraint(blocks, pltpu.HBM))


def finish_kernel(partials, block, pairs, own_ref, *refs):
    out_ref = refs[-1]
    step = pl.program_id(0)
    lane = lax.broadcasted_iota(jnp.int32, (own_ref.shape[0], block), 1)
    levels = [level_of(refs[2 * p + 1][...]) * (1.0 / TOP) for p in range(partials)]
    for pair in range(pairs):
        for half in range(2):
            at = (2 * pair + half) * block
            row = (step * pairs + pair) * 2 + half
            total = own_ref[:, at : at + block]
            for p in range(partials):
                word = refs[2 * p][:, pair * block : (pair + 1) * block]
                value = (word >> 16) if half else ((word << 16) >> 16)
                level = jnp.max(jnp.where(lane == row, levels[p], 0.0), axis=1, keepdims=True)
                total = total + value.astype(jnp.float32) * level
            out_ref[:, at : at + block] = total.astype(out_ref.dtype)


def finish(own_sums, own_start, coded, coded_start, out, start, size, states, block):
    width = own_sums.shape[1]
    words = width // block // 2
    pairs = words // 2 if words % 2 == 0 else 1
    rows, wide, narrow = pl.Element(size), pl.Element(2 * pairs * block), pl.Element(pairs * block)
    own_at, coded_at = start - own_start, start - coded_start
    in_specs = [pl.BlockSpec((rows, wide), lambda i: (own_at, i * 2 * pairs * block))]
    operands = [own_sums]
    for array in coded:
        in_specs.append(pl.BlockSpec((rows, narrow), lambda i: (coded_at, i * pairs * block)))
        in_specs.append(pl.BlockSpec((rows, pl.Element(block)), lambda i: (coded_at, words * block)))
        operands += [array, array]
    aliases = {}
    if out is not None:
        aliases = {len(operands): 0}
        in_specs.append(pl.BlockSpec(memory_space=pl.ANY))
        operands.append(out)
    return pl.pallas_call(
        functools.partial(finish_kernel, len(coded), block, pairs),
        out_shape=jax.ShapeDtypeStruct((states, width), jnp.bfloat16),
        grid=(words // pairs,),
        in_specs=in_specs,
        out_specs=pl.BlockSpec((rows, wide), lambda i: (start, i * 2 * pairs * block)),
        input_output_aliases=aliases,
        compiler_params=pltpu.CompilerParams(vmem_limit_bytes=VMEM_LIMIT),
        cost_estimate=pl.CostEstimate(flops=1, bytes_accessed=1, transcendentals=0),
        name="finish",
    )(*operands)


def starts_of(sizes):
    return [sum(sizes[:i]) for i in range(len(sizes))]


def on_device(vectors, blocks, columns, counts):
    states, width = vectors.shape
    rows, slots, block, _ = blocks.shape
    reach = W * block
    basis_size, state_size = lax.axis_size("basis"), lax.axis_size("state")
    if states % 256 == 0:
        sizes = (5 * states // 16, 3 * states // 8, 5 * states // 16)
        own_sizes = (7 * states // 16, 9 * states // 16)
    else:
        sizes, own_sizes = (states,), (states,)
    starts, own_starts = starts_of(sizes), starts_of(own_sizes)

    slot_index = lax.axis_index("state") * slots + jnp.arange(slots, dtype=jnp.int32)
    relative = columns - (lax.axis_index("basis") * rows - W)
    zeros_at = rows + 2 * W
    index = jnp.where(slot_index[None, :] < counts[:, None], relative, zeros_at).reshape(-1)

    up = [(i, i + 1) for i in range(basis_size - 1)]
    down = [(i + 1, i) for i in range(basis_size - 1)]

    def edges_of(piece, *others):
        edges = (piece[:, width - reach :], piece[:, :reach])
        return lax.optimization_barrier((*edges, *others))[:2] if others else edges

    def halo(edges):
        return lax.ppermute(edges[0], "basis", up), lax.ppermute(edges[1], "basis", down)

    def shifted(piece, shift):
        return lax.ppermute(piece, "state", [(i, (i + shift) % state_size) for i in range(state_size)])

    def own_edges(part, *others):
        return edges_of(vectors[own_starts[part] : own_starts[part] + own_sizes[part]], *others)

    def own_part(part, ends):
        return (ends[0], vectors, ends[1], own_starts[part], own_sizes[part], False)

    def their_part(n):
        return (ends[n][0], theirs[n], ends[n][1], 0, theirs[n].shape[0], True)

    messages = [(shift, c) for shift in range(1, state_size) for c in range(len(sizes))]
    count = len(messages)
    theirs, edges, ends, sent, own_sums, received = [], [], [], [], [], []
    first_edges = own_edges(0)
    first = halo(first_edges)
    for n, (shift, c) in enumerate(messages):
        source = after(vectors, *(first_edges if n == 1 else first)) if n else vectors
        theirs.append(shifted(source[starts[c] : starts[c] + sizes[c]], shift))

    def compute(n):
        later = edges[n + 1] if n + 1 < count else ()
        if n == min(1, count - 1):
            own_sums.extend(products(after(index, *later) if later else index, [own_part(0, first)], blocks))
            later = (*later, own_sums[0])
        sent.extend(products(after(index, *later) if later else index, [their_part(n)], blocks))

    for n in range(count):
        edges.append(edges_of(theirs[n]))
        ends.append(halo(edges[n]))
        if n:
            compute(n - 1)
    if len(own_sizes) > 1:
        last = halo(own_edges(1, *edges[-1], *sent[-1:]))
    compute(count - 1)
    coded = [[] for _ in sizes]
    for n, (shift, c) in enumerate(messages):
        message = after(sent[n], received[n - 1]) if n else sent[n]
        received.append(shifted(message, -shift))
        coded[c].append(received[n])
    out = None
    for part, own_size in enumerate(own_sizes):
        if part:
            own_sums += products(after(index, out), [own_part(part, last)], blocks)
        for c, size in enumerate(sizes):
            at = max(own_starts[part], starts[c])
            end = min(own_starts[part] + own_size, starts[c] + size)
            if at < end:
                out = finish(
                    own_sums[part], own_starts[part], coded[c], starts[c], out, at, end - at, states, block
                )
    return out


def solution(mesh):
    in_specs = (
        P("state", "basis"),
        P("basis", "state", None, None),
        P("basis", "state"),
        P("basis"),
    )
    out_specs = P("state", "basis")
    return jax.shard_map(
        on_device, mesh=mesh, in_specs=in_specs, out_specs=out_specs, check_vma=False
    )
```

```python
import functools
import math

import jax
import jax.numpy as jnp
from jax import lax
from jax.experimental import pallas as pl
from jax.experimental.pallas import tpu as pltpu
from jax.sharding import PartitionSpec as P

W = 36
VMEM_LIMIT = 32 * 1024 * 1024
TOP = 32767.0
FINE = 65536.0
SMALLEST = 2.0**-100


def after(array, *others):
    return lax.optimization_barrier((array, *others))[0]


def fill(sources, plan, ext):
    at, step = 0, 16
    for part, (start, size, _) in enumerate(plan):
        left, own, right = sources[3 * part : 3 * part + 3]
        reach, width = left.shape[1], own.shape[1]

        @pl.loop(0, size // step)
        def _(i, left=left, own=own, right=right, start=start, at=at, reach=reach, width=width):
            here = pl.ds(pl.multiple_of(i * step, step), step)
            mine = pl.ds(pl.multiple_of(start + i * step, step), step)
            to = pl.ds(pl.multiple_of(at + i * step, step), step)
            ext[to, :reach] = left[here, :]
            ext[to, reach : reach + width] = own[mine, :]
            ext[to, reach + width : 2 * reach + width] = right[here, :]

        at += size


def row_sums(index_ref, row, slots, block, ext, panel_ref):
    picked = jnp.concatenate(
        [
            ext[:, pl.ds(pl.multiple_of(index_ref[row * slots + slot] * block, block), block)]
            for slot in range(slots)
        ],
        axis=1,
    )
    panel = jnp.concatenate([panel_ref[slot] for slot in range(slots)], axis=1)
    return lax.dot_general(
        picked, panel, (((1,), (1,)), ((), ())), preferred_element_type=jnp.float32
    )


def level_code(top):
    return jnp.ceil(jnp.log2(jnp.maximum(top, SMALLEST)) * FINE).astype(jnp.int32)


def level_of(code):
    return jnp.exp2(code.astype(jnp.float32) * (1.0 / FINE))


def code_into(out_ref, first, block, words, sums):
    lane = lax.broadcasted_iota(jnp.int32, (out_ref.shape[0], block), 1)
    codes = out_ref[:, words * block :]
    values = []
    for member, mine in enumerate(sums):
        code = level_code(jnp.max(jnp.abs(mine), axis=1, keepdims=True))
        codes = jnp.where(lane == first + member, code, codes)
        scaled = jnp.round(mine * (TOP / level_of(code)))
        values.append(jnp.clip(scaled, -TOP, TOP).astype(jnp.int32))
    out_ref[:, words * block :] = codes
    for pair in range(len(sums) // 2):
        word = (values[2 * pair + 1] << 16) | (values[2 * pair] & 0xFFFF)
        at = pl.multiple_of((first // 2 + pair) * block, block)
        out_ref[:, pl.ds(at, block)] = word


def products_kernel(plan, group, slots, block, words, index_ref, *refs):
    parts = len(plan)
    sources, blocks_ref = refs[: 3 * parts], refs[3 * parts]
    outs, (ext, panels, panel_sems) = refs[3 * parts + 1 : 4 * parts + 1], refs[4 * parts + 1 :]
    rows, pieces = panels.shape[0], panel_sems.shape[0]
    piece = rows // pieces

    def panel_copy(n):
        here = pl.ds(n * piece, piece)
        return pltpu.make_async_copy(blocks_ref.at[here], panels.at[here], panel_sems.at[n])

    for n in range(pieces):
        panel_copy(n).start()
    fill(sources, plan, ext)
    end = ext.shape[1] - block
    ext[:, end:] = jnp.zeros((ext.shape[0], block), ext.dtype)
    for (_, size, coded), out_ref in zip(plan, outs):
        if coded:
            out_ref[:, words * block :] = jnp.zeros((size, block), jnp.int32)

    @pl.loop(0, rows // group)
    def _(step):
        for n in range(group // piece):
            panel_copy(step * (group // piece) + n).wait()
        first = step * group
        sums = [
            row_sums(index_ref, first + member, slots, block, ext, panels.at[first + member])
            for member in range(group)
        ]
        at = 0
        for (_, size, coded), out_ref in zip(plan, outs):
            mine = [total[at : at + size] for total in sums]
            if coded:
                code_into(out_ref, first, block, words, mine)
            else:
                for member in range(group):
                    column = pl.multiple_of((first + member) * block, block)
                    out_ref[:, pl.ds(column, block)] = mine[member]
            at += size


def products(index, parts, blocks):
    rows, slots, block, _ = blocks.shape
    reach, width = parts[0][0].shape[1], parts[0][1].shape[1]
    plan = tuple(part[3:] for part in parts)
    states = sum(size for _, size, _ in plan)
    group, words = 8 if rows % 8 == 0 else 2, rows // 2
    sources = [array for part in parts for array in part[:3]]
    in_vmem = pl.BlockSpec(memory_space=pltpu.VMEM)
    out_shape = []
    for _, size, coded in plan:
        if coded:
            out_shape.append(jax.ShapeDtypeStruct((size, (words + 1) * block), jnp.int32))
        else:
            out_shape.append(jax.ShapeDtypeStruct((size, width), jnp.float32))
    return pl.pallas_call(
        functools.partial(products_kernel, plan, group, slots, block, words),
        out_shape=out_shape,
        in_specs=[pl.BlockSpec(memory_space=pltpu.SMEM)]
        + [in_vmem] * len(sources)
        + [pl.BlockSpec(memory_space=pltpu.HBM)],
        out_specs=[in_vmem] * len(plan),
        scratch_shapes=[
            pltpu.VMEM((states, 2 * reach + width + block), parts[0][1].dtype),
            pltpu.VMEM(blocks.shape, blocks.dtype),
            pltpu.SemaphoreType.DMA((rows // 2,)),
        ],
        compiler_params=pltpu.CompilerParams(vmem_limit_bytes=VMEM_LIMIT),
        cost_estimate=pl.CostEstimate(flops=1, bytes_accessed=1, transcendentals=0),
        name="products",
    )(index, *sources, pltpu.with_memory_space_constraint(blocks, pltpu.HBM))


def finish_kernel(partials, block, pairs, own_ref, *refs):
    out_ref = refs[-1]
    step = pl.program_id(0)
    lane = lax.broadcasted_iota(jnp.int32, (own_ref.shape[0], block), 1)
    levels = [level_of(refs[2 * p + 1][...]) * (1.0 / TOP) for p in range(partials)]
    for pair in range(pairs):
        for half in range(2):
            at = (2 * pair + half) * block
            row = (step * pairs + pair) * 2 + half
            total = own_ref[:, at : at + block]
            for p in range(partials):
                word = refs[2 * p][:, pair * block : (pair + 1) * block]
                value = (word >> 16) if half else ((word << 16) >> 16)
                level = jnp.max(jnp.where(lane == row, levels[p], 0.0), axis=1, keepdims=True)
                total = total + value.astype(jnp.float32) * level
            out_ref[:, at : at + block] = total.astype(out_ref.dtype)


def finish(own_sums, own_start, coded, coded_start, out, start, size, states, block):
    width = own_sums.shape[1]
    words = width // block // 2
    pairs = words // 2 if words % 2 == 0 else 1
    rows, wide, narrow = pl.Element(size), pl.Element(2 * pairs * block), pl.Element(pairs * block)
    own_at, coded_at = start - own_start, start - coded_start
    in_specs = [pl.BlockSpec((rows, wide), lambda i: (own_at, i * 2 * pairs * block))]
    operands = [own_sums]
    for array in coded:
        in_specs.append(pl.BlockSpec((rows, narrow), lambda i: (coded_at, i * pairs * block)))
        in_specs.append(pl.BlockSpec((rows, pl.Element(block)), lambda i: (coded_at, words * block)))
        operands += [array, array]
    aliases = {}
    if out is not None:
        aliases = {len(operands): 0}
        in_specs.append(pl.BlockSpec(memory_space=pl.ANY))
        operands.append(out)
    return pl.pallas_call(
        functools.partial(finish_kernel, len(coded), block, pairs),
        out_shape=jax.ShapeDtypeStruct((states, width), jnp.bfloat16),
        grid=(words // pairs,),
        in_specs=in_specs,
        out_specs=pl.BlockSpec((rows, wide), lambda i: (start, i * 2 * pairs * block)),
        input_output_aliases=aliases,
        compiler_params=pltpu.CompilerParams(vmem_limit_bytes=VMEM_LIMIT),
        cost_estimate=pl.CostEstimate(flops=1, bytes_accessed=1, transcendentals=0),
        name="finish",
    )(*operands)


def starts_of(sizes):
    return [sum(sizes[:i]) for i in range(len(sizes))]


def on_device(vectors, blocks, columns, counts):
    states, width = vectors.shape
    rows, slots, block, _ = blocks.shape
    reach = W * block
    basis_size, state_size = lax.axis_size("basis"), lax.axis_size("state")
    if states % 256 == 0:
        sizes = (5 * states // 16, 3 * states // 8, 5 * states // 16)
        own_sizes = (7 * states // 16, 9 * states // 16)
    else:
        sizes, own_sizes = (states,), (states,)
    starts, own_starts = starts_of(sizes), starts_of(own_sizes)

    slot_index = lax.axis_index("state") * slots + jnp.arange(slots, dtype=jnp.int32)
    relative = columns - (lax.axis_index("basis") * rows - W)
    zeros_at = rows + 2 * W
    index = jnp.where(slot_index[None, :] < counts[:, None], relative, zeros_at).reshape(-1)

    up = [(i, i + 1) for i in range(basis_size - 1)]
    down = [(i + 1, i) for i in range(basis_size - 1)]

    def edges_of(piece, *others):
        edges = (piece[:, width - reach :], piece[:, :reach])
        return lax.optimization_barrier((*edges, *others))[:2] if others else edges

    def halo(edges):
        return lax.ppermute(edges[0], "basis", up), lax.ppermute(edges[1], "basis", down)

    def shifted(piece, shift):
        return lax.ppermute(piece, "state", [(i, (i + shift) % state_size) for i in range(state_size)])

    def own_edges(part, *others):
        return edges_of(vectors[own_starts[part] : own_starts[part] + own_sizes[part]], *others)

    def own_part(part, ends):
        return (ends[0], vectors, ends[1], own_starts[part], own_sizes[part], False)

    def their_part(n):
        return (ends[n][0], theirs[n], ends[n][1], 0, theirs[n].shape[0], True)

    messages = [(shift, c) for shift in range(1, state_size) for c in range(len(sizes))]
    count = len(messages)
    theirs, edges, ends, sent, own_sums, received = [], [], [], [], [], []
    first_edges = own_edges(0)
    first = halo(first_edges)
    for n, (shift, c) in enumerate(messages):
        source = after(vectors, *(first_edges if n == 1 else first)) if n else vectors
        theirs.append(shifted(source[starts[c] : starts[c] + sizes[c]], shift))

    def compute(n):
        later = edges[n + 1] if n + 1 < count else ()
        sent.extend(products(after(index, *later) if later else index, [their_part(n)], blocks))
        if n == 0:
            own_sums.extend(products(after(index, sent[0]), [own_part(0, first)], blocks))

    for n in range(count):
        edges.append(edges_of(theirs[n], *(own_sums if n > 1 else ())))
        ends.append(halo(edges[n]))
        if n:
            compute(n - 1)
    if len(own_sizes) > 1:
        last = halo(own_edges(1, *edges[-1], *sent[-1:]))
    compute(count - 1)
    coded = [[] for _ in sizes]
    for n, (shift, c) in enumerate(messages):
        message = after(sent[n], received[n - 1]) if n else sent[n]
        received.append(shifted(message, -shift))
        coded[c].append(received[n])
    out = None
    for part, own_size in enumerate(own_sizes):
        if part:
            own_sums += products(after(index, out), [own_part(part, last)], blocks)
        for c, size in enumerate(sizes):
            at = max(own_starts[part], starts[c])
            end = min(own_starts[part] + own_size, starts[c] + size)
            if at < end:
                out = finish(
                    own_sums[part], own_starts[part], coded[c], starts[c], out, at, end - at, states, block
                )
    return out


def solution(mesh):
    in_specs = (
        P("state", "basis"),
        P("basis", "state", None, None),
        P("basis", "state"),
        P("basis"),
    )
    out_specs = P("state", "basis")
    return jax.shard_map(
        on_device, mesh=mesh, in_specs=in_specs, out_specs=out_specs, check_vma=False
    )
```

```python
import functools
import math

import jax
import jax.numpy as jnp
from jax import lax
from jax.experimental import pallas as pl
from jax.experimental.pallas import tpu as pltpu
from jax.sharding import PartitionSpec as P

W = 36
VMEM_LIMIT = 32 * 1024 * 1024
TOP = 32767.0
FINE = 65536.0
SMALLEST = 2.0**-100


def after(array, *others):
    return lax.optimization_barrier((array, *others))[0]


def fill(sources, plan, ext):
    at, step = 0, 16
    for part, (start, size, _) in enumerate(plan):
        left, own, right = sources[3 * part : 3 * part + 3]
        reach, width = left.shape[1], own.shape[1]

        @pl.loop(0, size // step)
        def _(i, left=left, own=own, right=right, start=start, at=at, reach=reach, width=width):
            here = pl.ds(pl.multiple_of(i * step, step), step)
            mine = pl.ds(pl.multiple_of(start + i * step, step), step)
            to = pl.ds(pl.multiple_of(at + i * step, step), step)
            ext[to, :reach] = left[here, :]
            ext[to, reach : reach + width] = own[mine, :]
            ext[to, reach + width : 2 * reach + width] = right[here, :]

        at += size


def row_sums(index_ref, row, slots, block, ext, panel_ref):
    picked = jnp.concatenate(
        [
            ext[:, pl.ds(pl.multiple_of(index_ref[row * slots + slot] * block, block), block)]
            for slot in range(slots)
        ],
        axis=1,
    )
    panel = jnp.concatenate([panel_ref[slot] for slot in range(slots)], axis=1)
    return lax.dot_general(
        picked, panel, (((1,), (1,)), ((), ())), preferred_element_type=jnp.float32
    )


def level_code(top):
    return jnp.ceil(jnp.log2(jnp.maximum(top, SMALLEST)) * FINE).astype(jnp.int32)


def level_of(code):
    return jnp.exp2(code.astype(jnp.float32) * (1.0 / FINE))


def code_into(out_ref, first, block, words, sums):
    lane = lax.broadcasted_iota(jnp.int32, (out_ref.shape[0], block), 1)
    codes = out_ref[:, words * block :]
    values = []
    for member, mine in enumerate(sums):
        code = level_code(jnp.max(jnp.abs(mine), axis=1, keepdims=True))
        codes = jnp.where(lane == first + member, code, codes)
        scaled = jnp.round(mine * (TOP / level_of(code)))
        values.append(jnp.clip(scaled, -TOP, TOP).astype(jnp.int32))
    out_ref[:, words * block :] = codes
    for pair in range(len(sums) // 2):
        word = (values[2 * pair + 1] << 16) | (values[2 * pair] & 0xFFFF)
        at = pl.multiple_of((first // 2 + pair) * block, block)
        out_ref[:, pl.ds(at, block)] = word


def products_kernel(plan, group, slots, block, words, index_ref, *refs):
    parts = len(plan)
    sources, blocks_ref = refs[: 3 * parts], refs[3 * parts]
    outs, (ext, panels, panel_sems) = refs[3 * parts + 1 : 4 * parts + 1], refs[4 * parts + 1 :]
    rows, pieces = panels.shape[0], panel_sems.shape[0]
    piece = rows // pieces

    def panel_copy(n):
        here = pl.ds(n * piece, piece)
        return pltpu.make_async_copy(blocks_ref.at[here], panels.at[here], panel_sems.at[n])

    for n in range(pieces):
        panel_copy(n).start()
    fill(sources, plan, ext)
    end = ext.shape[1] - block
    ext[:, end:] = jnp.zeros((ext.shape[0], block), ext.dtype)
    for (_, size, coded), out_ref in zip(plan, outs):
        if coded:
            out_ref[:, words * block :] = jnp.zeros((size, block), jnp.int32)

    @pl.loop(0, rows // group)
    def _(step):
        for n in range(group // piece):
            panel_copy(step * (group // piece) + n).wait()
        first = step * group
        sums = [
            row_sums(index_ref, first + member, slots, block, ext, panels.at[first + member])
            for member in range(group)
        ]
        at = 0
        for (_, size, coded), out_ref in zip(plan, outs):
            mine = [total[at : at + size] for total in sums]
            if coded:
                code_into(out_ref, first, block, words, mine)
            else:
                for member in range(group):
                    column = pl.multiple_of((first + member) * block, block)
                    out_ref[:, pl.ds(column, block)] = mine[member]
            at += size


def products(index, parts, blocks):
    rows, slots, block, _ = blocks.shape
    reach, width = parts[0][0].shape[1], parts[0][1].shape[1]
    plan = tuple(part[3:] for part in parts)
    states = sum(size for _, size, _ in plan)
    group, words = 8 if rows % 8 == 0 else 2, rows // 2
    sources = [array for part in parts for array in part[:3]]
    in_vmem = pl.BlockSpec(memory_space=pltpu.VMEM)
    out_shape = []
    for _, size, coded in plan:
        if coded:
            out_shape.append(jax.ShapeDtypeStruct((size, (words + 1) * block), jnp.int32))
        else:
            out_shape.append(jax.ShapeDtypeStruct((size, width), jnp.float32))
    return pl.pallas_call(
        functools.partial(products_kernel, plan, group, slots, block, words),
        out_shape=out_shape,
        in_specs=[pl.BlockSpec(memory_space=pltpu.SMEM)]
        + [in_vmem] * len(sources)
        + [pl.BlockSpec(memory_space=pltpu.HBM)],
        out_specs=[in_vmem] * len(plan),
        scratch_shapes=[
            pltpu.VMEM((states, 2 * reach + width + block), parts[0][1].dtype),
            pltpu.VMEM(blocks.shape, blocks.dtype),
            pltpu.SemaphoreType.DMA((rows // 2,)),
        ],
        compiler_params=pltpu.CompilerParams(vmem_limit_bytes=VMEM_LIMIT),
        cost_estimate=pl.CostEstimate(flops=1, bytes_accessed=1, transcendentals=0),
        name="products",
    )(index, *sources, pltpu.with_memory_space_constraint(blocks, pltpu.HBM))


def finish_kernel(partials, block, pairs, own_ref, *refs):
    out_ref = refs[-1]
    step = pl.program_id(0)
    lane = lax.broadcasted_iota(jnp.int32, (own_ref.shape[0], block), 1)
    levels = [level_of(refs[2 * p + 1][...]) * (1.0 / TOP) for p in range(partials)]
    for pair in range(pairs):
        for half in range(2):
            at = (2 * pair + half) * block
            row = (step * pairs + pair) * 2 + half
            total = own_ref[:, at : at + block]
            for p in range(partials):
                word = refs[2 * p][:, pair * block : (pair + 1) * block]
                value = (word >> 16) if half else ((word << 16) >> 16)
                level = jnp.max(jnp.where(lane == row, levels[p], 0.0), axis=1, keepdims=True)
                total = total + value.astype(jnp.float32) * level
            out_ref[:, at : at + block] = total.astype(out_ref.dtype)


def finish(own_sums, own_start, coded, coded_start, out, start, size, states, block):
    width = own_sums.shape[1]
    words = width // block // 2
    pairs = words // 2 if words % 2 == 0 else 1
    rows, wide, narrow = pl.Element(size), pl.Element(2 * pairs * block), pl.Element(pairs * block)
    own_at, coded_at = start - own_start, start - coded_start
    in_specs = [pl.BlockSpec((rows, wide), lambda i: (own_at, i * 2 * pairs * block))]
    operands = [own_sums]
    for array in coded:
        in_specs.append(pl.BlockSpec((rows, narrow), lambda i: (coded_at, i * pairs * block)))
        in_specs.append(pl.BlockSpec((rows, pl.Element(block)), lambda i: (coded_at, words * block)))
        operands += [array, array]
    aliases = {}
    if out is not None:
        aliases = {len(operands): 0}
        in_specs.append(pl.BlockSpec(memory_space=pl.ANY))
        operands.append(out)
    return pl.pallas_call(
        functools.partial(finish_kernel, len(coded), block, pairs),
        out_shape=jax.ShapeDtypeStruct((states, width), jnp.bfloat16),
        grid=(words // pairs,),
        in_specs=in_specs,
        out_specs=pl.BlockSpec((rows, wide), lambda i: (start, i * 2 * pairs * block)),
        input_output_aliases=aliases,
        compiler_params=pltpu.CompilerParams(vmem_limit_bytes=VMEM_LIMIT),
        cost_estimate=pl.CostEstimate(flops=1, bytes_accessed=1, transcendentals=0),
        name="finish",
    )(*operands)


def starts_of(sizes):
    return [sum(sizes[:i]) for i in range(len(sizes))]


def on_device(vectors, blocks, columns, counts):
    states, width = vectors.shape
    rows, slots, block, _ = blocks.shape
    reach = W * block
    basis_size, state_size = lax.axis_size("basis"), lax.axis_size("state")
    if states % 256 == 0:
        sizes = (5 * states // 16, 3 * states // 8, 5 * states // 16)
        own_sizes = (7 * states // 16, 9 * states // 16)
    else:
        sizes, own_sizes = (states,), (states,)
    starts, own_starts = starts_of(sizes), starts_of(own_sizes)

    slot_index = lax.axis_index("state") * slots + jnp.arange(slots, dtype=jnp.int32)
    relative = columns - (lax.axis_index("basis") * rows - W)
    zeros_at = rows + 2 * W
    index = jnp.where(slot_index[None, :] < counts[:, None], relative, zeros_at).reshape(-1)

    up = [(i, i + 1) for i in range(basis_size - 1)]
    down = [(i + 1, i) for i in range(basis_size - 1)]

    def edges_of(piece, *others):
        edges = (piece[:, width - reach :], piece[:, :reach])
        return lax.optimization_barrier((*edges, *others))[:2] if others else edges

    def halo(edges):
        return lax.ppermute(edges[0], "basis", up), lax.ppermute(edges[1], "basis", down)

    def shifted(piece, shift):
        return lax.ppermute(piece, "state", [(i, (i + shift) % state_size) for i in range(state_size)])

    def own_edges(part, *others):
        return edges_of(vectors[own_starts[part] : own_starts[part] + own_sizes[part]], *others)

    def own_part(part, ends):
        return (ends[0], vectors, ends[1], own_starts[part], own_sizes[part], False)

    def their_part(n):
        return (ends[n][0], theirs[n], ends[n][1], 0, theirs[n].shape[0], True)

    messages = [(shift, c) for shift in range(1, state_size) for c in range(len(sizes))]
    count = len(messages)
    theirs, edges, ends, sent, own_sums, received = [], [], [], [], [], []
    first_edges = own_edges(0)
    first = halo(first_edges)
    for n, (shift, c) in enumerate(messages):
        source = after(vectors, *(first_edges if n == 1 else first)) if n else vectors
        theirs.append(shifted(source[starts[c] : starts[c] + sizes[c]], shift))

    def compute(n):
        later = edges[n + 1] if n + 1 < count else ()
        sent.extend(products(after(index, *later) if later else index, [their_part(n)], blocks))
        if n == 0:
            own_sums.extend(products(after(index, sent[0]), [own_part(0, first)], blocks))

    for n in range(count):
        edges.append(edges_of(theirs[n], *(own_sums if n > 1 else ())))
        ends.append(halo(edges[n]))
        if n:
            compute(n - 1)
    coded = [[] for _ in sizes]

    def send(n):
        shift, c = messages[n]
        message = after(sent[n], received[n - 1]) if n else sent[n]
        received.append(shifted(message, -shift))
        coded[c].append(received[n])

    def finish_piece(part, c, out):
        own_end, end = own_starts[part] + own_sizes[part], starts[c] + sizes[c]
        at, end = max(own_starts[part], starts[c]), min(own_end, end)
        if at >= end:
            return out
        return finish(
            own_sums[part], own_starts[part], coded[c], starts[c], out, at, end - at, states, block
        )

    out, done = None, set()
    if len(own_sizes) > 1:
        send(0)
        if state_size == 2:
            out = finish_piece(0, 0, out)
            done.add((0, 0))
        held = (out,) if done else ()
        last = halo(own_edges(1, *edges[-1], *sent[-1:], *held))
    compute(count - 1)
    for n in range(len(received), count):
        send(n)
    for part in range(len(own_sizes)):
        if part:
            own_sums += products(after(index, out), [own_part(part, last)], blocks)
        for c in range(len(sizes)):
            if (part, c) not in done:
                out = finish_piece(part, c, out)
    return out


def solution(mesh):
    in_specs = (
        P("state", "basis"),
        P("basis", "state", None, None),
        P("basis", "state"),
        P("basis"),
    )
    out_specs = P("state", "basis")
    return jax.shard_map(
        on_device, mesh=mesh, in_specs=in_specs, out_specs=out_specs, check_vma=False
    )
```

```python
import functools
import math

import jax
import jax.numpy as jnp
from jax import lax
from jax.experimental import pallas as pl
from jax.experimental.pallas import tpu as pltpu
from jax.sharding import PartitionSpec as P

W = 36
VMEM_LIMIT = 32 * 1024 * 1024
TOP = 32767.0
FINE = 65536.0
SMALLEST = 2.0**-100


def after(array, *others):
    return lax.optimization_barrier((array, *others))[0]


def fill(sources, plan, ext):
    at, step = 0, 16
    for part, (start, size, _) in enumerate(plan):
        left, own, right = sources[3 * part : 3 * part + 3]
        reach, width = left.shape[1], own.shape[1]

        @pl.loop(0, size // step)
        def _(i, left=left, own=own, right=right, start=start, at=at, reach=reach, width=width):
            here = pl.ds(pl.multiple_of(i * step, step), step)
            mine = pl.ds(pl.multiple_of(start + i * step, step), step)
            to = pl.ds(pl.multiple_of(at + i * step, step), step)
            ext[to, :reach] = left[here, :]
            ext[to, reach : reach + width] = own[mine, :]
            ext[to, reach + width : 2 * reach + width] = right[here, :]

        at += size


def row_sums(index_ref, row, slots, block, ext, panel_ref):
    picked = jnp.concatenate(
        [
            ext[:, pl.ds(pl.multiple_of(index_ref[row * slots + slot] * block, block), block)]
            for slot in range(slots)
        ],
        axis=1,
    )
    panel = jnp.concatenate([panel_ref[slot] for slot in range(slots)], axis=1)
    return lax.dot_general(
        picked, panel, (((1,), (1,)), ((), ())), preferred_element_type=jnp.float32
    )


def level_code(top):
    return jnp.ceil(jnp.log2(jnp.maximum(top, SMALLEST)) * FINE).astype(jnp.int32)


def level_of(code):
    return jnp.exp2(code.astype(jnp.float32) * (1.0 / FINE))


def code_into(out_ref, first, block, words, sums):
    lane = lax.broadcasted_iota(jnp.int32, (out_ref.shape[0], block), 1)
    codes = out_ref[:, words * block :]
    values = []
    for member, mine in enumerate(sums):
        code = level_code(jnp.max(jnp.abs(mine), axis=1, keepdims=True))
        codes = jnp.where(lane == first + member, code, codes)
        scaled = jnp.round(mine * (TOP / level_of(code)))
        values.append(jnp.clip(scaled, -TOP, TOP).astype(jnp.int32))
    out_ref[:, words * block :] = codes
    for pair in range(len(sums) // 2):
        word = (values[2 * pair + 1] << 16) | (values[2 * pair] & 0xFFFF)
        at = pl.multiple_of((first // 2 + pair) * block, block)
        out_ref[:, pl.ds(at, block)] = word


def products_kernel(plan, group, slots, block, words, index_ref, *refs):
    parts = len(plan)
    sources, blocks_ref = refs[: 3 * parts], refs[3 * parts]
    outs, (ext, panels, panel_sems) = refs[3 * parts + 1 : 4 * parts + 1], refs[4 * parts + 1 :]
    rows, pieces = panels.shape[0], panel_sems.shape[0]
    piece = rows // pieces

    def panel_copy(n):
        here = pl.ds(n * piece, piece)
        return pltpu.make_async_copy(blocks_ref.at[here], panels.at[here], panel_sems.at[n])

    for n in range(pieces):
        panel_copy(n).start()
    fill(sources, plan, ext)
    end = ext.shape[1] - block
    ext[:, end:] = jnp.zeros((ext.shape[0], block), ext.dtype)
    for (_, size, coded), out_ref in zip(plan, outs):
        if coded:
            out_ref[:, words * block :] = jnp.zeros((size, block), jnp.int32)

    @pl.loop(0, rows // group)
    def _(step):
        for n in range(group // piece):
            panel_copy(step * (group // piece) + n).wait()
        first = step * group
        sums = [
            row_sums(index_ref, first + member, slots, block, ext, panels.at[first + member])
            for member in range(group)
        ]
        at = 0
        for (_, size, coded), out_ref in zip(plan, outs):
            mine = [total[at : at + size] for total in sums]
            if coded:
                code_into(out_ref, first, block, words, mine)
            else:
                for member in range(group):
                    column = pl.multiple_of((first + member) * block, block)
                    out_ref[:, pl.ds(column, block)] = mine[member]
            at += size


def products(index, parts, blocks):
    rows, slots, block, _ = blocks.shape
    reach, width = parts[0][0].shape[1], parts[0][1].shape[1]
    plan = tuple(part[3:] for part in parts)
    states = sum(size for _, size, _ in plan)
    group, words = 8 if rows % 8 == 0 else 2, rows // 2
    sources = [array for part in parts for array in part[:3]]
    in_vmem = pl.BlockSpec(memory_space=pltpu.VMEM)
    out_shape = []
    for _, size, coded in plan:
        if coded:
            out_shape.append(jax.ShapeDtypeStruct((size, (words + 1) * block), jnp.int32))
        else:
            out_shape.append(jax.ShapeDtypeStruct((size, width), jnp.float32))
    return pl.pallas_call(
        functools.partial(products_kernel, plan, group, slots, block, words),
        out_shape=out_shape,
        in_specs=[pl.BlockSpec(memory_space=pltpu.SMEM)]
        + [in_vmem] * len(sources)
        + [pl.BlockSpec(memory_space=pltpu.HBM)],
        out_specs=[in_vmem] * len(plan),
        scratch_shapes=[
            pltpu.VMEM((states, 2 * reach + width + block), parts[0][1].dtype),
            pltpu.VMEM(blocks.shape, blocks.dtype),
            pltpu.SemaphoreType.DMA((rows // 2,)),
        ],
        compiler_params=pltpu.CompilerParams(vmem_limit_bytes=VMEM_LIMIT),
        cost_estimate=pl.CostEstimate(flops=1, bytes_accessed=1, transcendentals=0),
        name="products",
    )(index, *sources, pltpu.with_memory_space_constraint(blocks, pltpu.HBM))


def finish_kernel(partials, block, pairs, own_ref, *refs):
    out_ref = refs[-1]
    step = pl.program_id(0)
    lane = lax.broadcasted_iota(jnp.int32, (own_ref.shape[0], block), 1)
    levels = [level_of(refs[2 * p + 1][...]) * (1.0 / TOP) for p in range(partials)]
    for pair in range(pairs):
        for half in range(2):
            at = (2 * pair + half) * block
            row = (step * pairs + pair) * 2 + half
            total = own_ref[:, at : at + block]
            for p in range(partials):
                word = refs[2 * p][:, pair * block : (pair + 1) * block]
                value = (word >> 16) if half else ((word << 16) >> 16)
                level = jnp.max(jnp.where(lane == row, levels[p], 0.0), axis=1, keepdims=True)
                total = total + value.astype(jnp.float32) * level
            out_ref[:, at : at + block] = total.astype(out_ref.dtype)


def finish(own_sums, own_start, coded, coded_start, out, start, size, states, block):
    width = own_sums.shape[1]
    words = width // block // 2
    pairs = words // 2 if words % 2 == 0 else 1
    rows, wide, narrow = pl.Element(size), pl.Element(2 * pairs * block), pl.Element(pairs * block)
    own_at, coded_at = start - own_start, start - coded_start
    in_specs = [pl.BlockSpec((rows, wide), lambda i: (own_at, i * 2 * pairs * block))]
    operands = [own_sums]
    for array in coded:
        in_specs.append(pl.BlockSpec((rows, narrow), lambda i: (coded_at, i * pairs * block)))
        in_specs.append(pl.BlockSpec((rows, pl.Element(block)), lambda i: (coded_at, words * block)))
        operands += [array, array]
    aliases = {}
    if out is not None:
        aliases = {len(operands): 0}
        in_specs.append(pl.BlockSpec(memory_space=pl.ANY))
        operands.append(out)
    return pl.pallas_call(
        functools.partial(finish_kernel, len(coded), block, pairs),
        out_shape=jax.ShapeDtypeStruct((states, width), jnp.bfloat16),
        grid=(words // pairs,),
        in_specs=in_specs,
        out_specs=pl.BlockSpec((rows, wide), lambda i: (start, i * 2 * pairs * block)),
        input_output_aliases=aliases,
        compiler_params=pltpu.CompilerParams(vmem_limit_bytes=VMEM_LIMIT),
        cost_estimate=pl.CostEstimate(flops=1, bytes_accessed=1, transcendentals=0),
        name="finish",
    )(*operands)


def starts_of(sizes):
    return [sum(sizes[:i]) for i in range(len(sizes))]


def on_device(vectors, blocks, columns, counts):
    states, width = vectors.shape
    rows, slots, block, _ = blocks.shape
    reach = W * block
    basis_size, state_size = lax.axis_size("basis"), lax.axis_size("state")
    if states % 256 == 0:
        sizes = (5 * states // 16, 3 * states // 8, 5 * states // 16)
        own_sizes = (7 * states // 16, 9 * states // 16)
    else:
        sizes, own_sizes = (states,), (states,)
    starts, own_starts = starts_of(sizes), starts_of(own_sizes)

    slot_index = lax.axis_index("state") * slots + jnp.arange(slots, dtype=jnp.int32)
    relative = columns - (lax.axis_index("basis") * rows - W)
    zeros_at = rows + 2 * W
    index = jnp.where(slot_index[None, :] < counts[:, None], relative, zeros_at).reshape(-1)

    up = [(i, i + 1) for i in range(basis_size - 1)]
    down = [(i + 1, i) for i in range(basis_size - 1)]

    def edges_of(piece, *others):
        edges = (piece[:, width - reach :], piece[:, :reach])
        return lax.optimization_barrier((*edges, *others))[:2] if others else edges

    def halo(edges):
        return lax.ppermute(edges[0], "basis", up), lax.ppermute(edges[1], "basis", down)

    def shifted(piece, shift):
        return lax.ppermute(piece, "state", [(i, (i + shift) % state_size) for i in range(state_size)])

    def own_edges(part, *others):
        return edges_of(vectors[own_starts[part] : own_starts[part] + own_sizes[part]], *others)

    def own_part(part, ends):
        return (ends[0], vectors, ends[1], own_starts[part], own_sizes[part], False)

    def their_part(n):
        return (ends[n][0], theirs[n], ends[n][1], 0, theirs[n].shape[0], True)

    messages = [(shift, c) for shift in range(1, state_size) for c in range(len(sizes))]
    count = len(messages)
    theirs, edges, ends, sent, own_sums, received = [], [], [], [], [], []
    first_edges = own_edges(0)
    first = halo(first_edges)
    for n, (shift, c) in enumerate(messages):
        source = after(vectors, *(first_edges[::-1] if n == 1 else first)) if n else vectors
        theirs.append(shifted(source[starts[c] : starts[c] + sizes[c]], shift))

    def compute(n):
        later = (*edges[n + 1][:: -1 if n == 0 else 1], *edges[n][::-1]) if n + 1 < count else ()
        sent.extend(products(after(index, *later) if later else index, [their_part(n)], blocks))
        if n == 0:
            own_sums.extend(products(after(index, sent[0]), [own_part(0, first)], blocks))

    for n in range(count):
        edges.append(edges_of(theirs[n], *(own_sums if n > 1 else ())))
        ends.append(halo(edges[n]))
        if n:
            compute(n - 1)
    coded = [[] for _ in sizes]

    def send(n):
        shift, c = messages[n]
        message = after(sent[n], received[n - 1]) if n else sent[n]
        received.append(shifted(message, -shift))
        coded[c].append(received[n])

    def finish_piece(part, c, out):
        own_end, end = own_starts[part] + own_sizes[part], starts[c] + sizes[c]
        at, end = max(own_starts[part], starts[c]), min(own_end, end)
        if at >= end:
            return out
        return finish(
            own_sums[part], own_starts[part], coded[c], starts[c], out, at, end - at, states, block
        )

    out, done = None, set()
    if len(own_sizes) > 1:
        send(0)
        if state_size == 2:
            out = finish_piece(0, 0, out)
            done.add((0, 0))
        held = (out,) if done else ()
        last = halo(own_edges(1, *edges[-1], *sent[-1:], *held))
    compute(count - 1)
    for n in range(len(received), count):
        send(n)
    for part in range(len(own_sizes)):
        if part:
            own_sums += products(after(index, out), [own_part(part, last)], blocks)
        for c in range(len(sizes)):
            if (part, c) not in done:
                out = finish_piece(part, c, out)
    return out


def solution(mesh):
    in_specs = (
        P("state", "basis"),
        P("basis", "state", None, None),
        P("basis", "state"),
        P("basis"),
    )
    out_specs = P("state", "basis")
    return jax.shard_map(
        on_device, mesh=mesh, in_specs=in_specs, out_specs=out_specs, check_vma=False
    )
```

```python
import functools
import math

import jax
import jax.numpy as jnp
from jax import lax
from jax.experimental import pallas as pl
from jax.experimental.pallas import tpu as pltpu
from jax.sharding import PartitionSpec as P

W = 36
VMEM_LIMIT = 32 * 1024 * 1024
TOP = 32767.0
FINE = 65536.0
SMALLEST = 2.0**-100


def after(array, *others):
    return lax.optimization_barrier((array, *others))[0]


def fill(sources, plan, ext):
    at, step = 0, 16
    for part, (start, size, _) in enumerate(plan):
        left, own, right = sources[3 * part : 3 * part + 3]
        reach, width = left.shape[1], own.shape[1]

        @pl.loop(0, size // step)
        def _(i, left=left, own=own, right=right, start=start, at=at, reach=reach, width=width):
            here = pl.ds(pl.multiple_of(i * step, step), step)
            mine = pl.ds(pl.multiple_of(start + i * step, step), step)
            to = pl.ds(pl.multiple_of(at + i * step, step), step)
            ext[to, :reach] = left[here, :]
            ext[to, reach : reach + width] = own[mine, :]
            ext[to, reach + width : 2 * reach + width] = right[here, :]

        at += size


def row_sums(index_ref, row, slots, block, ext, panel_ref):
    picked = jnp.concatenate(
        [
            ext[:, pl.ds(pl.multiple_of(index_ref[row * slots + slot] * block, block), block)]
            for slot in range(slots)
        ],
        axis=1,
    )
    panel = jnp.concatenate([panel_ref[slot] for slot in range(slots)], axis=1)
    return lax.dot_general(
        picked, panel, (((1,), (1,)), ((), ())), preferred_element_type=jnp.float32
    )


def level_code(top):
    return jnp.ceil(jnp.log2(jnp.maximum(top, SMALLEST)) * FINE).astype(jnp.int32)


def level_of(code):
    return jnp.exp2(code.astype(jnp.float32) * (1.0 / FINE))


def code_into(out_ref, first, block, words, sums):
    lane = lax.broadcasted_iota(jnp.int32, (out_ref.shape[0], block), 1)
    codes = out_ref[:, words * block :]
    values = []
    for member, mine in enumerate(sums):
        code = level_code(jnp.max(jnp.abs(mine), axis=1, keepdims=True))
        codes = jnp.where(lane == first + member, code, codes)
        scaled = jnp.round(mine * (TOP / level_of(code)))
        values.append(jnp.clip(scaled, -TOP, TOP).astype(jnp.int32))
    out_ref[:, words * block :] = codes
    for pair in range(len(sums) // 2):
        word = (values[2 * pair + 1] << 16) | (values[2 * pair] & 0xFFFF)
        at = pl.multiple_of((first // 2 + pair) * block, block)
        out_ref[:, pl.ds(at, block)] = word


def products_kernel(plan, group, slots, block, words, index_ref, *refs):
    parts = len(plan)
    sources, blocks_ref = refs[: 3 * parts], refs[3 * parts]
    outs, (ext, panels, panel_sems) = refs[3 * parts + 1 : 4 * parts + 1], refs[4 * parts + 1 :]
    rows, pieces = panels.shape[0], panel_sems.shape[0]
    piece = rows // pieces

    def panel_copy(n):
        here = pl.ds(n * piece, piece)
        return pltpu.make_async_copy(blocks_ref.at[here], panels.at[here], panel_sems.at[n])

    for n in range(pieces):
        panel_copy(n).start()
    fill(sources, plan, ext)
    end = ext.shape[1] - block
    ext[:, end:] = jnp.zeros((ext.shape[0], block), ext.dtype)
    for (_, size, coded), out_ref in zip(plan, outs):
        if coded:
            out_ref[:, words * block :] = jnp.zeros((size, block), jnp.int32)

    @pl.loop(0, rows // group)
    def _(step):
        for n in range(group // piece):
            panel_copy(step * (group // piece) + n).wait()
        first = step * group
        sums = [
            row_sums(index_ref, first + member, slots, block, ext, panels.at[first + member])
            for member in range(group)
        ]
        at = 0
        for (_, size, coded), out_ref in zip(plan, outs):
            mine = [total[at : at + size] for total in sums]
            if coded:
                code_into(out_ref, first, block, words, mine)
            else:
                for member in range(group):
                    column = pl.multiple_of((first + member) * block, block)
                    out_ref[:, pl.ds(column, block)] = mine[member]
            at += size


def products(index, parts, blocks):
    rows, slots, block, _ = blocks.shape
    reach, width = parts[0][0].shape[1], parts[0][1].shape[1]
    plan = tuple(part[3:] for part in parts)
    states = sum(size for _, size, _ in plan)
    group, words = 8 if rows % 8 == 0 else 2, rows // 2
    sources = [array for part in parts for array in part[:3]]
    in_vmem = pl.BlockSpec(memory_space=pltpu.VMEM)
    out_shape = []
    for _, size, coded in plan:
        if coded:
            out_shape.append(jax.ShapeDtypeStruct((size, (words + 1) * block), jnp.int32))
        else:
            out_shape.append(jax.ShapeDtypeStruct((size, width), jnp.float32))
    return pl.pallas_call(
        functools.partial(products_kernel, plan, group, slots, block, words),
        out_shape=out_shape,
        in_specs=[pl.BlockSpec(memory_space=pltpu.SMEM)]
        + [in_vmem] * len(sources)
        + [pl.BlockSpec(memory_space=pltpu.HBM)],
        out_specs=[in_vmem] * len(plan),
        scratch_shapes=[
            pltpu.VMEM((states, 2 * reach + width + block), parts[0][1].dtype),
            pltpu.VMEM(blocks.shape, blocks.dtype),
            pltpu.SemaphoreType.DMA((rows // 2,)),
        ],
        compiler_params=pltpu.CompilerParams(vmem_limit_bytes=VMEM_LIMIT),
        cost_estimate=pl.CostEstimate(flops=1, bytes_accessed=1, transcendentals=0),
        name="products",
    )(index, *sources, pltpu.with_memory_space_constraint(blocks, pltpu.HBM))


def finish_kernel(pieces, block, pairs, own_ref, *refs):
    out_ref = refs[-1]
    step = pl.program_id(0)
    n = 0
    for offset, length, partials in pieces:
        lane = lax.broadcasted_iota(jnp.int32, (length, block), 1)
        rows = pl.ds(offset, length)
        some = [refs[2 * p : 2 * p + 2] for p in range(n, n + partials)]
        levels = [level_of(codes[...]) * (1.0 / TOP) for _, codes in some]
        n += partials
        for pair in range(pairs):
            for half in range(2):
                at = (2 * pair + half) * block
                row = (step * pairs + pair) * 2 + half
                total = own_ref[rows, at : at + block]
                for (words, _), mine in zip(some, levels):
                    word = words[:, pair * block : (pair + 1) * block]
                    value = (word >> 16) if half else ((word << 16) >> 16)
                    level = jnp.max(jnp.where(lane == row, mine, 0.0), axis=1, keepdims=True)
                    total = total + value.astype(jnp.float32) * level
                out_ref[rows, at : at + block] = total.astype(out_ref.dtype)


def finish(own_sums, own_start, pieces, out, states, block):
    width = own_sums.shape[1]
    words = width // block // 2
    pairs = words // 2 if words % 2 == 0 else 1
    start, size = pieces[0][0], sum(piece[1] for piece in pieces)
    rows, wide = pl.Element(size), pl.Element(2 * pairs * block)
    own_at = start - own_start
    in_specs = [pl.BlockSpec((rows, wide), lambda i: (own_at, i * 2 * pairs * block))]
    operands, shapes = [own_sums], []
    for at, length, arrays, coded_start in pieces:
        shapes.append((at - start, length, len(arrays)))
        some, first = pl.Element(length), at - coded_start
        for array in arrays:
            in_specs.append(
                pl.BlockSpec((some, pl.Element(pairs * block)), lambda i, first=first: (first, i * pairs * block))
            )
            in_specs.append(
                pl.BlockSpec((some, pl.Element(block)), lambda i, first=first: (first, words * block))
            )
            operands += [array, array]
    aliases = {}
    if out is not None:
        aliases = {len(operands): 0}
        in_specs.append(pl.BlockSpec(memory_space=pl.ANY))
        operands.append(out)
    return pl.pallas_call(
        functools.partial(finish_kernel, tuple(shapes), block, pairs),
        out_shape=jax.ShapeDtypeStruct((states, width), jnp.bfloat16),
        grid=(words // pairs,),
        in_specs=in_specs,
        out_specs=pl.BlockSpec((rows, wide), lambda i: (start, i * 2 * pairs * block)),
        input_output_aliases=aliases,
        compiler_params=pltpu.CompilerParams(vmem_limit_bytes=VMEM_LIMIT),
        cost_estimate=pl.CostEstimate(flops=1, bytes_accessed=1, transcendentals=0),
        name="finish",
    )(*operands)


def starts_of(sizes):
    return [sum(sizes[:i]) for i in range(len(sizes))]


def on_device(vectors, blocks, columns, counts):
    states, width = vectors.shape
    rows, slots, block, _ = blocks.shape
    reach = W * block
    basis_size, state_size = lax.axis_size("basis"), lax.axis_size("state")
    if states % 256 == 0:
        sizes = (5 * states // 16, 3 * states // 8, 5 * states // 16)
        own_sizes = (7 * states // 16, 9 * states // 16)
    else:
        sizes, own_sizes = (states,), (states,)
    starts, own_starts = starts_of(sizes), starts_of(own_sizes)

    slot_index = lax.axis_index("state") * slots + jnp.arange(slots, dtype=jnp.int32)
    relative = columns - (lax.axis_index("basis") * rows - W)
    zeros_at = rows + 2 * W
    index = jnp.where(slot_index[None, :] < counts[:, None], relative, zeros_at).reshape(-1)

    up = [(i, i + 1) for i in range(basis_size - 1)]
    down = [(i + 1, i) for i in range(basis_size - 1)]

    def edges_of(piece, *others):
        edges = (piece[:, width - reach :], piece[:, :reach])
        return lax.optimization_barrier((*edges, *others))[:2] if others else edges

    def halo(edges):
        return lax.ppermute(edges[0], "basis", up), lax.ppermute(edges[1], "basis", down)

    def shifted(piece, shift):
        return lax.ppermute(piece, "state", [(i, (i + shift) % state_size) for i in range(state_size)])

    def own_edges(part, *others):
        return edges_of(vectors[own_starts[part] : own_starts[part] + own_sizes[part]], *others)

    def own_part(part, ends):
        return (ends[0], vectors, ends[1], own_starts[part], own_sizes[part], False)

    def their_part(n):
        return (ends[n][0], theirs[n], ends[n][1], 0, theirs[n].shape[0], True)

    messages = [(shift, c) for shift in range(1, state_size) for c in range(len(sizes))]
    count = len(messages)
    theirs, edges, ends, sent, own_sums, received = [], [], [], [], [], []
    first_edges = own_edges(0)
    first = halo(first_edges)
    for n, (shift, c) in enumerate(messages):
        source = after(vectors, *(first_edges[::-1] if n == 1 else first)) if n else vectors
        theirs.append(shifted(source[starts[c] : starts[c] + sizes[c]], shift))

    def compute(n):
        later = (*edges[n + 1][:: -1 if n == 0 else 1], *edges[n][::-1]) if n + 1 < count else ()
        sent.extend(products(after(index, *later) if later else index, [their_part(n)], blocks))
        if n == 0:
            own_sums.extend(products(after(index, sent[0]), [own_part(0, first)], blocks))

    for n in range(count):
        edges.append(edges_of(theirs[n], *(own_sums if n > 1 else ())))
        ends.append(halo(edges[n]))
        if n:
            compute(n - 1)
    coded = [[] for _ in sizes]

    def send(n):
        shift, c = messages[n]
        message = after(sent[n], received[n - 1]) if n else sent[n]
        received.append(shifted(message, -shift))
        coded[c].append(received[n])

    def finish_pieces(part, chunks, out):
        pieces = []
        for c in chunks:
            at = max(own_starts[part], starts[c])
            end = min(own_starts[part] + own_sizes[part], starts[c] + sizes[c])
            if at < end:
                pieces.append((at, end - at, coded[c], starts[c]))
        return finish(own_sums[part], own_starts[part], pieces, out, states, block) if pieces else out

    out, done = None, set()
    if len(own_sizes) > 1:
        send(0)
        if state_size == 2:
            out = finish_pieces(0, (0,), out)
            done.add((0, 0))
        held = (out,) if done else ()
        last = halo(own_edges(1, *edges[-1], *sent[-1:], *held))
    compute(count - 1)
    for n in range(len(received), count):
        send(n)
    for part in range(len(own_sizes)):
        if part:
            own_sums += products(after(index, out), [own_part(part, last)], blocks)
        out = finish_pieces(part, [c for c in range(len(sizes)) if (part, c) not in done], out)
    return out


def solution(mesh):
    in_specs = (
        P("state", "basis"),
        P("basis", "state", None, None),
        P("basis", "state"),
        P("basis"),
    )
    out_specs = P("state", "basis")
    return jax.shard_map(
        on_device, mesh=mesh, in_specs=in_specs, out_specs=out_specs, check_vma=False
    )
```

```python
import functools
import math

import jax
import jax.numpy as jnp
from jax import lax
from jax.experimental import pallas as pl
from jax.experimental.pallas import tpu as pltpu
from jax.sharding import PartitionSpec as P

W = 36
VMEM_LIMIT = 32 * 1024 * 1024
TOP = 32767.0
FINE = 65536.0
SMALLEST = 2.0**-100


def after(array, *others):
    return lax.optimization_barrier((array, *others))[0]


def fill(sources, plan, ext):
    at, step = 0, 16
    for part, (start, size, _) in enumerate(plan):
        left, own, right = sources[3 * part : 3 * part + 3]
        reach, width = left.shape[1], own.shape[1]

        @pl.loop(0, size // step)
        def _(i, left=left, own=own, right=right, start=start, at=at, reach=reach, width=width):
            here = pl.ds(pl.multiple_of(i * step, step), step)
            mine = pl.ds(pl.multiple_of(start + i * step, step), step)
            to = pl.ds(pl.multiple_of(at + i * step, step), step)
            ext[to, :reach] = left[here, :]
            ext[to, reach : reach + width] = own[mine, :]
            ext[to, reach + width : 2 * reach + width] = right[here, :]

        at += size


def row_sums(index_ref, row, slots, block, ext, panel_ref):
    picked = jnp.concatenate(
        [
            ext[:, pl.ds(pl.multiple_of(index_ref[row * slots + slot] * block, block), block)]
            for slot in range(slots)
        ],
        axis=1,
    )
    panel = jnp.concatenate([panel_ref[slot] for slot in range(slots)], axis=1)
    return lax.dot_general(
        picked, panel, (((1,), (1,)), ((), ())), preferred_element_type=jnp.float32
    )


def level_code(top):
    return jnp.ceil(jnp.log2(jnp.maximum(top, SMALLEST)) * FINE).astype(jnp.int32)


def level_of(code):
    return jnp.exp2(code.astype(jnp.float32) * (1.0 / FINE))


def code_into(out_ref, first, block, words, sums):
    lane = lax.broadcasted_iota(jnp.int32, (out_ref.shape[0], block), 1)
    codes = out_ref[:, words * block :]
    values = []
    for member, mine in enumerate(sums):
        code = level_code(jnp.max(jnp.abs(mine), axis=1, keepdims=True))
        codes = jnp.where(lane == first + member, code, codes)
        scaled = jnp.round(mine * (TOP / level_of(code)))
        values.append(jnp.clip(scaled, -TOP, TOP).astype(jnp.int32))
    out_ref[:, words * block :] = codes
    for pair in range(len(sums) // 2):
        word = (values[2 * pair + 1] << 16) | (values[2 * pair] & 0xFFFF)
        at = pl.multiple_of((first // 2 + pair) * block, block)
        out_ref[:, pl.ds(at, block)] = word


def products_kernel(plan, group, slots, block, words, index_ref, *refs):
    parts = len(plan)
    sources, blocks_ref = refs[: 3 * parts], refs[3 * parts]
    outs, (ext, panels, panel_sems) = refs[3 * parts + 1 : 4 * parts + 1], refs[4 * parts + 1 :]
    rows, pieces = panels.shape[0], panel_sems.shape[0]
    piece = rows // pieces

    def panel_copy(n):
        here = pl.ds(n * piece, piece)
        return pltpu.make_async_copy(blocks_ref.at[here], panels.at[here], panel_sems.at[n])

    for n in range(pieces):
        panel_copy(n).start()
    fill(sources, plan, ext)
    end = ext.shape[1] - block
    ext[:, end:] = jnp.zeros((ext.shape[0], block), ext.dtype)
    for (_, size, coded), out_ref in zip(plan, outs):
        if coded:
            out_ref[:, words * block :] = jnp.zeros((size, block), jnp.int32)

    @pl.loop(0, rows // group)
    def _(step):
        for n in range(group // piece):
            panel_copy(step * (group // piece) + n).wait()
        first = step * group
        sums = [
            row_sums(index_ref, first + member, slots, block, ext, panels.at[first + member])
            for member in range(group)
        ]
        at = 0
        for (_, size, coded), out_ref in zip(plan, outs):
            mine = [total[at : at + size] for total in sums]
            if coded:
                code_into(out_ref, first, block, words, mine)
            else:
                for member in range(group):
                    column = pl.multiple_of((first + member) * block, block)
                    out_ref[:, pl.ds(column, block)] = mine[member]
            at += size


def products(index, parts, blocks):
    rows, slots, block, _ = blocks.shape
    reach, width = parts[0][0].shape[1], parts[0][1].shape[1]
    plan = tuple(part[3:] for part in parts)
    states = sum(size for _, size, _ in plan)
    group, words = 8 if rows % 8 == 0 else 2, rows // 2
    sources = [array for part in parts for array in part[:3]]
    in_vmem = pl.BlockSpec(memory_space=pltpu.VMEM)
    out_shape = []
    for _, size, coded in plan:
        if coded:
            out_shape.append(jax.ShapeDtypeStruct((size, (words + 1) * block), jnp.int32))
        else:
            out_shape.append(jax.ShapeDtypeStruct((size, width), jnp.float32))
    return pl.pallas_call(
        functools.partial(products_kernel, plan, group, slots, block, words),
        out_shape=out_shape,
        in_specs=[pl.BlockSpec(memory_space=pltpu.SMEM)]
        + [in_vmem] * len(sources)
        + [pl.BlockSpec(memory_space=pltpu.HBM)],
        out_specs=[in_vmem] * len(plan),
        scratch_shapes=[
            pltpu.VMEM((states, 2 * reach + width + block), parts[0][1].dtype),
            pltpu.VMEM(blocks.shape, blocks.dtype),
            pltpu.SemaphoreType.DMA((rows // 2,)),
        ],
        compiler_params=pltpu.CompilerParams(vmem_limit_bytes=VMEM_LIMIT),
        cost_estimate=pl.CostEstimate(flops=1, bytes_accessed=1, transcendentals=0),
        name="products",
    )(index, *sources, pltpu.with_memory_space_constraint(blocks, pltpu.HBM))


def finish_kernel(pieces, block, pairs, own_ref, *refs):
    out_ref = refs[-1]
    step = pl.program_id(0)
    n = 0
    for offset, length, partials in pieces:
        lane = lax.broadcasted_iota(jnp.int32, (length, block), 1)
        rows = pl.ds(offset, length)
        some = [refs[2 * p : 2 * p + 2] for p in range(n, n + partials)]
        levels = [level_of(codes[...]) * (1.0 / TOP) for _, codes in some]
        n += partials
        for pair in range(pairs):
            for half in range(2):
                at = (2 * pair + half) * block
                row = (step * pairs + pair) * 2 + half
                total = own_ref[rows, at : at + block]
                for (words, _), mine in zip(some, levels):
                    word = words[:, pair * block : (pair + 1) * block]
                    value = (word >> 16) if half else ((word << 16) >> 16)
                    level = jnp.max(jnp.where(lane == row, mine, 0.0), axis=1, keepdims=True)
                    total = total + value.astype(jnp.float32) * level
                out_ref[rows, at : at + block] = total.astype(out_ref.dtype)


def finish(own_sums, own_start, pieces, out, states, block):
    width = own_sums.shape[1]
    words = width // block // 2
    steps = 4 if len(pieces) > 1 and words % 4 == 0 else 2
    pairs = words // steps if words % steps == 0 else 1
    start, size = pieces[0][0], sum(piece[1] for piece in pieces)
    rows, wide = pl.Element(size), pl.Element(2 * pairs * block)
    own_at = start - own_start
    in_specs = [pl.BlockSpec((rows, wide), lambda i: (own_at, i * 2 * pairs * block))]
    operands, shapes = [own_sums], []
    for at, length, arrays, coded_start in pieces:
        shapes.append((at - start, length, len(arrays)))
        some, first = pl.Element(length), at - coded_start
        for array in arrays:
            in_specs.append(
                pl.BlockSpec((some, pl.Element(pairs * block)), lambda i, first=first: (first, i * pairs * block))
            )
            in_specs.append(
                pl.BlockSpec((some, pl.Element(block)), lambda i, first=first: (first, words * block))
            )
            operands += [array, array]
    aliases = {}
    if out is not None:
        aliases = {len(operands): 0}
        in_specs.append(pl.BlockSpec(memory_space=pl.ANY))
        operands.append(out)
    return pl.pallas_call(
        functools.partial(finish_kernel, tuple(shapes), block, pairs),
        out_shape=jax.ShapeDtypeStruct((states, width), jnp.bfloat16),
        grid=(words // pairs,),
        in_specs=in_specs,
        out_specs=pl.BlockSpec((rows, wide), lambda i: (start, i * 2 * pairs * block)),
        input_output_aliases=aliases,
        compiler_params=pltpu.CompilerParams(vmem_limit_bytes=VMEM_LIMIT),
        cost_estimate=pl.CostEstimate(flops=1, bytes_accessed=1, transcendentals=0),
        name="finish",
    )(*operands)


def starts_of(sizes):
    return [sum(sizes[:i]) for i in range(len(sizes))]


def on_device(vectors, blocks, columns, counts):
    states, width = vectors.shape
    rows, slots, block, _ = blocks.shape
    reach = W * block
    basis_size, state_size = lax.axis_size("basis"), lax.axis_size("state")
    if states % 256 == 0:
        sizes = (5 * states // 16, 3 * states // 8, 5 * states // 16)
        own_sizes = (7 * states // 16, 9 * states // 16)
    else:
        sizes, own_sizes = (states,), (states,)
    starts, own_starts = starts_of(sizes), starts_of(own_sizes)

    slot_index = lax.axis_index("state") * slots + jnp.arange(slots, dtype=jnp.int32)
    relative = columns - (lax.axis_index("basis") * rows - W)
    zeros_at = rows + 2 * W
    index = jnp.where(slot_index[None, :] < counts[:, None], relative, zeros_at).reshape(-1)

    up = [(i, i + 1) for i in range(basis_size - 1)]
    down = [(i + 1, i) for i in range(basis_size - 1)]

    def edges_of(piece, *others):
        edges = (piece[:, width - reach :], piece[:, :reach])
        return lax.optimization_barrier((*edges, *others))[:2] if others else edges

    def halo(edges):
        return lax.ppermute(edges[0], "basis", up), lax.ppermute(edges[1], "basis", down)

    def shifted(piece, shift):
        return lax.ppermute(piece, "state", [(i, (i + shift) % state_size) for i in range(state_size)])

    def own_edges(part, *others):
        return edges_of(vectors[own_starts[part] : own_starts[part] + own_sizes[part]], *others)

    def own_part(part, ends):
        return (ends[0], vectors, ends[1], own_starts[part], own_sizes[part], False)

    def their_part(n):
        return (ends[n][0], theirs[n], ends[n][1], 0, theirs[n].shape[0], True)

    messages = [(shift, c) for shift in range(1, state_size) for c in range(len(sizes))]
    count = len(messages)
    theirs, edges, ends, sent, own_sums, received = [], [], [], [], [], []
    first_edges = own_edges(0)
    first = halo(first_edges)
    for n, (shift, c) in enumerate(messages):
        source = after(vectors, *(first_edges[::-1] if n == 1 else first)) if n else vectors
        theirs.append(shifted(source[starts[c] : starts[c] + sizes[c]], shift))

    def compute(n):
        later = (*edges[n + 1][:: -1 if n == 0 else 1], *edges[n][::-1]) if n + 1 < count else ()
        sent.extend(products(after(index, *later) if later else index, [their_part(n)], blocks))
        if n == 0:
            own_sums.extend(products(after(index, sent[0]), [own_part(0, first)], blocks))

    for n in range(count):
        edges.append(edges_of(theirs[n], *(own_sums if n > 1 else ())))
        ends.append(halo(edges[n]))
        if n:
            compute(n - 1)
    coded = [[] for _ in sizes]

    def send(n):
        shift, c = messages[n]
        message = after(sent[n], received[n - 1]) if n else sent[n]
        received.append(shifted(message, -shift))
        coded[c].append(received[n])

    def finish_pieces(part, chunks, out):
        pieces = []
        for c in chunks:
            at = max(own_starts[part], starts[c])
            end = min(own_starts[part] + own_sizes[part], starts[c] + sizes[c])
            if at < end:
                pieces.append((at, end - at, coded[c], starts[c]))
        return finish(own_sums[part], own_starts[part], pieces, out, states, block) if pieces else out

    out, done = None, set()
    if len(own_sizes) > 1:
        send(0)
        if state_size == 2:
            out = finish_pieces(0, (0,), out)
            done.add((0, 0))
        held = (out,) if done else ()
        last = halo(own_edges(1, *edges[-1], *sent[-1:], *held))
    compute(count - 1)
    for n in range(len(received), count):
        send(n)
    for part in range(len(own_sizes)):
        if part:
            own_sums += products(after(index, out), [own_part(part, last)], blocks)
        out = finish_pieces(part, [c for c in range(len(sizes)) if (part, c) not in done], out)
    return out


def solution(mesh):
    in_specs = (
        P("state", "basis"),
        P("basis", "state", None, None),
        P("basis", "state"),
        P("basis"),
    )
    out_specs = P("state", "basis")
    return jax.shard_map(
        on_device, mesh=mesh, in_specs=in_specs, out_specs=out_specs, check_vma=False
    )
```
